32 devices in a mesh: dp: 16 (over z, y, core), cls: 2 (over x).
Axes of the slice: x: 2, y: 2, z: 4, core: 2. Of those that a mesh axis runs over, the one named last changes fastest.
Arguments:
- features: bfloat16 [2048, 12544], P('dp', 'cls'), may hold values from -6 to 6
- fc_weight: bfloat16 [12544, 512], P('cls'), may hold values from -0.0546875 to 0.0546875
- class_weight: bfloat16 [1024, 512], P('cls'), may hold values from -0.29882812 to 0.29882812
- labels: int32 [2048], P('dp'), may hold values from 0 to 1023
Outputs:
- fc_grad: bfloat16 [12544, 512], P('cls')
- class_grad: bfloat16 [1024, 512], P('cls')
The draws below stay inside these ranges and needn't reach their ends.
All inputs are finite; a program needn't handle non-finite values.
Results may differ from the reference program's by a relative error of at most 0.024.
Values may be sent and summed in bfloat16 or wider, within the bound.
A program may use at most 64 MiB of HBM per device.

```python
import math
import jax
import jax.numpy as jnp
from jax import lax

D = 512
FIN = 12544
FACES = 2048
CLASSES = 1024
N_CLS = 2


def touch_ends(entries, rng, least, high):
    spot = [jax.random.randint(jax.random.fold_in(rng, axis), (), 0, length) for axis, length in enumerate(entries.shape)]
    longest = entries.shape.index(max(entries.shape))
    next_to = spot[:longest] + [(spot[longest] + 1) % entries.shape[longest]] + spot[longest + 1:]
    return entries.at[tuple(spot)].set(least).at[tuple(next_to)].set(high)


def block_levels(rng, dims, cuts, least, high):
    def one(axis_at, shards_of):
        steps = jax.random.uniform(jax.random.fold_in(jax.random.fold_in(rng, 6), axis_at), (shards_of,), jnp.float32, least / len(cuts), high / len(cuts))
        return jnp.repeat(jnp.exp(steps), dims[axis_at] // shards_of).reshape((-1,) + (1,) * (len(dims) - axis_at - 1))

    gain = one(*cuts[0])
    for cut in cuts[1:]:
        gain = gain * one(*cut)
    return gain


def normal_values(key, extent, scale, limit, cuts=(), held_as=jnp.bfloat16):
    drawn = jax.random.normal(key, extent, jnp.float32) * scale
    if len(cuts) > 0:
        drawn = block_levels(key, extent, cuts, -0.22, 0.18) * drawn
    return jnp.clip(drawn, min=-limit, max=limit).astype(held_as)


def setup_inputs(seed: int = 0) -> dict:
    arg_keys = jax.random.split(jax.random.key(seed), 5)
    features = normal_values(arg_keys[0], (FACES, FIN), 1.0, 6.0, ((0, 16), (1, 2)))
    fc_weight = normal_values(arg_keys[1], (FIN, D), FIN ** -0.5, 0.0546875, ((0, 2),))
    class_weight = normal_values(arg_keys[2], (CLASSES, D), 0.05, 0.29882812, ((0, 2),))
    labels = touch_ends(jax.random.randint(arg_keys[3], (FACES,), 0, CLASSES), jax.random.fold_in(arg_keys[3], 1), 0, CLASSES - 1).astype(jnp.int32)
    return dict(features=features, fc_weight=fc_weight, class_weight=class_weight, labels=labels)


SCALE = 64.0
MARGIN = 0.5
SOFTEN = 0.01
EPSILON = 1e-06

def margin_terms(cosine, is_target):
    sine = jnp.sqrt(1.0 + SOFTEN - cosine * cosine)
    shifted = cosine * math.cos(MARGIN) - sine * math.sin(MARGIN)
    powers = jnp.exp(SCALE * jnp.where(is_target, shifted, cosine))
    slopes = SCALE * jnp.where(is_target, math.cos(MARGIN) + math.sin(MARGIN) * cosine / sine, 1.0)
    return (powers, slopes)

def softmax_grad(powers, totals, slopes, is_target, loss_weight):
    onehot = is_target.astype(jnp.float32)
    return ((powers / totals[:, None] - onehot) * loss_weight * slopes).astype(jnp.bfloat16)

def rounded_term(left, right):
    term = jnp.dot(left, right, preferred_element_type=jnp.float32).astype(jnp.bfloat16)
    term = lax.optimization_barrier(term)
    return term.astype(jnp.float32)

def reference(features, fc_weight, class_weight, labels):
    face_count = features.shape[0]
    block_width = features.shape[1] // N_CLS
    raw_embed = jnp.zeros((face_count, fc_weight.shape[1]), jnp.float32)
    for block in range(N_CLS):
        low = block * block_width
        raw_embed = raw_embed + rounded_term(features[:, low:low + block_width], fc_weight[low:low + block_width])
    embed_norm = jnp.sqrt(lax.optimization_barrier(jnp.sum(raw_embed * raw_embed, axis=1, keepdims=True)) + EPSILON)
    unit_f = raw_embed / embed_norm
    unit_embed = unit_f.astype(jnp.bfloat16)
    class_f = class_weight.astype(jnp.float32)
    class_norm = jnp.sqrt(lax.optimization_barrier(jnp.sum(class_f * class_f, axis=1, keepdims=True)) + EPSILON)
    class_unit_f = class_f / class_norm
    class_unit = class_unit_f.astype(jnp.bfloat16)
    cosine = lax.dot_general(unit_embed, class_unit, (((1,), (1,)), ((), ())), preferred_element_type=jnp.float32)
    columns = lax.broadcasted_iota(jnp.int32, cosine.shape, 1)
    is_target = columns == labels[:, None]
    powers, slopes = margin_terms(cosine, is_target)
    totals = lax.optimization_barrier(jnp.sum(powers, axis=1))
    loss_weight = 1.0 / math.sqrt(face_count)
    cos_grad = softmax_grad(powers, totals, slopes, is_target, loss_weight)
    class_block = class_weight.shape[0] // N_CLS
    unit_grad = jnp.zeros((face_count, class_weight.shape[1]), jnp.float32)
    for block in range(N_CLS):
        low = block * class_block
        unit_grad = unit_grad + rounded_term(cos_grad[:, low:low + class_block], class_unit[low:low + class_block])
    class_part = lax.dot_general(cos_grad, unit_embed, (((0,), (0,)), ((), ())), preferred_element_type=jnp.float32)
    raw_grad = ((unit_grad - unit_f * lax.optimization_barrier(jnp.sum(unit_f * unit_grad, axis=1, keepdims=True))) / embed_norm).astype(jnp.bfloat16)
    fc_grad = lax.dot_general(features, raw_grad, (((0,), (0,)), ((), ())), preferred_element_type=jnp.float32)
    class_grad = (class_part - class_unit_f * lax.optimization_barrier(jnp.sum(class_unit_f * class_part, axis=1, keepdims=True))) / class_norm
    return (fc_grad.astype(jnp.bfloat16), class_grad.astype(jnp.bfloat16))
```

```python
import functools
import math

import jax
import jax.numpy as jnp
from jax import lax
from jax.experimental import pallas as pl
from jax.experimental.pallas import tpu as pltpu
from jax.sharding import PartitionSpec as P

SCALE = 64.0
MARGIN = 0.5
SOFTEN = 0.01
EPSILON = 1e-06


def margin_terms(cosine, is_target):
    sine = jnp.sqrt(1.0 + SOFTEN - cosine * cosine)
    shifted = cosine * math.cos(MARGIN) - sine * math.sin(MARGIN)
    powers = jnp.exp(SCALE * jnp.where(is_target, shifted, cosine))
    slopes = SCALE * jnp.where(is_target, math.cos(MARGIN) + math.sin(MARGIN) * cosine / sine, 1.0)
    return (powers, slopes)


def softmax_grad(powers, totals, slopes, is_target, loss_weight):
    onehot = is_target.astype(jnp.float32)
    return ((powers / totals[:, None] - onehot) * loss_weight * slopes).astype(jnp.bfloat16)


def shards(features, fc_weight, class_weight, labels):
    rows_group = features.shape[0]
    class_count = class_weight.shape[0]
    loss_weight = 1.0 / math.sqrt(rows_group * lax.axis_size("dp"))
    position = lax.axis_index("cls")
    rows_block = features
    raw_embed = lax.psum_scatter(
        jnp.dot(rows_block, fc_weight, preferred_element_type=jnp.float32).astype(jnp.bfloat16),
        "cls",
        scatter_dimension=0,
        tiled=True,
    ).astype(jnp.float32)
    embed_norm = jnp.sqrt(jnp.sum(raw_embed * raw_embed, axis=1, keepdims=True) + EPSILON)
    unit_f = raw_embed / embed_norm
    unit_embed = unit_f.astype(jnp.bfloat16)
    class_f = class_weight.astype(jnp.float32)
    class_norm = jnp.sqrt(jnp.sum(class_f * class_f, axis=1, keepdims=True) + EPSILON)
    class_unit_f = class_f / class_norm
    class_unit = class_unit_f.astype(jnp.bfloat16)
    faces_all = lax.all_gather(unit_embed, "cls", axis=0, tiled=True)
    cosine = lax.dot_general(
        faces_all, class_unit, (((1,), (1,)), ((), ())), preferred_element_type=jnp.float32
    )
    columns = position * class_count + lax.broadcasted_iota(jnp.int32, cosine.shape, 1)
    is_target = columns == labels[:, None]
    powers, slopes = margin_terms(cosine, is_target)
    totals = lax.psum(jnp.sum(powers, axis=1), "cls")
    cos_grad = softmax_grad(powers, totals, slopes, is_target, loss_weight)
    rows_block = cos_grad
    unit_grad = lax.psum_scatter(
        jnp.dot(rows_block, class_unit, preferred_element_type=jnp.float32).astype(jnp.bfloat16),
        "cls",
        scatter_dimension=0,
        tiled=True,
    ).astype(jnp.float32)
    class_part = lax.dot_general(
        cos_grad, faces_all, (((0,), (0,)), ((), ())), preferred_element_type=jnp.float32
    )
    raw_grad = (
        (unit_grad - unit_f * jnp.sum(unit_f * unit_grad, axis=1, keepdims=True)) / embed_norm
    ).astype(jnp.bfloat16)
    rows_block = features
    fc_part = lax.dot_general(
        rows_block,
        lax.all_gather(raw_grad, "cls", axis=0, tiled=True),
        (((0,), (0,)), ((), ())),
        preferred_element_type=jnp.float32,
    )
    fc_total, class_total = lax.psum((fc_part, class_part), "dp")
    fc_out = fc_total.astype(jnp.bfloat16)
    class_grad = (
        class_total - class_unit_f * jnp.sum(class_unit_f * class_total, axis=1, keepdims=True)
    ) / class_norm
    return (fc_out, class_grad.astype(jnp.bfloat16))


MESH = pl.DeviceIdType.MESH
LANES = 128
PLANE = 4
ROUNDED = jnp.bfloat16


def split_rows(blocks, parts):
    base, more = divmod(blocks, parts)
    runs, start = [], 0
    for part in range(parts):
        size = base + (1 if part < more else 0)
        runs.append((start * LANES, size * LANES))
        start += size
    return runs


def kernel(
    nz, chunks, faces_total,
    feat_hbm, w_hbm, cw_ref, lab_ref,
    fc_out, class_out,
    feat, w, gath, praw, rraw, unit_all, cu, tot_s, tot_r, cosg, cg_all, pgrad, rgrad,
    rg_all, cpart, cslots, cout, f, sendb, from_left, from_right, slab,
    load_sem, x_send, x_recv, p_send, p_recv, own_sem, c_send, c_recv,
    ca_send, ca_recv, cp_send, cp_recv, rs_send, rl_recv, rr_recv,
    az_send, az_recv, ay_send, ay_recv, ac_send, ac_recv, out_sem,
):
    rows, fin = feat.shape
    classes, dim = cw_ref.shape
    wide = gath.shape[1]
    per = (fin // LANES // PLANE) * LANES
    cq = classes // PLANE
    cz = cq // nz
    dp = lax.axis_index("dp")
    x = lax.axis_index("cls")
    z, q = dp // PLANE, dp % PLANE
    y, core = q // 2, q % 2
    q_y = (1 - y) * 2 + core
    q_c = y * 2 + 1 - core
    q_d = (1 - y) * 2 + 1 - core
    x_dev = {"cls": 1 - x}
    y_dev = {"dp": z * PLANE + q_y}
    c_dev = {"dp": z * PLANE + q_c}
    right = {"dp": jnp.minimum(z + 1, nz - 1) * PLANE + q}
    left = {"dp": jnp.maximum(z - 1, 0) * PLANE + q}
    plane = [(q + d) % PLANE for d in range(1, PLANE)]
    plane_from = [(q + PLANE - d) % PLANE for d in range(1, PLANE)]
    line = [(z + d) % nz for d in range(1, nz)]
    line_from = [(z + nz - d) % nz for d in range(1, nz)]
    pending = []

    def send(cond, make):
        if cond is None:
            make().start()
        else:
            @pl.when(cond)
            def _():
                make().start()
        pending.append((cond, make))

    def remote(src, dst, s, r, dev):
        return lambda: pltpu.make_async_remote_copy(
            src_ref=src(), dst_ref=dst(), send_sem=s(), recv_sem=r(),
            device_id=dev, device_id_type=MESH,
        )

    def landed(dst, r):
        pltpu.make_async_remote_copy(
            src_ref=dst, dst_ref=dst, send_sem=r, recv_sem=r,
            device_id=x_dev, device_id_type=MESH,
        ).wait_recv()

    def at(i, n):
        return pl.ds(pl.multiple_of(i * n, n), n)

    steps = load_sem.shape[0] // 2
    kk = fin // steps
    loads = []
    for k in range(steps):
        part = pl.ds(k * kk, kk)
        pair = (
            pltpu.make_async_copy(w_hbm.at[part, :], w.at[part, :], load_sem.at[2 * k]),
            pltpu.make_async_copy(feat_hbm.at[:, part], feat.at[:, part], load_sem.at[2 * k + 1]),
        )
        for copy in pair:
            copy.start()
        loads.append(pair)

    barrier = pltpu.get_barrier_semaphore()
    peers = [x_dev] + [{"dp": z * PLANE + p} for p in plane] + [{"dp": t * PLANE + q} for t in line]
    for dev in peers:
        pl.semaphore_signal(barrier, inc=1, device_id=dev, device_id_type=MESH)
    pl.semaphore_wait(barrier, len(peers))

    mine = at(q, rows)
    own_feat = pltpu.make_async_copy(
        feat_hbm.at[:, pl.ds(pl.multiple_of(q * per, LANES), wide)], gath.at[mine, :], own_sem.at[0]
    )
    own_feat.start()
    for i, p in enumerate(plane):
        cols = pl.ds(pl.multiple_of(p * per, LANES), wide)
        send(None, remote(
            lambda cols=cols: feat_hbm.at[:, cols], lambda: gath.at[mine, :],
            lambda i=i: p_send.at[0, i], lambda i=i: p_recv.at[0, i], {"dp": z * PLANE + p},
        ))

    total = jnp.zeros((rows, dim), jnp.float32)
    for k in range(steps):
        for copy in loads[k]:
            copy.wait()
        part = pl.ds(k * kk, kk)
        total = total + jnp.dot(feat[:, part], w[part, :], preferred_element_type=jnp.float32)
    praw[...] = total.astype(ROUNDED)
    send(None, remote(lambda: praw, lambda: rraw, lambda: x_send.at[0], lambda: x_recv.at[0], x_dev))

    class_f = cw_ref[...].astype(jnp.float32)
    class_norm = jnp.sqrt(jnp.sum(class_f * class_f, axis=1, keepdims=True) + EPSILON)
    cu[...] = (class_f / class_norm).astype(ROUNDED)

    landed(rraw, x_recv.at[0])
    raw = praw[...].astype(jnp.float32) + rraw[...].astype(jnp.float32)
    norm = jnp.sqrt(jnp.sum(raw * raw, axis=1, keepdims=True) + EPSILON)
    unit_f = raw / norm
    unit = unit_f.astype(ROUNDED)
    unit_all[mine, :] = unit
    for i, p in enumerate(plane):
        send(None, remote(
            lambda: unit_all.at[mine, :], lambda: unit_all.at[mine, :],
            lambda i=i: p_send.at[1, i], lambda i=i: p_recv.at[1, i], {"dp": z * PLANE + p},
        ))
    cosine = lax.dot_general(
        unit, cu[...], (((1,), (1,)), ((), ())), preferred_element_type=jnp.float32
    )
    columns = x * classes + lax.broadcasted_iota(jnp.int32, cosine.shape, 1)
    is_target = columns == lab_ref[...]
    powers, slopes = margin_terms(cosine, is_target)
    partial = jnp.sum(powers, axis=1, keepdims=True)
    tot_s[...] = jnp.broadcast_to(partial, tot_s.shape)
    send(None, remote(lambda: tot_s, lambda: tot_r, lambda: x_send.at[1], lambda: x_recv.at[1], x_dev))
    landed(tot_r, x_recv.at[1])
    totals = partial + tot_r[:, 0:1]
    weight = 1.0 / math.sqrt(faces_total)
    grad = ((powers / totals - is_target.astype(jnp.float32)) * weight * slopes).astype(ROUNDED)
    cosg[...] = grad
    pgrad[...] = jnp.dot(grad, cu[...], preferred_element_type=jnp.float32).astype(ROUNDED)
    send(None, remote(lambda: pgrad, lambda: rgrad, lambda: x_send.at[2], lambda: x_recv.at[2], x_dev))
    for i, p in enumerate(plane):
        cols = at(p, cq)
        send(None, remote(
            lambda cols=cols: cosg.at[:, cols], lambda: cg_all.at[mine, :],
            lambda i=i: p_send.at[2, i], lambda i=i: p_recv.at[2, i], {"dp": z * PLANE + p},
        ))
    cg_all[mine, :] = cosg[:, at(q, cq)]

    landed(rgrad, x_recv.at[2])
    unit_grad = pgrad[...].astype(jnp.float32) + rgrad[...].astype(jnp.float32)
    along = jnp.sum(unit_f * unit_grad, axis=1, keepdims=True)
    rg_all[mine, :] = ((unit_grad - unit_f * along) / norm).astype(ROUNDED)
    for i, p in enumerate(plane):
        send(None, remote(
            lambda: rg_all.at[mine, :], lambda: rg_all.at[mine, :],
            lambda i=i: p_send.at[3, i], lambda i=i: p_recv.at[3, i], {"dp": z * PLANE + p},
        ))

    for i, p in enumerate(plane_from):
        theirs = at(p, rows)
        landed(unit_all.at[theirs, :], p_recv.at[1, i])
        landed(cg_all.at[theirs, :], p_recv.at[2, i])
    cpart[...] = lax.dot_general(
        cg_all[...], unit_all[...], (((0,), (0,)), ((), ())), preferred_element_type=jnp.float32
    )
    for i, t in enumerate(line):
        send(None, remote(
            lambda t=t: cpart.at[at(t, cz), :], lambda: cslots.at[z],
            lambda i=i: c_send.at[i], lambda i=i: c_recv.at[i], {"dp": t * PLANE + q},
        ))

    own_feat.wait()
    for i, p in enumerate(plane_from):
        theirs = at(p, rows)
        landed(gath.at[theirs, :], p_recv.at[0, i])
        landed(rg_all.at[theirs, :], p_recv.at[3, i])

    def multiply(c):
        first, size = chunks[c]
        part = pl.ds(first, size)
        product = lax.dot_general(
            gath[:, part], rg_all[...], (((0,), (0,)), ((), ())), preferred_element_type=jnp.float32
        )
        for j in range(nz):
            f[j, part, :] = product[:, j * LANES:(j + 1) * LANES]

    def reduce(c):
        first, size = chunks[c]
        part = pl.ds(first, size)

        def pass_on(j, going, starts, arrived, sem, dev, way):
            @pl.when(jnp.logical_and(going, starts))
            def _():
                sendb[j, part, :] = f[j, part, :].astype(ROUNDED)

            @pl.when(jnp.logical_and(going, jnp.logical_not(starts)))
            def _():
                landed(arrived.at[j, part, :], sem.at[c, j])
                sendb[j, part, :] = (
                    f[j, part, :] + arrived[j, part, :].astype(jnp.float32)
                ).astype(ROUNDED)

            send(going, remote(
                lambda: sendb.at[j, part, :], lambda: arrived.at[j, part, :],
                lambda: rs_send.at[c, j], lambda: sem.at[c, j], dev,
            ))

        for i in range(nz - 1):
            j = nz - 1 - i
            pass_on(j, z < j, z == 0, from_left, rl_recv, right, 0)
            pass_on(i, z > i, z == nz - 1, from_right, rr_recv, left, 1)

        @pl.when(z > 0)
        def _():
            landed(from_left.at[z, part, :], rl_recv.at[c, z])
            f[z, part, :] += from_left[z, part, :].astype(jnp.float32)

        @pl.when(z < nz - 1)
        def _():
            landed(from_right.at[z, part, :], rr_recv.at[c, z])
            f[z, part, :] += from_right[z, part, :].astype(jnp.float32)

        slab[q, z, part, :] = f[z, part, :].astype(ROUNDED)
        spread(c, z, z < nz - 1, z > 0, None)

    def spread(c, s, to_right, to_left, there):
        first, size = chunks[c]
        part = pl.ds(first, size)
        block = lambda: slab.at[q, s, part, :]
        if to_right is not None:
            send(to_right, remote(block, block, lambda: az_send.at[c, s, 0], lambda: az_recv.at[c, s], right))
        if to_left is not None:
            send(to_left, remote(block, block, lambda: az_send.at[c, s, 1], lambda: az_recv.at[c, s], left))
        send(there, remote(block, block, lambda: ay_send.at[c, s], lambda: ay_recv.at[c, s], y_dev))
        send(there, remote(block, block, lambda: ac_send.at[0, c, s], lambda: ac_recv.at[0, c, s], c_dev))

    def gather_line(c):
        first, size = chunks[c]
        part = pl.ds(first, size)
        for d in range(1, nz):
            low, high = jnp.maximum(z - d, 0), jnp.minimum(z + d, nz - 1)
            has_low, has_high = z >= d, z + d < nz

            @pl.when(has_low)
            def _():
                landed(slab.at[q, low, part, :], az_recv.at[c, low])

            spread(c, low, jnp.logical_and(has_low, z < nz - 1), None, has_low)

            @pl.when(has_high)
            def _():
                landed(slab.at[q, high, part, :], az_recv.at[c, high])

            spread(c, high, None, jnp.logical_and(has_high, z > 0), has_high)

    def gather_across(c):
        first, size = chunks[c]
        part = pl.ds(first, size)
        for d in range(nz):
            s = (z + d) % nz
            landed(slab.at[q_y, s, part, :], ay_recv.at[c, s])
            block = lambda s=s: slab.at[q_y, s, part, :]
            send(None, remote(
                block, block, lambda s=s: ac_send.at[1, c, s], lambda s=s: ac_recv.at[1, c, s], c_dev,
            ))

    def class_rows():
        for i, t in enumerate(line_from):
            landed(cslots.at[t], c_recv.at[i])
        here = pl.ds(pl.multiple_of(q * cq + z * cz, cz), cz)
        sums = cpart[at(z, cz), :]
        for i, t in enumerate(line_from):
            sums = sums + cslots[t]
        mine_f = cw_ref[here, :].astype(jnp.float32)
        mine_norm = jnp.sqrt(jnp.sum(mine_f * mine_f, axis=1, keepdims=True) + EPSILON)
        mine_unit = mine_f / mine_norm
        along = jnp.sum(mine_unit * sums, axis=1, keepdims=True)
        cout[here, :] = ((sums - mine_unit * along) / mine_norm).astype(ROUNDED)
        for i, t in enumerate(line):
            send(None, remote(
                lambda: cout.at[here, :], lambda: cout.at[here, :],
                lambda i=i: ca_send.at[i], lambda i=i: ca_recv.at[i], {"dp": t * PLANE + q},
            ))

    def class_plane():
        for i, t in enumerate(line_from):
            there = pl.ds(pl.multiple_of(q * cq + t * cz, cz), cz)
            landed(cout.at[there, :], ca_recv.at[i])
        block = lambda: cout.at[at(q, cq), :]
        send(None, remote(block, block, lambda: cp_send.at[0], lambda: cp_recv.at[0], y_dev))
        send(None, remote(block, block, lambda: cp_send.at[1], lambda: cp_recv.at[1], c_dev))

    def class_across():
        landed(cout.at[at(q_y, cq), :], cp_recv.at[0])
        block = lambda: cout.at[at(q_y, cq), :]
        send(None, remote(block, block, lambda: cp_send.at[2], lambda: cp_recv.at[2], c_dev))

    count = len(chunks)
    for step in range(count + 2):
        if step < count:
            multiply(step)
            reduce(step)
        if step == 0:
            class_rows()
        if 1 <= step <= count:
            gather_line(step - 1)
        if step == 1:
            class_plane()
        if step >= 2:
            gather_across(step - 2)
        if step == 2:
            class_across()

    for c in range(count):
        part = pl.ds(*chunks[c])
        for s in range(nz):
            landed(slab.at[q_c, s, part, :], ac_recv.at[0, c, s])
            landed(slab.at[q_d, s, part, :], ac_recv.at[1, c, s])
    copies = []
    for p in range(PLANE):
        size = wide if p == PLANE - 1 else per
        for j in range(nz):
            copies.append(pltpu.make_async_copy(
                slab.at[p, j, pl.ds(0, size), :],
                fc_out.at[pl.ds(p * per, size), pl.ds(j * LANES, LANES)],
                out_sem.at[p * nz + j],
            ))
    for copy in copies:
        copy.start()
    landed(cout.at[at(q_c, cq), :], cp_recv.at[1])
    landed(cout.at[at(q_d, cq), :], cp_recv.at[2])
    class_out[...] = cout[...]
    for cond, make in pending:
        if cond is None:
            make().wait_send()
        else:
            @pl.when(cond)
            def _():
                make().wait_send()
    for copy in copies:
        copy.wait()


def fused(n_dp, features, fc_weight, class_weight, labels):
    rows, fin = features.shape
    classes, dim = class_weight.shape
    nz = n_dp // PLANE
    blocks = fin // LANES
    wide = (blocks - (PLANE - 1) * (blocks // PLANE)) * LANES
    chunks = split_rows(wide // LANES, min(4, wide // LANES))
    count = len(chunks)
    steps = max(d for d in range(1, 9) if blocks % d == 0)
    bf, f32, dma = jnp.bfloat16, jnp.float32, pltpu.SemaphoreType.DMA
    vmem, whole = pltpu.VMEM, pl.BlockSpec(memory_space=pltpu.VMEM)
    anywhere = pl.BlockSpec(memory_space=pl.ANY)
    return pl.pallas_call(
        functools.partial(kernel, nz, chunks, rows * n_dp),
        out_shape=(
            jax.ShapeDtypeStruct((fin, dim), bf),
            jax.ShapeDtypeStruct((classes, dim), bf),
        ),
        in_specs=[anywhere, anywhere, whole, whole],
        out_specs=(anywhere, whole),
        scratch_shapes=[
            vmem((rows, fin), bf), vmem((fin, dim), bf), vmem((PLANE * rows, wide), bf),
            vmem((rows, dim), bf), vmem((rows, dim), bf), vmem((PLANE * rows, dim), bf),
            vmem((classes, dim), bf), vmem((rows, LANES), f32), vmem((rows, LANES), f32),
            vmem((rows, classes), bf), vmem((PLANE * rows, classes // PLANE), bf),
            vmem((rows, dim), bf), vmem((rows, dim), bf), vmem((PLANE * rows, dim), bf),
            vmem((classes // PLANE, dim), f32), vmem((nz, classes // PLANE // nz, dim), f32),
            vmem((classes, dim), bf), vmem((nz, wide, LANES), f32),
            vmem((nz, wide, LANES), bf), vmem((nz, wide, LANES), bf), vmem((nz, wide, LANES), bf),
            vmem((PLANE, nz, wide, LANES), bf),
            dma((2 * steps,)), dma((3,)), dma((3,)), dma((4, PLANE - 1)), dma((4, PLANE - 1)),
            dma((1,)), dma((nz - 1,)), dma((nz - 1,)), dma((nz - 1,)), dma((nz - 1,)),
            dma((3,)), dma((3,)), dma((count, nz)), dma((count, nz)), dma((count, nz)),
            dma((count, nz, 2)), dma((count, nz)), dma((count, nz)), dma((count, nz)),
            dma((2, count, nz)), dma((2, count, nz)), dma((PLANE * nz,)),
        ],
        compiler_params=pltpu.CompilerParams(
            collective_id=0, has_side_effects=True, vmem_limit_bytes=52 * 2**20
        ),
    )(features, fc_weight, class_weight, labels.reshape(rows, 1))


def choose(n_dp, n_cls, features, fc_weight, class_weight, labels):
    rows, fin = features.shape
    classes, dim = class_weight.shape
    nz = n_dp // PLANE
    fits = (
        n_cls == 2
        and n_dp % PLANE == 0
        and nz > 1
        and dim == nz * LANES
        and fin % LANES == 0
        and fin // LANES >= PLANE
        and rows % 16 == 0
        and rows <= 128
        and classes % (PLANE * LANES) == 0
        and classes // PLANE % (16 * nz) == 0
        and classes <= 512
        and fin <= 6272
    )
    if fits:
        return fused(n_dp, features, fc_weight, class_weight, labels)
    return shards(features, fc_weight, class_weight, labels)


def solution(mesh):
    placed = (P("dp", "cls"), P("cls", None), P("cls", None), P("dp"))
    return jax.shard_map(
        functools.partial(choose, mesh.shape["dp"], mesh.shape["cls"]),
        mesh=mesh,
        in_specs=placed,
        out_specs=(P("cls", None), P("cls", None)),
        check_vma=False,
    )
```

```python
import functools
import math

import jax
import jax.numpy as jnp
from jax import lax
from jax.experimental import pallas as pl
from jax.experimental.pallas import tpu as pltpu
from jax.sharding import PartitionSpec as P

SCALE = 64.0
MARGIN = 0.5
SOFTEN = 0.01
EPSILON = 1e-06


def margin_terms(cosine, is_target):
    sine = jnp.sqrt(1.0 + SOFTEN - cosine * cosine)
    shifted = cosine * math.cos(MARGIN) - sine * math.sin(MARGIN)
    powers = jnp.exp(SCALE * jnp.where(is_target, shifted, cosine))
    slopes = SCALE * jnp.where(is_target, math.cos(MARGIN) + math.sin(MARGIN) * cosine / sine, 1.0)
    return (powers, slopes)


def softmax_grad(powers, totals, slopes, is_target, loss_weight):
    onehot = is_target.astype(jnp.float32)
    return ((powers / totals[:, None] - onehot) * loss_weight * slopes).astype(jnp.bfloat16)


def shards(features, fc_weight, class_weight, labels):
    rows_group = features.shape[0]
    class_count = class_weight.shape[0]
    loss_weight = 1.0 / math.sqrt(rows_group * lax.axis_size("dp"))
    position = lax.axis_index("cls")
    rows_block = features
    raw_embed = lax.psum_scatter(
        jnp.dot(rows_block, fc_weight, preferred_element_type=jnp.float32).astype(jnp.bfloat16),
        "cls",
        scatter_dimension=0,
        tiled=True,
    ).astype(jnp.float32)
    embed_norm = jnp.sqrt(jnp.sum(raw_embed * raw_embed, axis=1, keepdims=True) + EPSILON)
    unit_f = raw_embed / embed_norm
    unit_embed = unit_f.astype(jnp.bfloat16)
    class_f = class_weight.astype(jnp.float32)
    class_norm = jnp.sqrt(jnp.sum(class_f * class_f, axis=1, keepdims=True) + EPSILON)
    class_unit_f = class_f / class_norm
    class_unit = class_unit_f.astype(jnp.bfloat16)
    faces_all = lax.all_gather(unit_embed, "cls", axis=0, tiled=True)
    cosine = lax.dot_general(
        faces_all, class_unit, (((1,), (1,)), ((), ())), preferred_element_type=jnp.float32
    )
    columns = position * class_count + lax.broadcasted_iota(jnp.int32, cosine.shape, 1)
    is_target = columns == labels[:, None]
    powers, slopes = margin_terms(cosine, is_target)
    totals = lax.psum(jnp.sum(powers, axis=1), "cls")
    cos_grad = softmax_grad(powers, totals, slopes, is_target, loss_weight)
    rows_block = cos_grad
    unit_grad = lax.psum_scatter(
        jnp.dot(rows_block, class_unit, preferred_element_type=jnp.float32).astype(jnp.bfloat16),
        "cls",
        scatter_dimension=0,
        tiled=True,
    ).astype(jnp.float32)
    class_part = lax.dot_general(
        cos_grad, faces_all, (((0,), (0,)), ((), ())), preferred_element_type=jnp.float32
    )
    raw_grad = (
        (unit_grad - unit_f * jnp.sum(unit_f * unit_grad, axis=1, keepdims=True)) / embed_norm
    ).astype(jnp.bfloat16)
    rows_block = features
    fc_part = lax.dot_general(
        rows_block,
        lax.all_gather(raw_grad, "cls", axis=0, tiled=True),
        (((0,), (0,)), ((), ())),
        preferred_element_type=jnp.float32,
    )
    fc_total, class_total = lax.psum((fc_part, class_part), "dp")
    fc_out = fc_total.astype(jnp.bfloat16)
    class_grad = (
        class_total - class_unit_f * jnp.sum(class_unit_f * class_total, axis=1, keepdims=True)
    ) / class_norm
    return (fc_out, class_grad.astype(jnp.bfloat16))


MESH = pl.DeviceIdType.MESH
LANES = 128
PLANE = 4
ROUNDED = jnp.bfloat16


def split_rows(blocks, parts):
    base, more = divmod(blocks, parts)
    runs, start = [], 0
    for part in range(parts):
        size = base + (1 if part < more else 0)
        runs.append((start * LANES, size * LANES))
        start += size
    return runs


def kernel(
    nz, chunks, faces_total,
    feat_hbm, w_hbm, cw_hbm, lab_hbm,
    fc_out, cout,
    slab, feat, w, cw_ref, lab_ref, gath, praw, rraw, unit_all, cu, tot_s, tot_r, cosg, cg_all, pgrad, rgrad,
    rg_all, cpart, cslots, f, send1, recv1, send2, recv2,
    load_sem, x_send, x_recv, p_send, p_recv, own_sem, c_send, c_recv,
    ca_send, ca_recv, cp_send, cp_recv, z_send, z_recv, y_send, y_recv, n_send, n_recv, out_sem,
):
    rows, fin = feat.shape
    classes, dim = cw_ref.shape
    wide = gath.shape[1]
    per = (fin // LANES // PLANE) * LANES
    cq = classes // PLANE
    cz = cq // nz
    dp = lax.axis_index("dp")
    x = lax.axis_index("cls")
    z, q = dp // PLANE, dp % PLANE
    y, core = q // 2, q % 2
    q_y = (1 - y) * 2 + core
    q_c = y * 2 + 1 - core
    q_d = (1 - y) * 2 + 1 - core
    x_dev = {"cls": 1 - x}
    y_dev = {"dp": z * PLANE + q_y}
    c_dev = {"dp": z * PLANE + q_c}
    half, side = z // 2, z % 2
    near = {"dp": (half * 2 + 1 - side) * PLANE + q}
    far = {"dp": ((1 - half) * 2 + side) * PLANE + q}
    owned = side * 2 + half
    plane = [(q + d) % PLANE for d in range(1, PLANE)]
    plane_from = [(q + PLANE - d) % PLANE for d in range(1, PLANE)]
    line = [(z + d) % nz for d in range(1, nz)]
    line_from = [(z + nz - d) % nz for d in range(1, nz)]
    pending = []

    def send(cond, make):
        if cond is None:
            make().start()
        else:
            @pl.when(cond)
            def _():
                make().start()
        pending.append((cond, make))

    def remote(src, dst, s, r, dev):
        return lambda: pltpu.make_async_remote_copy(
            src_ref=src(), dst_ref=dst(), send_sem=s(), recv_sem=r(),
            device_id=dev, device_id_type=MESH,
        )

    def landed(dst, r):
        pltpu.make_async_remote_copy(
            src_ref=dst, dst_ref=dst, send_sem=r, recv_sem=r,
            device_id=x_dev, device_id_type=MESH,
        ).wait_recv()

    def at(i, n):
        return pl.ds(pl.multiple_of(i * n, n), n)

    small = [
        pltpu.make_async_copy(cw_hbm, cw_ref, own_sem.at[1]),
        pltpu.make_async_copy(lab_hbm, lab_ref, own_sem.at[2]),
    ]
    for copy in small:
        copy.start()
    steps = load_sem.shape[0] // 2
    kk = fin // steps
    loads = []
    for k in range(steps):
        part = pl.ds(k * kk, kk)
        pair = (
            pltpu.make_async_copy(w_hbm.at[part, :], w.at[part, :], load_sem.at[2 * k]),
            pltpu.make_async_copy(feat_hbm.at[:, part], feat.at[:, part], load_sem.at[2 * k + 1]),
        )
        for copy in pair:
            copy.start()
        loads.append(pair)

    barrier = pltpu.get_barrier_semaphore()
    peers = [x_dev] + [{"dp": z * PLANE + p} for p in plane] + [{"dp": t * PLANE + q} for t in line]
    for dev in peers:
        pl.semaphore_signal(barrier, inc=1, device_id=dev, device_id_type=MESH)
    pl.semaphore_wait(barrier, len(peers))

    mine = at(q, rows)
    own_feat = pltpu.make_async_copy(
        feat_hbm.at[:, pl.ds(pl.multiple_of(q * per, LANES), wide)], gath.at[mine, :], own_sem.at[0]
    )
    own_feat.start()
    for i, p in enumerate(plane):
        cols = pl.ds(pl.multiple_of(p * per, LANES), wide)
        send(None, remote(
            lambda cols=cols: feat_hbm.at[:, cols], lambda: gath.at[mine, :],
            lambda i=i: p_send.at[0, i], lambda i=i: p_recv.at[0, i], {"dp": z * PLANE + p},
        ))

    total = jnp.zeros((rows, dim), jnp.float32)
    for k in range(steps):
        for copy in loads[k]:
            copy.wait()
        part = pl.ds(k * kk, kk)
        total = total + jnp.dot(feat[:, part], w[part, :], preferred_element_type=jnp.float32)
    praw[...] = total.astype(ROUNDED)
    send(None, remote(lambda: praw, lambda: rraw, lambda: x_send.at[0], lambda: x_recv.at[0], x_dev))

    for copy in small:
        copy.wait()
    class_f = cw_ref[...].astype(jnp.float32)
    class_norm = jnp.sqrt(jnp.sum(class_f * class_f, axis=1, keepdims=True) + EPSILON)
    cu[...] = (class_f / class_norm).astype(ROUNDED)

    landed(rraw, x_recv.at[0])
    raw = praw[...].astype(jnp.float32) + rraw[...].astype(jnp.float32)
    norm = jnp.sqrt(jnp.sum(raw * raw, axis=1, keepdims=True) + EPSILON)
    unit_f = raw / norm
    unit = unit_f.astype(ROUNDED)
    unit_all[mine, :] = unit
    for i, p in enumerate(plane):
        send(None, remote(
            lambda: unit_all.at[mine, :], lambda: unit_all.at[mine, :],
            lambda i=i: p_send.at[1, i], lambda i=i: p_recv.at[1, i], {"dp": z * PLANE + p},
        ))
    cosine = lax.dot_general(
        unit, cu[...], (((1,), (1,)), ((), ())), preferred_element_type=jnp.float32
    )
    columns = x * classes + lax.broadcasted_iota(jnp.int32, cosine.shape, 1)
    label = jnp.broadcast_to(lab_ref[...], (LANES, rows)).T[:, 0:1]
    is_target = columns == label
    powers, slopes = margin_terms(cosine, is_target)
    partial = jnp.sum(powers, axis=1, keepdims=True)
    tot_s[...] = jnp.broadcast_to(partial, tot_s.shape)
    send(None, remote(lambda: tot_s, lambda: tot_r, lambda: x_send.at[1], lambda: x_recv.at[1], x_dev))
    landed(tot_r, x_recv.at[1])
    totals = partial + tot_r[:, 0:1]
    weight = 1.0 / math.sqrt(faces_total)
    grad = ((powers / totals - is_target.astype(jnp.float32)) * weight * slopes).astype(ROUNDED)
    cosg[...] = grad
    pgrad[...] = jnp.dot(grad, cu[...], preferred_element_type=jnp.float32).astype(ROUNDED)
    send(None, remote(lambda: pgrad, lambda: rgrad, lambda: x_send.at[2], lambda: x_recv.at[2], x_dev))
    for i, p in enumerate(plane):
        cols = at(p, cq)
        send(None, remote(
            lambda cols=cols: cosg.at[:, cols], lambda: cg_all.at[mine, :],
            lambda i=i: p_send.at[2, i], lambda i=i: p_recv.at[2, i], {"dp": z * PLANE + p},
        ))
    cg_all[mine, :] = cosg[:, at(q, cq)]

    landed(rgrad, x_recv.at[2])
    unit_grad = pgrad[...].astype(jnp.float32) + rgrad[...].astype(jnp.float32)
    along = jnp.sum(unit_f * unit_grad, axis=1, keepdims=True)
    rg_all[mine, :] = ((unit_grad - unit_f * along) / norm).astype(ROUNDED)
    for i, p in enumerate(plane):
        send(None, remote(
            lambda: rg_all.at[mine, :], lambda: rg_all.at[mine, :],
            lambda i=i: p_send.at[3, i], lambda i=i: p_recv.at[3, i], {"dp": z * PLANE + p},
        ))

    for i, p in enumerate(plane_from):
        theirs = at(p, rows)
        landed(unit_all.at[theirs, :], p_recv.at[1, i])
        landed(cg_all.at[theirs, :], p_recv.at[2, i])
    cpart[...] = lax.dot_general(
        cg_all[...], unit_all[...], (((0,), (0,)), ((), ())), preferred_element_type=jnp.float32
    )
    for i, t in enumerate(line):
        send(None, remote(
            lambda t=t: cpart.at[at(t, cz), :], lambda: cslots.at[z],
            lambda i=i: c_send.at[i], lambda i=i: c_recv.at[i], {"dp": t * PLANE + q},
        ))

    own_feat.wait()
    for i, p in enumerate(plane_from):
        theirs = at(p, rows)
        landed(gath.at[theirs, :], p_recv.at[0, i])
        landed(rg_all.at[theirs, :], p_recv.at[3, i])

    count = len(chunks)
    split = max(count - 3, 0)
    writes = []

    def exchange(src, dst, sends, recvs, dev, *spot):
        send(None, remote(
            lambda: src, lambda: dst, lambda: sends.at[spot], lambda: recvs.at[spot], dev,
        ))

    def pair(p, which, part):
        return slab.at[p, pl.ds(which * 2, 2), part, :]

    def multiply(c, part):
        product = lax.dot_general(
            gath[:, part], rg_all[...], (((0,), (0,)), ((), ())), preferred_element_type=jnp.float32
        )
        for j in range(nz):
            f[j, part, :] = product[:, j * LANES:(j + 1) * LANES]
        for i in range(2):
            send1[i, part, :] = f[(1 - side) * 2 + i, part, :].astype(ROUNDED)
        exchange(send1.at[:, part, :], recv1.at[:, part, :], z_send, z_recv, near, 0, c)

    def sum_near(c, part):
        landed(recv1.at[:, part, :], z_recv.at[0, c])
        send2[part, :] = (
            f[side * 2 + 1 - half, part, :] + recv1[1 - half, part, :].astype(jnp.float32)
        ).astype(ROUNDED)
        exchange(send2.at[part, :], recv2.at[part, :], z_send, z_recv, far, 1, c)

    def sum_far(c, part):
        landed(recv2.at[part, :], z_recv.at[1, c])
        slab[q, owned, part, :] = (
            f[owned, part, :]
            + recv1[half, part, :].astype(jnp.float32)
            + recv2[part, :].astype(jnp.float32)
        ).astype(ROUNDED)
        block = slab.at[q, owned, part, :]
        exchange(block, block, z_send, z_recv, far, 2, c)

    def gather_far(c, part):
        landed(slab.at[q, side * 2 + 1 - half, part, :], z_recv.at[2, c])
        block = pair(q, side, part)
        exchange(block, block, z_send, z_recv, near, 3, c)
        exchange(block, block, y_send, y_recv, y_dev, side, c)
        exchange(block, block, n_send, n_recv, c_dev, side, c)

    def gather_near(c, part):
        block = pair(q, 1 - side, part)
        landed(block, z_recv.at[3, c])
        exchange(block, block, y_send, y_recv, y_dev, 1 - side, c)
        exchange(block, block, n_send, n_recv, c_dev, 1 - side, c)

    def gather_across(c, part):
        for which in (side, 1 - side):
            block = pair(q_y, which, part)
            landed(block, y_recv.at[which, c])
            exchange(block, block, n_send, n_recv, c_dev, 2 + which, c)

    def gather_core(c, part):
        for which in range(2):
            landed(pair(q_c, which, part), n_recv.at[which, c])
            landed(pair(q_d, which, part), n_recv.at[2 + which, c])
        if c in (split, count - 1):
            low = 0 if c == split else chunks[split + 1][0]
            high = part.start + part.size
            for p in range(PLANE):
                size = (high if p == PLANE - 1 else min(high, per)) - low
                for j in range(nz):
                    copy = pltpu.make_async_copy(
                        slab.at[p, j, pl.ds(low, size), :],
                        fc_out.at[pl.ds(p * per + low, size), pl.ds(j * LANES, LANES)],
                        out_sem.at[int(c != split), p * nz + j],
                    )
                    copy.start()
                    writes.append(copy)

    def class_rows():
        for i, t in enumerate(line_from):
            landed(cslots.at[t], c_recv.at[i])
        here = pl.ds(pl.multiple_of(q * cq + z * cz, cz), cz)
        sums = cpart[at(z, cz), :]
        for i, t in enumerate(line_from):
            sums = sums + cslots[t]
        mine_f = cw_ref[here, :].astype(jnp.float32)
        mine_norm = jnp.sqrt(jnp.sum(mine_f * mine_f, axis=1, keepdims=True) + EPSILON)
        mine_unit = mine_f / mine_norm
        along = jnp.sum(mine_unit * sums, axis=1, keepdims=True)
        cout[here, :] = ((sums - mine_unit * along) / mine_norm).astype(ROUNDED)
        for i, t in enumerate(line):
            send(None, remote(
                lambda: cout.at[here, :], lambda: cout.at[here, :],
                lambda i=i: ca_send.at[i], lambda i=i: ca_recv.at[i], {"dp": t * PLANE + q},
            ))

    def class_plane():
        for i, t in enumerate(line_from):
            there = pl.ds(pl.multiple_of(q * cq + t * cz, cz), cz)
            landed(cout.at[there, :], ca_recv.at[i])
        block = lambda: cout.at[at(q, cq), :]
        send(None, remote(block, block, lambda: cp_send.at[0], lambda: cp_recv.at[0], y_dev))
        send(None, remote(block, block, lambda: cp_send.at[1], lambda: cp_recv.at[1], c_dev))

    def class_across():
        landed(cout.at[at(q_y, cq), :], cp_recv.at[0])
        block = lambda: cout.at[at(q_y, cq), :]
        send(None, remote(block, block, lambda: cp_send.at[2], lambda: cp_recv.at[2], c_dev))

    stages = (multiply, sum_near, sum_far, gather_far, gather_near, gather_across, gather_core)
    for tick in range(count + len(stages) - 1):
        for stage, run in enumerate(stages):
            c = tick - stage
            if 0 <= c < count:
                run(c, pl.ds(*chunks[c]))
        if tick == 1:
            class_rows()
        if tick == 2:
            class_plane()
        if tick == 3:
            class_across()

    landed(cout.at[at(q_c, cq), :], cp_recv.at[1])
    landed(cout.at[at(q_d, cq), :], cp_recv.at[2])
    for cond, make in pending:
        make().wait_send()
    for copy in writes:
        copy.wait()


def place(fc_in, class_in, fc_out, class_out, sems):
    pieces = sems.shape[0] - 1
    size = fc_in.shape[0] // pieces
    copies = [pltpu.make_async_copy(class_in, class_out, sems.at[pieces])]
    for i in range(pieces):
        part = pl.ds(i * size, size)
        copies.append(pltpu.make_async_copy(fc_in.at[part, :], fc_out.at[part, :], sems.at[i]))
    for copy in copies:
        copy.start()
    for copy in copies:
        copy.wait()


def fused(n_dp, features, fc_weight, class_weight, labels):
    rows, fin = features.shape
    classes, dim = class_weight.shape
    nz = n_dp // PLANE
    blocks = fin // LANES
    wide = (blocks - (PLANE - 1) * (blocks // PLANE)) * LANES
    chunks = split_rows(wide // LANES, min(7, wide // LANES))
    count = len(chunks)
    steps = max(d for d in range(1, 9) if blocks % d == 0)
    bf, f32, dma = jnp.bfloat16, jnp.float32, pltpu.SemaphoreType.DMA
    vmem, whole = pltpu.VMEM, pl.BlockSpec(memory_space=pltpu.VMEM)
    anywhere = pl.BlockSpec(memory_space=pl.ANY)
    results = pl.pallas_call(
        functools.partial(kernel, nz, chunks, rows * n_dp),
        out_shape=(
            jax.ShapeDtypeStruct((fin, dim), bf),
            jax.ShapeDtypeStruct((classes, dim), bf),
        ),
        in_specs=[anywhere] * 4,
        out_specs=(anywhere, whole),
        scratch_shapes=[
            vmem((PLANE, nz, wide, LANES), bf), vmem((rows, fin), bf), vmem((fin, dim), bf), vmem((classes, dim), bf),
            vmem((1, rows), jnp.int32), vmem((PLANE * rows, wide), bf),
            vmem((rows, dim), bf), vmem((rows, dim), bf), vmem((PLANE * rows, dim), bf),
            vmem((classes, dim), bf), vmem((rows, LANES), f32), vmem((rows, LANES), f32),
            vmem((rows, classes), bf), vmem((PLANE * rows, classes // PLANE), bf),
            vmem((rows, dim), bf), vmem((rows, dim), bf), vmem((PLANE * rows, dim), bf),
            vmem((classes // PLANE, dim), f32), vmem((nz, classes // PLANE // nz, dim), f32),
            vmem((nz, wide, LANES), f32), vmem((2, wide, LANES), bf), vmem((2, wide, LANES), bf),
            vmem((wide, LANES), bf), vmem((wide, LANES), bf),
            dma((2 * steps,)), dma((3,)), dma((3,)), dma((4, PLANE - 1)), dma((4, PLANE - 1)),
            dma((3,)), dma((nz - 1,)), dma((nz - 1,)), dma((nz - 1,)), dma((nz - 1,)),
            dma((3,)), dma((3,)), dma((4, count)), dma((4, count)),
            dma((2, count)), dma((2, count)), dma((4, count)), dma((4, count)),
            dma((2, PLANE * nz)),
        ],
        compiler_params=pltpu.CompilerParams(
            collective_id=0, has_side_effects=True, vmem_limit_bytes=56 * 2**20
        ),
    )(features, fc_weight, class_weight, labels.reshape(1, rows))
    return pl.pallas_call(
        place,
        out_shape=(
            jax.ShapeDtypeStruct((fin, dim), bf),
            jax.ShapeDtypeStruct((classes, dim), bf),
        ),
        in_specs=[anywhere, anywhere],
        out_specs=(anywhere, anywhere),
        scratch_shapes=[dma((steps + 1,))],
        compiler_params=pltpu.CompilerParams(vmem_limit_bytes=56 * 2**20),
    )(*results)


def choose(n_dp, n_cls, features, fc_weight, class_weight, labels):
    rows, fin = features.shape
    classes, dim = class_weight.shape
    nz = n_dp // PLANE
    fits = (
        n_cls == 2
        and n_dp % PLANE == 0
        and nz == 4
        and dim == nz * LANES
        and fin % LANES == 0
        and fin // LANES >= PLANE
        and rows == LANES
        and classes % (PLANE * LANES) == 0
        and classes // PLANE % (16 * nz) == 0
        and classes <= 512
        and fin <= 6272
    )
    if fits:
        return fused(n_dp, features, fc_weight, class_weight, labels)
    return shards(features, fc_weight, class_weight, labels)


def solution(mesh):
    placed = (P("dp", "cls"), P("cls", None), P("cls", None), P("dp"))
    return jax.shard_map(
        functools.partial(choose, mesh.shape["dp"], mesh.shape["cls"]),
        mesh=mesh,
        in_specs=placed,
        out_specs=(P("cls", None), P("cls", None)),
        check_vma=False,
    )
```

```python
import functools
import math

import jax
import jax.numpy as jnp
from jax import lax
from jax.experimental import pallas as pl
from jax.experimental.pallas import tpu as pltpu
from jax.sharding import PartitionSpec as P

SCALE = 64.0
MARGIN = 0.5
SOFTEN = 0.01
EPSILON = 1e-06


def margin_terms(cosine, is_target):
    sine = jnp.sqrt(1.0 + SOFTEN - cosine * cosine)
    shifted = cosine * math.cos(MARGIN) - sine * math.sin(MARGIN)
    powers = jnp.exp(SCALE * jnp.where(is_target, shifted, cosine))
    slopes = SCALE * jnp.where(is_target, math.cos(MARGIN) + math.sin(MARGIN) * cosine / sine, 1.0)
    return (powers, slopes)


def softmax_grad(powers, totals, slopes, is_target, loss_weight):
    onehot = is_target.astype(jnp.float32)
    return ((powers / totals[:, None] - onehot) * loss_weight * slopes).astype(jnp.bfloat16)


def shards(features, fc_weight, class_weight, labels):
    rows_group = features.shape[0]
    class_count = class_weight.shape[0]
    loss_weight = 1.0 / math.sqrt(rows_group * lax.axis_size("dp"))
    position = lax.axis_index("cls")
    rows_block = features
    raw_embed = lax.psum_scatter(
        jnp.dot(rows_block, fc_weight, preferred_element_type=jnp.float32).astype(jnp.bfloat16),
        "cls",
        scatter_dimension=0,
        tiled=True,
    ).astype(jnp.float32)
    embed_norm = jnp.sqrt(jnp.sum(raw_embed * raw_embed, axis=1, keepdims=True) + EPSILON)
    unit_f = raw_embed / embed_norm
    unit_embed = unit_f.astype(jnp.bfloat16)
    class_f = class_weight.astype(jnp.float32)
    class_norm = jnp.sqrt(jnp.sum(class_f * class_f, axis=1, keepdims=True) + EPSILON)
    class_unit_f = class_f / class_norm
    class_unit = class_unit_f.astype(jnp.bfloat16)
    faces_all = lax.all_gather(unit_embed, "cls", axis=0, tiled=True)
    cosine = lax.dot_general(
        faces_all, class_unit, (((1,), (1,)), ((), ())), preferred_element_type=jnp.float32
    )
    columns = position * class_count + lax.broadcasted_iota(jnp.int32, cosine.shape, 1)
    is_target = columns == labels[:, None]
    powers, slopes = margin_terms(cosine, is_target)
    totals = lax.psum(jnp.sum(powers, axis=1), "cls")
    cos_grad = softmax_grad(powers, totals, slopes, is_target, loss_weight)
    rows_block = cos_grad
    unit_grad = lax.psum_scatter(
        jnp.dot(rows_block, class_unit, preferred_element_type=jnp.float32).astype(jnp.bfloat16),
        "cls",
        scatter_dimension=0,
        tiled=True,
    ).astype(jnp.float32)
    class_part = lax.dot_general(
        cos_grad, faces_all, (((0,), (0,)), ((), ())), preferred_element_type=jnp.float32
    )
    raw_grad = (
        (unit_grad - unit_f * jnp.sum(unit_f * unit_grad, axis=1, keepdims=True)) / embed_norm
    ).astype(jnp.bfloat16)
    rows_block = features
    fc_part = lax.dot_general(
        rows_block,
        lax.all_gather(raw_grad, "cls", axis=0, tiled=True),
        (((0,), (0,)), ((), ())),
        preferred_element_type=jnp.float32,
    )
    fc_total, class_total = lax.psum((fc_part, class_part), "dp")
    fc_out = fc_total.astype(jnp.bfloat16)
    class_grad = (
        class_total - class_unit_f * jnp.sum(class_unit_f * class_total, axis=1, keepdims=True)
    ) / class_norm
    return (fc_out, class_grad.astype(jnp.bfloat16))


MESH = pl.DeviceIdType.MESH
LANES = 128
PLANE = 4
ROUNDED = jnp.bfloat16


def split_rows(blocks, parts):
    base, more = divmod(blocks, parts)
    runs, start = [], 0
    for part in range(parts):
        size = base + (1 if part < more else 0)
        runs.append((start * LANES, size * LANES))
        start += size
    return runs


def kernel(
    nz, chunks, faces_total,
    feat_hbm, w_hbm, cw_hbm, lab_hbm,
    fc_out, cout,
    slab, feat, w, cw_ref, lab_ref, gath, praw, rraw, unit_all, cu, tot_s, tot_r, cosg, cg_all, pgrad, rgrad,
    rg_all, cpart, cslots, f, send1, recv1, send2, recv2,
    load_sem, x_send, x_recv, p_send, p_recv, own_sem, c_send, c_recv,
    ca_send, ca_recv, cp_send, cp_recv, z_send, z_recv, y_send, y_recv, n_send, n_recv, out_sem,
):
    rows, fin = feat.shape
    classes, dim = cw_ref.shape
    wide = gath.shape[1]
    per = (fin // LANES // PLANE) * LANES
    cq = classes // PLANE
    cz = cq // nz
    dp = lax.axis_index("dp")
    x = lax.axis_index("cls")
    z, q = dp // PLANE, dp % PLANE
    y, core = q // 2, q % 2
    q_y = (1 - y) * 2 + core
    q_c = y * 2 + 1 - core
    q_d = (1 - y) * 2 + 1 - core
    x_dev = {"cls": 1 - x}
    y_dev = {"dp": z * PLANE + q_y}
    c_dev = {"dp": z * PLANE + q_c}
    half, side = z // 2, z % 2
    near = {"dp": (half * 2 + 1 - side) * PLANE + q}
    far = {"dp": ((1 - half) * 2 + side) * PLANE + q}
    owned = side * 2 + half
    plane = [(q + d) % PLANE for d in range(1, PLANE)]
    plane_from = [(q + PLANE - d) % PLANE for d in range(1, PLANE)]
    line = [(z + d) % nz for d in range(1, nz)]
    line_from = [(z + nz - d) % nz for d in range(1, nz)]
    pending = []

    def send(cond, make):
        if cond is None:
            make().start()
        else:
            @pl.when(cond)
            def _():
                make().start()
        pending.append((cond, make))

    def remote(src, dst, s, r, dev):
        return lambda: pltpu.make_async_remote_copy(
            src_ref=src(), dst_ref=dst(), send_sem=s(), recv_sem=r(),
            device_id=dev, device_id_type=MESH,
        )

    def landed(dst, r):
        pltpu.make_async_remote_copy(
            src_ref=dst, dst_ref=dst, send_sem=r, recv_sem=r,
            device_id=x_dev, device_id_type=MESH,
        ).wait_recv()

    def at(i, n):
        return pl.ds(pl.multiple_of(i * n, n), n)

    small = [
        pltpu.make_async_copy(cw_hbm, cw_ref, own_sem.at[1]),
        pltpu.make_async_copy(lab_hbm, lab_ref, own_sem.at[2]),
    ]
    for copy in small:
        copy.start()
    steps = load_sem.shape[0] // 2
    kk = fin // steps
    loads = []
    for k in range(steps):
        part = pl.ds(k * kk, kk)
        pair = (
            pltpu.make_async_copy(w_hbm.at[part, :], w.at[part, :], load_sem.at[2 * k]),
            pltpu.make_async_copy(feat_hbm.at[:, part], feat.at[:, part], load_sem.at[2 * k + 1]),
        )
        for copy in pair:
            copy.start()
        loads.append(pair)

    barrier = pltpu.get_barrier_semaphore()
    peers = [x_dev] + [{"dp": z * PLANE + p} for p in plane] + [{"dp": t * PLANE + q} for t in line]
    for dev in peers:
        pl.semaphore_signal(barrier, inc=1, device_id=dev, device_id_type=MESH)
    pl.semaphore_wait(barrier, len(peers))

    mine = at(q, rows)
    own_feat = pltpu.make_async_copy(
        feat_hbm.at[:, pl.ds(pl.multiple_of(q * per, LANES), wide)], gath.at[mine, :], own_sem.at[0]
    )
    own_feat.start()
    for i, p in enumerate(plane):
        cols = pl.ds(pl.multiple_of(p * per, LANES), wide)
        send(None, remote(
            lambda cols=cols: feat_hbm.at[:, cols], lambda: gath.at[mine, :],
            lambda i=i: p_send.at[0, i], lambda i=i: p_recv.at[0, i], {"dp": z * PLANE + p},
        ))

    total = jnp.zeros((rows, dim), jnp.float32)
    for k in range(steps):
        for copy in loads[k]:
            copy.wait()
        part = pl.ds(k * kk, kk)
        total = total + jnp.dot(feat[:, part], w[part, :], preferred_element_type=jnp.float32)
    praw[...] = total.astype(ROUNDED)
    send(None, remote(lambda: praw, lambda: rraw, lambda: x_send.at[0], lambda: x_recv.at[0], x_dev))

    for copy in small:
        copy.wait()
    class_f = cw_ref[...].astype(jnp.float32)
    class_norm = jnp.sqrt(jnp.sum(class_f * class_f, axis=1, keepdims=True) + EPSILON)
    cu[...] = (class_f / class_norm).astype(ROUNDED)

    landed(rraw, x_recv.at[0])
    raw = praw[...].astype(jnp.float32) + rraw[...].astype(jnp.float32)
    norm = jnp.sqrt(jnp.sum(raw * raw, axis=1, keepdims=True) + EPSILON)
    unit_f = raw / norm
    unit = unit_f.astype(ROUNDED)
    unit_all[mine, :] = unit
    for i, p in enumerate(plane):
        send(None, remote(
            lambda: unit_all.at[mine, :], lambda: unit_all.at[mine, :],
            lambda i=i: p_send.at[1, i], lambda i=i: p_recv.at[1, i], {"dp": z * PLANE + p},
        ))
    cosine = lax.dot_general(
        unit, cu[...], (((1,), (1,)), ((), ())), preferred_element_type=jnp.float32
    )
    columns = x * classes + lax.broadcasted_iota(jnp.int32, cosine.shape, 1)
    label = jnp.broadcast_to(lab_ref[...], (LANES, rows)).T[:, 0:1]
    is_target = columns == label
    powers, slopes = margin_terms(cosine, is_target)
    partial = jnp.sum(powers, axis=1, keepdims=True)
    tot_s[...] = jnp.broadcast_to(partial, (rows, LANES)).T[0:8, :]
    send(None, remote(lambda: tot_s, lambda: tot_r, lambda: x_send.at[1], lambda: x_recv.at[1], x_dev))
    landed(tot_r, x_recv.at[1])
    totals = partial + jnp.broadcast_to(tot_r[0:1, :], (LANES, rows)).T[:, 0:1]
    weight = 1.0 / math.sqrt(faces_total)
    grad = ((powers / totals - is_target.astype(jnp.float32)) * weight * slopes).astype(ROUNDED)
    cosg[...] = grad
    pgrad[...] = jnp.dot(grad, cu[...], preferred_element_type=jnp.float32).astype(ROUNDED)
    send(None, remote(lambda: pgrad, lambda: rgrad, lambda: x_send.at[2], lambda: x_recv.at[2], x_dev))
    for i, p in enumerate(plane):
        cols = at(p, cq)
        send(None, remote(
            lambda cols=cols: cosg.at[:, cols], lambda: cg_all.at[mine, :],
            lambda i=i: p_send.at[2, i], lambda i=i: p_recv.at[2, i], {"dp": z * PLANE + p},
        ))
    cg_all[mine, :] = cosg[:, at(q, cq)]

    landed(rgrad, x_recv.at[2])
    unit_grad = pgrad[...].astype(jnp.float32) + rgrad[...].astype(jnp.float32)
    along = jnp.sum(unit_f * unit_grad, axis=1, keepdims=True)
    rg_all[mine, :] = ((unit_grad - unit_f * along) / norm).astype(ROUNDED)
    for i, p in enumerate(plane):
        send(None, remote(
            lambda: rg_all.at[mine, :], lambda: rg_all.at[mine, :],
            lambda i=i: p_send.at[3, i], lambda i=i: p_recv.at[3, i], {"dp": z * PLANE + p},
        ))

    for i, p in enumerate(plane_from):
        theirs = at(p, rows)
        landed(unit_all.at[theirs, :], p_recv.at[1, i])
        landed(cg_all.at[theirs, :], p_recv.at[2, i])
    cpart[...] = lax.dot_general(
        cg_all[...], unit_all[...], (((0,), (0,)), ((), ())), preferred_element_type=jnp.float32
    )
    for i, t in enumerate(line):
        send(None, remote(
            lambda t=t: cpart.at[at(t, cz), :], lambda: cslots.at[z],
            lambda i=i: c_send.at[i], lambda i=i: c_recv.at[i], {"dp": t * PLANE + q},
        ))

    own_feat.wait()
    for i, p in enumerate(plane_from):
        theirs = at(p, rows)
        landed(gath.at[theirs, :], p_recv.at[0, i])
        landed(rg_all.at[theirs, :], p_recv.at[3, i])

    count = len(chunks)
    split = max(count - 3, 0)
    writes = []

    def exchange(src, dst, sends, recvs, dev, *spot):
        send(None, remote(
            lambda: src, lambda: dst, lambda: sends.at[spot], lambda: recvs.at[spot], dev,
        ))

    def pair(p, which, part):
        return slab.at[p, pl.ds(which * 2, 2), part, :]

    def multiply(c, part):
        product = lax.dot_general(
            gath[:, part], rg_all[...], (((0,), (0,)), ((), ())), preferred_element_type=jnp.float32
        )
        for j in range(nz):
            f[j, part, :] = product[:, j * LANES:(j + 1) * LANES]
        for i in range(2):
            send1[i, part, :] = f[(1 - side) * 2 + i, part, :].astype(ROUNDED)
        exchange(send1.at[:, part, :], recv1.at[:, part, :], z_send, z_recv, near, 0, c)

    def sum_near(c, part):
        landed(recv1.at[:, part, :], z_recv.at[0, c])
        send2[part, :] = (
            f[side * 2 + 1 - half, part, :] + recv1[1 - half, part, :].astype(jnp.float32)
        ).astype(ROUNDED)
        exchange(send2.at[part, :], recv2.at[part, :], z_send, z_recv, far, 1, c)

    def sum_far(c, part):
        landed(recv2.at[part, :], z_recv.at[1, c])
        slab[q, owned, part, :] = (
            f[owned, part, :]
            + recv1[half, part, :].astype(jnp.float32)
            + recv2[part, :].astype(jnp.float32)
        ).astype(ROUNDED)
        block = slab.at[q, owned, part, :]
        exchange(block, block, z_send, z_recv, far, 2, c)

    def gather_far(c, part):
        landed(slab.at[q, side * 2 + 1 - half, part, :], z_recv.at[2, c])
        block = pair(q, side, part)
        exchange(block, block, z_send, z_recv, near, 3, c)
        exchange(block, block, y_send, y_recv, y_dev, side, c)
        exchange(block, block, n_send, n_recv, c_dev, side, c)

    def gather_near(c, part):
        block = pair(q, 1 - side, part)
        landed(block, z_recv.at[3, c])
        exchange(block, block, y_send, y_recv, y_dev, 1 - side, c)
        exchange(block, block, n_send, n_recv, c_dev, 1 - side, c)

    def gather_across(c, part):
        for which in (side, 1 - side):
            block = pair(q_y, which, part)
            landed(block, y_recv.at[which, c])
            exchange(block, block, n_send, n_recv, c_dev, 2 + which, c)

    def gather_core(c, part):
        for which in range(2):
            landed(pair(q_c, which, part), n_recv.at[which, c])
            landed(pair(q_d, which, part), n_recv.at[2 + which, c])
        if c in (split, count - 1):
            low = 0 if c == split else chunks[split + 1][0]
            high = part.start + part.size
            for p in range(PLANE):
                size = (high if p == PLANE - 1 else min(high, per)) - low
                for j in range(nz):
                    copy = pltpu.make_async_copy(
                        slab.at[p, j, pl.ds(low, size), :],
                        fc_out.at[pl.ds(p * per + low, size), pl.ds(j * LANES, LANES)],
                        out_sem.at[int(c != split), p * nz + j],
                    )
                    copy.start()
                    writes.append(copy)

    def class_rows():
        for i, t in enumerate(line_from):
            landed(cslots.at[t], c_recv.at[i])
        here = pl.ds(pl.multiple_of(q * cq + z * cz, cz), cz)
        sums = cpart[at(z, cz), :]
        for i, t in enumerate(line_from):
            sums = sums + cslots[t]
        mine_f = cw_ref[here, :].astype(jnp.float32)
        mine_norm = jnp.sqrt(jnp.sum(mine_f * mine_f, axis=1, keepdims=True) + EPSILON)
        mine_unit = mine_f / mine_norm
        along = jnp.sum(mine_unit * sums, axis=1, keepdims=True)
        cout[here, :] = ((sums - mine_unit * along) / mine_norm).astype(ROUNDED)
        for i, t in enumerate(line):
            send(None, remote(
                lambda: cout.at[here, :], lambda: cout.at[here, :],
                lambda i=i: ca_send.at[i], lambda i=i: ca_recv.at[i], {"dp": t * PLANE + q},
            ))

    def class_plane():
        for i, t in enumerate(line_from):
            there = pl.ds(pl.multiple_of(q * cq + t * cz, cz), cz)
            landed(cout.at[there, :], ca_recv.at[i])
        block = lambda: cout.at[at(q, cq), :]
        send(None, remote(block, block, lambda: cp_send.at[0], lambda: cp_recv.at[0], y_dev))
        send(None, remote(block, block, lambda: cp_send.at[1], lambda: cp_recv.at[1], c_dev))

    def class_across():
        landed(cout.at[at(q_y, cq), :], cp_recv.at[0])
        block = lambda: cout.at[at(q_y, cq), :]
        send(None, remote(block, block, lambda: cp_send.at[2], lambda: cp_recv.at[2], c_dev))

    stages = (multiply, sum_near, sum_far, gather_far, gather_near, gather_across, gather_core)
    for tick in range(count + len(stages) - 1):
        for stage, run in enumerate(stages):
            c = tick - stage
            if 0 <= c < count:
                run(c, pl.ds(*chunks[c]))
        if tick == 1:
            class_rows()
        if tick == 2:
            class_plane()
        if tick == 3:
            class_across()

    landed(cout.at[at(q_c, cq), :], cp_recv.at[1])
    landed(cout.at[at(q_d, cq), :], cp_recv.at[2])
    for cond, make in pending:
        make().wait_send()
    for copy in writes:
        copy.wait()


def place(fc_in, class_in, fc_out, class_out):
    fc_out[...] = fc_in[...]
    class_out[...] = class_in[...]


def fused(n_dp, features, fc_weight, class_weight, labels):
    rows, fin = features.shape
    classes, dim = class_weight.shape
    nz = n_dp // PLANE
    blocks = fin // LANES
    wide = (blocks - (PLANE - 1) * (blocks // PLANE)) * LANES
    chunks = split_rows(wide // LANES, min(13, wide // LANES))
    count = len(chunks)
    steps = max(d for d in range(1, 9) if blocks % d == 0)
    bf, f32, dma = jnp.bfloat16, jnp.float32, pltpu.SemaphoreType.DMA
    vmem, whole = pltpu.VMEM, pl.BlockSpec(memory_space=pltpu.VMEM)
    anywhere = pl.BlockSpec(memory_space=pl.ANY)
    results = pl.pallas_call(
        functools.partial(kernel, nz, chunks, rows * n_dp),
        out_shape=(
            jax.ShapeDtypeStruct((fin, dim), bf),
            jax.ShapeDtypeStruct((classes, dim), bf),
        ),
        in_specs=[anywhere] * 4,
        out_specs=(anywhere, whole),
        scratch_shapes=[
            vmem((PLANE, nz, wide, LANES), bf), vmem((rows, fin), bf), vmem((fin, dim), bf), vmem((classes, dim), bf),
            vmem((1, rows), jnp.int32), vmem((PLANE * rows, wide), bf),
            vmem((rows, dim), bf), vmem((rows, dim), bf), vmem((PLANE * rows, dim), bf),
            vmem((classes, dim), bf), vmem((8, rows), f32), vmem((8, rows), f32),
            vmem((rows, classes), bf), vmem((PLANE * rows, classes // PLANE), bf),
            vmem((rows, dim), bf), vmem((rows, dim), bf), vmem((PLANE * rows, dim), bf),
            vmem((classes // PLANE, dim), f32), vmem((nz, classes // PLANE // nz, dim), f32),
            vmem((nz, wide, LANES), f32), vmem((2, wide, LANES), bf), vmem((2, wide, LANES), bf),
            vmem((wide, LANES), bf), vmem((wide, LANES), bf),
            dma((2 * steps,)), dma((3,)), dma((3,)), dma((4, PLANE - 1)), dma((4, PLANE - 1)),
            dma((3,)), dma((nz - 1,)), dma((nz - 1,)), dma((nz - 1,)), dma((nz - 1,)),
            dma((3,)), dma((3,)), dma((4, count)), dma((4, count)),
            dma((2, count)), dma((2, count)), dma((4, count)), dma((4, count)),
            dma((2, PLANE * nz)),
        ],
        compiler_params=pltpu.CompilerParams(
            collective_id=0, has_side_effects=True, vmem_limit_bytes=56 * 2**20
        ),
    )(features, fc_weight, class_weight, labels.reshape(1, rows))
    blocks_of = tuple(
        pl.BlockSpec((size // steps if size % (16 * steps) == 0 else size, dim),
                     (lambda i: (i, 0)) if size % (16 * steps) == 0 else (lambda i: (0, 0)))
        for size in (fin, classes)
    )
    return pl.pallas_call(
        place,
        grid=(steps,),
        out_shape=(
            jax.ShapeDtypeStruct((fin, dim), bf),
            jax.ShapeDtypeStruct((classes, dim), bf),
        ),
        in_specs=blocks_of,
        out_specs=blocks_of,
        compiler_params=pltpu.CompilerParams(vmem_limit_bytes=56 * 2**20),
    )(*results)


def choose(n_dp, n_cls, features, fc_weight, class_weight, labels):
    rows, fin = features.shape
    classes, dim = class_weight.shape
    nz = n_dp // PLANE
    fits = (
        n_cls == 2
        and n_dp % PLANE == 0
        and nz == 4
        and dim == nz * LANES
        and fin % LANES == 0
        and fin // LANES >= PLANE
        and rows == LANES
        and classes % (PLANE * LANES) == 0
        and classes // PLANE % (16 * nz) == 0
        and classes <= 512
        and fin <= 6272
    )
    if fits:
        return fused(n_dp, features, fc_weight, class_weight, labels)
    return shards(features, fc_weight, class_weight, labels)


def solution(mesh):
    placed = (P("dp", "cls"), P("cls", None), P("cls", None), P("dp"))
    return jax.shard_map(
        functools.partial(choose, mesh.shape["dp"], mesh.shape["cls"]),
        mesh=mesh,
        in_specs=placed,
        out_specs=(P("cls", None), P("cls", None)),
        check_vma=False,
    )
```

```python
import functools
import math

import jax
import jax.numpy as jnp
from jax import lax
from jax.experimental import pallas as pl
from jax.experimental.pallas import tpu as pltpu
from jax.sharding import PartitionSpec as P

SCALE = 64.0
MARGIN = 0.5
SOFTEN = 0.01
EPSILON = 1e-06


def margin_terms(cosine, is_target):
    sine = jnp.sqrt(1.0 + SOFTEN - cosine * cosine)
    shifted = cosine * math.cos(MARGIN) - sine * math.sin(MARGIN)
    powers = jnp.exp(SCALE * jnp.where(is_target, shifted, cosine))
    slopes = SCALE * jnp.where(is_target, math.cos(MARGIN) + math.sin(MARGIN) * cosine / sine, 1.0)
    return (powers, slopes)


def softmax_grad(powers, totals, slopes, is_target, loss_weight):
    onehot = is_target.astype(jnp.float32)
    return ((powers / totals[:, None] - onehot) * loss_weight * slopes).astype(jnp.bfloat16)


def shards(features, fc_weight, class_weight, labels):
    rows_group = features.shape[0]
    class_count = class_weight.shape[0]
    loss_weight = 1.0 / math.sqrt(rows_group * lax.axis_size("dp"))
    position = lax.axis_index("cls")
    rows_block = features
    raw_embed = lax.psum_scatter(
        jnp.dot(rows_block, fc_weight, preferred_element_type=jnp.float32).astype(jnp.bfloat16),
        "cls",
        scatter_dimension=0,
        tiled=True,
    ).astype(jnp.float32)
    embed_norm = jnp.sqrt(jnp.sum(raw_embed * raw_embed, axis=1, keepdims=True) + EPSILON)
    unit_f = raw_embed / embed_norm
    unit_embed = unit_f.astype(jnp.bfloat16)
    class_f = class_weight.astype(jnp.float32)
    class_norm = jnp.sqrt(jnp.sum(class_f * class_f, axis=1, keepdims=True) + EPSILON)
    class_unit_f = class_f / class_norm
    class_unit = class_unit_f.astype(jnp.bfloat16)
    faces_all = lax.all_gather(unit_embed, "cls", axis=0, tiled=True)
    cosine = lax.dot_general(
        faces_all, class_unit, (((1,), (1,)), ((), ())), preferred_element_type=jnp.float32
    )
    columns = position * class_count + lax.broadcasted_iota(jnp.int32, cosine.shape, 1)
    is_target = columns == labels[:, None]
    powers, slopes = margin_terms(cosine, is_target)
    totals = lax.psum(jnp.sum(powers, axis=1), "cls")
    cos_grad = softmax_grad(powers, totals, slopes, is_target, loss_weight)
    rows_block = cos_grad
    unit_grad = lax.psum_scatter(
        jnp.dot(rows_block, class_unit, preferred_element_type=jnp.float32).astype(jnp.bfloat16),
        "cls",
        scatter_dimension=0,
        tiled=True,
    ).astype(jnp.float32)
    class_part = lax.dot_general(
        cos_grad, faces_all, (((0,), (0,)), ((), ())), preferred_element_type=jnp.float32
    )
    raw_grad = (
        (unit_grad - unit_f * jnp.sum(unit_f * unit_grad, axis=1, keepdims=True)) / embed_norm
    ).astype(jnp.bfloat16)
    rows_block = features
    fc_part = lax.dot_general(
        rows_block,
        lax.all_gather(raw_grad, "cls", axis=0, tiled=True),
        (((0,), (0,)), ((), ())),
        preferred_element_type=jnp.float32,
    )
    fc_total, class_total = lax.psum((fc_part, class_part), "dp")
    fc_out = fc_total.astype(jnp.bfloat16)
    class_grad = (
        class_total - class_unit_f * jnp.sum(class_unit_f * class_total, axis=1, keepdims=True)
    ) / class_norm
    return (fc_out, class_grad.astype(jnp.bfloat16))


MESH = pl.DeviceIdType.MESH
LANES = 128
PLANE = 4
ROUNDED = jnp.bfloat16


def split_rows(blocks, parts):
    base, more = divmod(blocks, parts)
    runs, start = [], 0
    for part in range(parts):
        size = base + (1 if part < more else 0)
        runs.append((start * LANES, size * LANES))
        start += size
    return runs


def kernel(
    nz, chunks, faces_total,
    feat_hbm, w_hbm, cw_hbm, lab_hbm,
    *refs,
):
    count = len(chunks)
    slabs, refs = refs[:count], refs[count:]
    kernel_body(nz, chunks, faces_total, feat_hbm, w_hbm, cw_hbm, lab_hbm, slabs, *refs)


def kernel_body(
    nz, chunks, faces_total,
    feat_hbm, w_hbm, cw_hbm, lab_hbm,
    slabs, cout,
    feat, w, cw_ref, lab_ref, gath, praw, rraw, unit_all, cu, tot_s, tot_r, cosg, cg_all, pgrad, rgrad,
    rg_all, cpart, cslots, f, send1, recv1, send2, recv2,
    load_sem, x_send, x_recv, p_send, p_recv, own_sem, c_send, c_recv,
    ca_send, ca_recv, cp_send, cp_recv, z_send, z_recv, y_send, y_recv, n_send, n_recv,
):
    rows, fin = feat.shape
    classes, dim = cw_ref.shape
    wide = gath.shape[1]
    per = (fin // LANES // PLANE) * LANES
    cq = classes // PLANE
    cz = cq // nz
    dp = lax.axis_index("dp")
    x = lax.axis_index("cls")
    z, q = dp // PLANE, dp % PLANE
    y, core = q // 2, q % 2
    q_y = (1 - y) * 2 + core
    q_c = y * 2 + 1 - core
    q_d = (1 - y) * 2 + 1 - core
    x_dev = {"cls": 1 - x}
    y_dev = {"dp": z * PLANE + q_y}
    c_dev = {"dp": z * PLANE + q_c}
    half, side = z // 2, z % 2
    near = {"dp": (half * 2 + 1 - side) * PLANE + q}
    far = {"dp": ((1 - half) * 2 + side) * PLANE + q}
    owned = side * 2 + half
    plane = [(q + d) % PLANE for d in range(1, PLANE)]
    plane_from = [(q + PLANE - d) % PLANE for d in range(1, PLANE)]
    line = [(z + d) % nz for d in range(1, nz)]
    line_from = [(z + nz - d) % nz for d in range(1, nz)]
    pending = []

    def send(cond, make):
        if cond is None:
            make().start()
        else:
            @pl.when(cond)
            def _():
                make().start()
        pending.append((cond, make))

    def remote(src, dst, s, r, dev):
        return lambda: pltpu.make_async_remote_copy(
            src_ref=src(), dst_ref=dst(), send_sem=s(), recv_sem=r(),
            device_id=dev, device_id_type=MESH,
        )

    def landed(dst, r):
        pltpu.make_async_remote_copy(
            src_ref=dst, dst_ref=dst, send_sem=r, recv_sem=r,
            device_id=x_dev, device_id_type=MESH,
        ).wait_recv()

    def at(i, n):
        return pl.ds(pl.multiple_of(i * n, n), n)

    small = [
        pltpu.make_async_copy(cw_hbm, cw_ref, own_sem.at[1]),
        pltpu.make_async_copy(lab_hbm, lab_ref, own_sem.at[2]),
    ]
    for copy in small:
        copy.start()
    steps = load_sem.shape[0] // 2
    kk = fin // steps
    loads = []
    for k in range(steps):
        part = pl.ds(k * kk, kk)
        pair = (
            pltpu.make_async_copy(w_hbm.at[part, :], w.at[part, :], load_sem.at[2 * k]),
            pltpu.make_async_copy(feat_hbm.at[:, part], feat.at[:, part], load_sem.at[2 * k + 1]),
        )
        for copy in pair:
            copy.start()
        loads.append(pair)

    barrier = pltpu.get_barrier_semaphore()
    peers = [x_dev] + [{"dp": z * PLANE + p} for p in plane] + [{"dp": t * PLANE + q} for t in line]
    for dev in peers:
        pl.semaphore_signal(barrier, inc=1, device_id=dev, device_id_type=MESH)
    pl.semaphore_wait(barrier, len(peers))

    mine = at(q, rows)
    own_feat = pltpu.make_async_copy(
        feat_hbm.at[:, pl.ds(pl.multiple_of(q * per, LANES), wide)], gath.at[mine, :], own_sem.at[0]
    )
    own_feat.start()
    total = jnp.zeros((rows, dim), jnp.float32)
    for k in range(steps):
        for copy in loads[k]:
            copy.wait()
        part = pl.ds(k * kk, kk)
        total = total + jnp.dot(feat[:, part], w[part, :], preferred_element_type=jnp.float32)
    praw[...] = total.astype(ROUNDED)
    send(None, remote(lambda: praw, lambda: rraw, lambda: x_send.at[0], lambda: x_recv.at[0], x_dev))

    for i, p in enumerate(plane):
        cols = pl.ds(pl.multiple_of(p * per, LANES), wide)
        send(None, remote(
            lambda cols=cols: feat.at[:, cols], lambda: gath.at[mine, :],
            lambda i=i: p_send.at[0, i], lambda i=i: p_recv.at[0, i], {"dp": z * PLANE + p},
        ))

    for copy in small:
        copy.wait()
    class_f = cw_ref[...].astype(jnp.float32)
    class_norm = jnp.sqrt(jnp.sum(class_f * class_f, axis=1, keepdims=True) + EPSILON)
    cu[...] = (class_f / class_norm).astype(ROUNDED)

    landed(rraw, x_recv.at[0])
    raw = praw[...].astype(jnp.float32) + rraw[...].astype(jnp.float32)
    norm = jnp.sqrt(jnp.sum(raw * raw, axis=1, keepdims=True) + EPSILON)
    unit_f = raw / norm
    unit = unit_f.astype(ROUNDED)
    unit_all[mine, :] = unit
    for i, p in enumerate(plane):
        send(None, remote(
            lambda: unit_all.at[mine, :], lambda: unit_all.at[mine, :],
            lambda i=i: p_send.at[1, i], lambda i=i: p_recv.at[1, i], {"dp": z * PLANE + p},
        ))
    cosine = lax.dot_general(
        unit, cu[...], (((1,), (1,)), ((), ())), preferred_element_type=jnp.float32
    )
    columns = x * classes + lax.broadcasted_iota(jnp.int32, cosine.shape, 1)
    label = jnp.broadcast_to(lab_ref[...], (LANES, rows)).T[:, 0:1]
    is_target = columns == label
    powers, slopes = margin_terms(cosine, is_target)
    partial = jnp.sum(powers, axis=1, keepdims=True)
    tot_s[...] = jnp.broadcast_to(partial, (rows, LANES)).T[0:8, :]
    send(None, remote(lambda: tot_s, lambda: tot_r, lambda: x_send.at[1], lambda: x_recv.at[1], x_dev))
    landed(tot_r, x_recv.at[1])
    totals = partial + jnp.broadcast_to(tot_r[0:1, :], (LANES, rows)).T[:, 0:1]
    weight = 1.0 / math.sqrt(faces_total)
    grad = ((powers / totals - is_target.astype(jnp.float32)) * weight * slopes).astype(ROUNDED)
    cosg[...] = grad
    pgrad[...] = jnp.dot(grad, cu[...], preferred_element_type=jnp.float32).astype(ROUNDED)
    send(None, remote(lambda: pgrad, lambda: rgrad, lambda: x_send.at[2], lambda: x_recv.at[2], x_dev))
    for i, p in enumerate(plane):
        cols = at(p, cq)
        send(None, remote(
            lambda cols=cols: cosg.at[:, cols], lambda: cg_all.at[mine, :],
            lambda i=i: p_send.at[2, i], lambda i=i: p_recv.at[2, i], {"dp": z * PLANE + p},
        ))
    cg_all[mine, :] = cosg[:, at(q, cq)]

    landed(rgrad, x_recv.at[2])
    unit_grad = pgrad[...].astype(jnp.float32) + rgrad[...].astype(jnp.float32)
    along = jnp.sum(unit_f * unit_grad, axis=1, keepdims=True)
    rg_all[mine, :] = ((unit_grad - unit_f * along) / norm).astype(ROUNDED)
    for i, p in enumerate(plane):
        send(None, remote(
            lambda: rg_all.at[mine, :], lambda: rg_all.at[mine, :],
            lambda i=i: p_send.at[3, i], lambda i=i: p_recv.at[3, i], {"dp": z * PLANE + p},
        ))

    for i, p in enumerate(plane_from):
        theirs = at(p, rows)
        landed(unit_all.at[theirs, :], p_recv.at[1, i])
        landed(cg_all.at[theirs, :], p_recv.at[2, i])
    cpart[...] = lax.dot_general(
        cg_all[...], unit_all[...], (((0,), (0,)), ((), ())), preferred_element_type=jnp.float32
    )
    for i, t in enumerate(line):
        send(None, remote(
            lambda t=t: cpart.at[at(t, cz), :], lambda: cslots.at[z],
            lambda i=i: c_send.at[i], lambda i=i: c_recv.at[i], {"dp": t * PLANE + q},
        ))

    own_feat.wait()
    for i, p in enumerate(plane_from):
        theirs = at(p, rows)
        landed(gath.at[theirs, :], p_recv.at[0, i])
        landed(rg_all.at[theirs, :], p_recv.at[3, i])

    count = len(chunks)

    def exchange(src, dst, sends, recvs, dev, *spot):
        send(None, remote(
            lambda: src, lambda: dst, lambda: sends.at[spot], lambda: recvs.at[spot], dev,
        ))

    def pair(c, p, which):
        return slabs[c].at[p, pl.ds(which * 2, 2), :, :]

    def multiply(c, part):
        product = lax.dot_general(
            gath[:, part], rg_all[...], (((0,), (0,)), ((), ())), preferred_element_type=jnp.float32
        )
        for j in range(nz):
            f[j, part, :] = product[:, j * LANES:(j + 1) * LANES]
        for i in range(2):
            send1[i, part, :] = f[(1 - side) * 2 + i, part, :].astype(ROUNDED)
        exchange(send1.at[:, part, :], recv1.at[:, part, :], z_send, z_recv, near, 0, c)

    def sum_near(c, part):
        landed(recv1.at[:, part, :], z_recv.at[0, c])
        send2[part, :] = (
            f[side * 2 + 1 - half, part, :] + recv1[1 - half, part, :].astype(jnp.float32)
        ).astype(ROUNDED)
        exchange(send2.at[part, :], recv2.at[part, :], z_send, z_recv, far, 1, c)

    def sum_far(c, part):
        landed(recv2.at[part, :], z_recv.at[1, c])
        slabs[c][q, owned, :, :] = (
            f[owned, part, :]
            + recv1[half, part, :].astype(jnp.float32)
            + recv2[part, :].astype(jnp.float32)
        ).astype(ROUNDED)
        block = slabs[c].at[q, owned, :, :]
        exchange(block, block, z_send, z_recv, far, 2, c)

    def gather_far(c, part):
        landed(slabs[c].at[q, side * 2 + 1 - half, :, :], z_recv.at[2, c])
        block = pair(c, q, side)
        exchange(block, block, z_send, z_recv, near, 3, c)
        exchange(block, block, y_send, y_recv, y_dev, side, c)
        exchange(block, block, n_send, n_recv, c_dev, side, c)

    def gather_near(c, part):
        block = pair(c, q, 1 - side)
        landed(block, z_recv.at[3, c])
        exchange(block, block, y_send, y_recv, y_dev, 1 - side, c)
        exchange(block, block, n_send, n_recv, c_dev, 1 - side, c)

    def gather_across(c, part):
        for which in (side, 1 - side):
            block = pair(c, q_y, which)
            landed(block, y_recv.at[which, c])
            exchange(block, block, n_send, n_recv, c_dev, 2 + which, c)

    def gather_core(c, part):
        for which in range(2):
            landed(pair(c, q_c, which), n_recv.at[which, c])
            landed(pair(c, q_d, which), n_recv.at[2 + which, c])

    def class_rows():
        for i, t in enumerate(line_from):
            landed(cslots.at[t], c_recv.at[i])
        here = pl.ds(pl.multiple_of(q * cq + z * cz, cz), cz)
        sums = cpart[at(z, cz), :]
        for i, t in enumerate(line_from):
            sums = sums + cslots[t]
        mine_f = cw_ref[here, :].astype(jnp.float32)
        mine_norm = jnp.sqrt(jnp.sum(mine_f * mine_f, axis=1, keepdims=True) + EPSILON)
        mine_unit = mine_f / mine_norm
        along = jnp.sum(mine_unit * sums, axis=1, keepdims=True)
        cout[here, :] = ((sums - mine_unit * along) / mine_norm).astype(ROUNDED)
        for i, t in enumerate(line):
            send(None, remote(
                lambda: cout.at[here, :], lambda: cout.at[here, :],
                lambda i=i: ca_send.at[i], lambda i=i: ca_recv.at[i], {"dp": t * PLANE + q},
            ))

    def class_plane():
        for i, t in enumerate(line_from):
            there = pl.ds(pl.multiple_of(q * cq + t * cz, cz), cz)
            landed(cout.at[there, :], ca_recv.at[i])
        block = lambda: cout.at[at(q, cq), :]
        send(None, remote(block, block, lambda: cp_send.at[0], lambda: cp_recv.at[0], y_dev))
        send(None, remote(block, block, lambda: cp_send.at[1], lambda: cp_recv.at[1], c_dev))

    def class_across():
        landed(cout.at[at(q_y, cq), :], cp_recv.at[0])
        block = lambda: cout.at[at(q_y, cq), :]
        send(None, remote(block, block, lambda: cp_send.at[2], lambda: cp_recv.at[2], c_dev))

    stages = (multiply, sum_near, sum_far, gather_far, gather_near, gather_across, gather_core)
    for tick in range(count + len(stages) - 1):
        for stage, run in enumerate(stages):
            c = tick - stage
            if 0 <= c < count:
                run(c, pl.ds(*chunks[c]))
        if tick == 1:
            class_rows()
        if tick == 2:
            class_plane()
        if tick == 3:
            class_across()

    landed(cout.at[at(q_c, cq), :], cp_recv.at[1])
    landed(cout.at[at(q_d, cq), :], cp_recv.at[2])
    for cond, make in pending:
        make().wait_send()


def place(chunks, per, *refs):
    count = len(chunks)
    slabs, cout = refs[:count], refs[count]
    fc_out, class_out, rows_of, sems = refs[count + 1:]
    copies = [pltpu.make_async_copy(cout, class_out, sems.at[0])]
    copies[0].start()
    for p in range(PLANE):
        for c, (first, size) in enumerate(chunks):
            size = size if p == PLANE - 1 else min(size, per - first)
            if size > 0:
                start = p * per + first
                for j in range(slabs[c].shape[1]):
                    rows_of[pl.ds(start, size), pl.ds(j * LANES, LANES)] = slabs[c][p, j, pl.ds(0, size), :]
                copies.append(pltpu.make_async_copy(
                    rows_of.at[pl.ds(start, size), :], fc_out.at[pl.ds(start, size), :], sems.at[len(copies)],
                ))
                copies[-1].start()
    for copy in copies:
        copy.wait()


def fused(n_dp, features, fc_weight, class_weight, labels):
    rows, fin = features.shape
    classes, dim = class_weight.shape
    nz = n_dp // PLANE
    blocks = fin // LANES
    wide = (blocks - (PLANE - 1) * (blocks // PLANE)) * LANES
    chunks = split_rows(wide // LANES, min(7, wide // LANES))
    count = len(chunks)
    steps = max(d for d in range(1, 9) if blocks % d == 0)
    bf, f32, dma = jnp.bfloat16, jnp.float32, pltpu.SemaphoreType.DMA
    vmem, whole = pltpu.VMEM, pl.BlockSpec(memory_space=pltpu.VMEM)
    anywhere = pl.BlockSpec(memory_space=pl.ANY)
    results = pl.pallas_call(
        functools.partial(kernel, nz, chunks, rows * n_dp),
        out_shape=(
            *[jax.ShapeDtypeStruct((PLANE, nz, size, LANES), bf) for _, size in chunks],
            jax.ShapeDtypeStruct((classes, dim), bf),
        ),
        in_specs=[anywhere] * 4,
        out_specs=(whole,) * (count + 1),
        scratch_shapes=[
            vmem((rows, fin), bf), vmem((fin, dim), bf), vmem((classes, dim), bf),
            vmem((1, rows), jnp.int32), vmem((PLANE * rows, wide), bf),
            vmem((rows, dim), bf), vmem((rows, dim), bf), vmem((PLANE * rows, dim), bf),
            vmem((classes, dim), bf), vmem((8, rows), f32), vmem((8, rows), f32),
            vmem((rows, classes), bf), vmem((PLANE * rows, classes // PLANE), bf),
            vmem((rows, dim), bf), vmem((rows, dim), bf), vmem((PLANE * rows, dim), bf),
            vmem((classes // PLANE, dim), f32), vmem((nz, classes // PLANE // nz, dim), f32),
            vmem((nz, wide, LANES), f32), vmem((2, wide, LANES), bf), vmem((2, wide, LANES), bf),
            vmem((wide, LANES), bf), vmem((wide, LANES), bf),
            dma((2 * steps,)), dma((3,)), dma((3,)), dma((4, PLANE - 1)), dma((4, PLANE - 1)),
            dma((3,)), dma((nz - 1,)), dma((nz - 1,)), dma((nz - 1,)), dma((nz - 1,)),
            dma((3,)), dma((3,)), dma((4, count)), dma((4, count)),
            dma((2, count)), dma((2, count)), dma((4, count)), dma((4, count)),
        ],
        compiler_params=pltpu.CompilerParams(
            collective_id=0, has_side_effects=True, vmem_limit_bytes=46 * 2**20
        ),
    )(features, fc_weight, class_weight, labels.reshape(1, rows))
    return pl.pallas_call(
        functools.partial(place, chunks, blocks // PLANE * LANES),
        out_shape=(
            jax.ShapeDtypeStruct((fin, dim), bf),
            jax.ShapeDtypeStruct((classes, dim), bf),
        ),
        in_specs=[whole] * (count + 1),
        out_specs=(anywhere, anywhere),
        scratch_shapes=[vmem((fin, dim), bf), dma((PLANE * count + 1,))],
        compiler_params=pltpu.CompilerParams(vmem_limit_bytes=16 * 2**20),
    )(*results)


def choose(n_dp, n_cls, features, fc_weight, class_weight, labels):
    rows, fin = features.shape
    classes, dim = class_weight.shape
    nz = n_dp // PLANE
    fits = (
        n_cls == 2
        and n_dp % PLANE == 0
        and nz == 4
        and dim == nz * LANES
        and fin % LANES == 0
        and fin // LANES >= PLANE
        and rows == LANES
        and classes % (PLANE * LANES) == 0
        and classes // PLANE % (16 * nz) == 0
        and classes <= 512
        and fin <= 6272
    )
    if fits:
        return fused(n_dp, features, fc_weight, class_weight, labels)
    return shards(features, fc_weight, class_weight, labels)


def solution(mesh):
    placed = (P("dp", "cls"), P("cls", None), P("cls", None), P("dp"))
    return jax.shard_map(
        functools.partial(choose, mesh.shape["dp"], mesh.shape["cls"]),
        mesh=mesh,
        in_specs=placed,
        out_specs=(P("cls", None), P("cls", None)),
        check_vma=False,
    )
```

```python
import functools
import math

import jax
import jax.numpy as jnp
from jax import lax
from jax.experimental import pallas as pl
from jax.experimental.pallas import tpu as pltpu
from jax.sharding import PartitionSpec as P

SCALE = 64.0
MARGIN = 0.5
SOFTEN = 0.01
EPSILON = 1e-06


def margin_terms(cosine, is_target):
    sine = jnp.sqrt(1.0 + SOFTEN - cosine * cosine)
    shifted = cosine * math.cos(MARGIN) - sine * math.sin(MARGIN)
    powers = jnp.exp(SCALE * jnp.where(is_target, shifted, cosine))
    slopes = SCALE * jnp.where(is_target, math.cos(MARGIN) + math.sin(MARGIN) * cosine / sine, 1.0)
    return (powers, slopes)


def softmax_grad(powers, totals, slopes, is_target, loss_weight):
    onehot = is_target.astype(jnp.float32)
    return ((powers / totals[:, None] - onehot) * loss_weight * slopes).astype(jnp.bfloat16)


def shards(features, fc_weight, class_weight, labels):
    rows_group = features.shape[0]
    class_count = class_weight.shape[0]
    loss_weight = 1.0 / math.sqrt(rows_group * lax.axis_size("dp"))
    position = lax.axis_index("cls")
    rows_block = features
    raw_embed = lax.psum_scatter(
        jnp.dot(rows_block, fc_weight, preferred_element_type=jnp.float32).astype(jnp.bfloat16),
        "cls",
        scatter_dimension=0,
        tiled=True,
    ).astype(jnp.float32)
    embed_norm = jnp.sqrt(jnp.sum(raw_embed * raw_embed, axis=1, keepdims=True) + EPSILON)
    unit_f = raw_embed / embed_norm
    unit_embed = unit_f.astype(jnp.bfloat16)
    class_f = class_weight.astype(jnp.float32)
    class_norm = jnp.sqrt(jnp.sum(class_f * class_f, axis=1, keepdims=True) + EPSILON)
    class_unit_f = class_f / class_norm
    class_unit = class_unit_f.astype(jnp.bfloat16)
    faces_all = lax.all_gather(unit_embed, "cls", axis=0, tiled=True)
    cosine = lax.dot_general(
        faces_all, class_unit, (((1,), (1,)), ((), ())), preferred_element_type=jnp.float32
    )
    columns = position * class_count + lax.broadcasted_iota(jnp.int32, cosine.shape, 1)
    is_target = columns == labels[:, None]
    powers, slopes = margin_terms(cosine, is_target)
    totals = lax.psum(jnp.sum(powers, axis=1), "cls")
    cos_grad = softmax_grad(powers, totals, slopes, is_target, loss_weight)
    rows_block = cos_grad
    unit_grad = lax.psum_scatter(
        jnp.dot(rows_block, class_unit, preferred_element_type=jnp.float32).astype(jnp.bfloat16),
        "cls",
        scatter_dimension=0,
        tiled=True,
    ).astype(jnp.float32)
    class_part = lax.dot_general(
        cos_grad, faces_all, (((0,), (0,)), ((), ())), preferred_element_type=jnp.float32
    )
    raw_grad = (
        (unit_grad - unit_f * jnp.sum(unit_f * unit_grad, axis=1, keepdims=True)) / embed_norm
    ).astype(jnp.bfloat16)
    rows_block = features
    fc_part = lax.dot_general(
        rows_block,
        lax.all_gather(raw_grad, "cls", axis=0, tiled=True),
        (((0,), (0,)), ((), ())),
        preferred_element_type=jnp.float32,
    )
    fc_total, class_total = lax.psum((fc_part, class_part), "dp")
    fc_out = fc_total.astype(jnp.bfloat16)
    class_grad = (
        class_total - class_unit_f * jnp.sum(class_unit_f * class_total, axis=1, keepdims=True)
    ) / class_norm
    return (fc_out, class_grad.astype(jnp.bfloat16))


MESH = pl.DeviceIdType.MESH
LANES = 128
PLANE = 4
ROUNDED = jnp.bfloat16


def split_rows(blocks):
    sizes = [1] + [2] * ((blocks - 1) // 2)
    sizes += [1] * (blocks - sum(sizes))
    return [(sum(sizes[:i]) * LANES, size * LANES) for i, size in enumerate(sizes)]


def kernel(
    nz, chunks, faces_total,
    feat_hbm, w_hbm, cw_hbm, lab_hbm,
    *refs,
):
    count = len(chunks)
    slabs, refs = refs[:count], refs[count:]
    kernel_body(nz, chunks, faces_total, feat_hbm, w_hbm, cw_hbm, lab_hbm, slabs, *refs)


def kernel_body(
    nz, chunks, faces_total,
    feat_hbm, w_hbm, cw_hbm, lab_hbm,
    slabs, cout,
    feat, w, cw_ref, lab_ref, gath, praw, rraw, unit_all, cu, tot_s, tot_r, cosg, cg_all, pgrad, rgrad,
    rg_all, cpart, cslots, f, send1, recv1, send2, recv2,
    load_sem, x_send, x_recv, p_send, p_recv, own_sem, c_send, c_recv,
    ca_send, ca_recv, cp_send, cp_recv, z_send, z_recv, y_send, y_recv, n_send, n_recv,
):
    rows, fin = feat.shape
    classes, dim = cw_ref.shape
    wide = gath.shape[1]
    per = (fin // LANES // PLANE) * LANES
    cq = classes // PLANE
    cz = cq // nz
    dp = lax.axis_index("dp")
    x = lax.axis_index("cls")
    z, q = dp // PLANE, dp % PLANE
    y, core = q // 2, q % 2
    q_y = (1 - y) * 2 + core
    q_c = y * 2 + 1 - core
    q_d = (1 - y) * 2 + 1 - core
    x_dev = {"cls": 1 - x}
    y_dev = {"dp": z * PLANE + q_y}
    c_dev = {"dp": z * PLANE + q_c}
    half, side = z // 2, z % 2
    near = {"dp": (half * 2 + 1 - side) * PLANE + q}
    far = {"dp": ((1 - half) * 2 + side) * PLANE + q}
    owned = side * 2 + half
    plane = [(q + d) % PLANE for d in range(1, PLANE)]
    plane_from = [(q + PLANE - d) % PLANE for d in range(1, PLANE)]
    line = [(z + d) % nz for d in range(1, nz)]
    line_from = [(z + nz - d) % nz for d in range(1, nz)]
    pending = []

    def send(cond, make):
        if cond is None:
            make().start()
        else:
            @pl.when(cond)
            def _():
                make().start()
        pending.append((cond, make))

    def remote(src, dst, s, r, dev):
        return lambda: pltpu.make_async_remote_copy(
            src_ref=src(), dst_ref=dst(), send_sem=s(), recv_sem=r(),
            device_id=dev, device_id_type=MESH,
        )

    def landed(dst, r):
        pltpu.make_async_remote_copy(
            src_ref=dst, dst_ref=dst, send_sem=r, recv_sem=r,
            device_id=x_dev, device_id_type=MESH,
        ).wait_recv()

    def at(i, n):
        return pl.ds(pl.multiple_of(i * n, n), n)

    small = [
        pltpu.make_async_copy(cw_hbm, cw_ref, own_sem.at[1]),
        pltpu.make_async_copy(lab_hbm, lab_ref, own_sem.at[2]),
    ]
    for copy in small:
        copy.start()
    steps = load_sem.shape[0]
    kk = fin // steps
    feat_load = pltpu.make_async_copy(feat_hbm, feat, own_sem.at[3])
    feat_load.start()
    loads = []
    for k in range(steps):
        part = pl.ds(k * kk, kk)
        copy = pltpu.make_async_copy(w_hbm.at[part, :], w.at[part, :], load_sem.at[k])
        copy.start()
        loads.append(copy)

    barrier = pltpu.get_barrier_semaphore()
    peers = [x_dev] + [{"dp": z * PLANE + p} for p in plane] + [{"dp": t * PLANE + q} for t in line]
    for dev in peers:
        pl.semaphore_signal(barrier, inc=1, device_id=dev, device_id_type=MESH)
    pl.semaphore_wait(barrier, len(peers))

    mine = at(q, rows)
    own_feat = pltpu.make_async_copy(
        feat_hbm.at[:, pl.ds(pl.multiple_of(q * per, LANES), wide)], gath.at[mine, :], own_sem.at[0]
    )
    own_feat.start()
    feat_load.wait()
    for i, p in enumerate(plane):
        cols = pl.ds(pl.multiple_of(p * per, LANES), wide)
        send(None, remote(
            lambda cols=cols: feat.at[:, cols], lambda: gath.at[mine, :],
            lambda i=i: p_send.at[0, i], lambda i=i: p_recv.at[0, i], {"dp": z * PLANE + p},
        ))

    total = jnp.zeros((rows, dim), jnp.float32)
    for k in range(steps):
        loads[k].wait()
        part = pl.ds(k * kk, kk)
        total = total + jnp.dot(feat[:, part], w[part, :], preferred_element_type=jnp.float32)
    praw[...] = total.astype(ROUNDED)
    send(None, remote(lambda: praw, lambda: rraw, lambda: x_send.at[0], lambda: x_recv.at[0], x_dev))

    for copy in small:
        copy.wait()
    class_f = cw_ref[...].astype(jnp.float32)
    class_norm = jnp.sqrt(jnp.sum(class_f * class_f, axis=1, keepdims=True) + EPSILON)
    cu[...] = (class_f / class_norm).astype(ROUNDED)

    landed(rraw, x_recv.at[0])
    raw = praw[...].astype(jnp.float32) + rraw[...].astype(jnp.float32)
    norm = jnp.sqrt(jnp.sum(raw * raw, axis=1, keepdims=True) + EPSILON)
    unit_f = raw / norm
    unit = unit_f.astype(ROUNDED)
    unit_all[mine, :] = unit
    for i, dev in enumerate((y_dev, c_dev)):
        send(None, remote(
            lambda: unit_all.at[mine, :], lambda: unit_all.at[mine, :],
            lambda i=i: p_send.at[1, i], lambda i=i: p_recv.at[1, i], dev,
        ))
    cosine = lax.dot_general(
        unit, cu[...], (((1,), (1,)), ((), ())), preferred_element_type=jnp.float32
    )
    columns = x * classes + lax.broadcasted_iota(jnp.int32, cosine.shape, 1)
    label = jnp.broadcast_to(lab_ref[...], (LANES, rows)).T[:, 0:1]
    is_target = columns == label
    powers, slopes = margin_terms(cosine, is_target)
    partial = jnp.sum(powers, axis=1, keepdims=True)
    tot_s[...] = jnp.broadcast_to(partial, (rows, LANES)).T[0:8, :]
    send(None, remote(lambda: tot_s, lambda: tot_r, lambda: x_send.at[1], lambda: x_recv.at[1], x_dev))
    landed(tot_r, x_recv.at[1])
    totals = partial + jnp.broadcast_to(tot_r[0:1, :], (LANES, rows)).T[:, 0:1]
    weight = 1.0 / math.sqrt(faces_total)
    grad = ((powers / totals - is_target.astype(jnp.float32)) * weight * slopes).astype(ROUNDED)
    cosg[...] = grad
    pgrad[...] = jnp.dot(grad, cu[...], preferred_element_type=jnp.float32).astype(ROUNDED)
    send(None, remote(lambda: pgrad, lambda: rgrad, lambda: x_send.at[2], lambda: x_recv.at[2], x_dev))
    for i, p in enumerate(plane):
        cols = at(p, cq)
        send(None, remote(
            lambda cols=cols: cosg.at[:, cols], lambda: cg_all.at[mine, :],
            lambda i=i: p_send.at[2, i], lambda i=i: p_recv.at[2, i], {"dp": z * PLANE + p},
        ))
    cg_all[mine, :] = cosg[:, at(q, cq)]

    landed(rgrad, x_recv.at[2])
    unit_grad = pgrad[...].astype(jnp.float32) + rgrad[...].astype(jnp.float32)
    along = jnp.sum(unit_f * unit_grad, axis=1, keepdims=True)
    rg_all[mine, :] = ((unit_grad - unit_f * along) / norm).astype(ROUNDED)
    for i, p in enumerate(plane):
        send(None, remote(
            lambda: rg_all.at[mine, :], lambda: rg_all.at[mine, :],
            lambda i=i: p_send.at[3, i], lambda i=i: p_recv.at[3, i], {"dp": z * PLANE + p},
        ))

    across = at(q_y, rows)
    landed(unit_all.at[across, :], p_recv.at[1, 0])
    send(None, remote(
        lambda: unit_all.at[across, :], lambda: unit_all.at[across, :],
        lambda: p_send.at[1, 2], lambda: p_recv.at[1, 2], c_dev,
    ))
    for i, p in enumerate(plane_from):
        landed(cg_all.at[at(p, rows), :], p_recv.at[2, i])
    landed(unit_all.at[at(q_c, rows), :], p_recv.at[1, 1])
    landed(unit_all.at[at(q_d, rows), :], p_recv.at[1, 2])
    cpart[...] = lax.dot_general(
        cg_all[...], unit_all[...], (((0,), (0,)), ((), ())), preferred_element_type=jnp.float32
    )
    for i, t in enumerate(line):
        send(None, remote(
            lambda t=t: cpart.at[at(t, cz), :], lambda: cslots.at[z],
            lambda i=i: c_send.at[i], lambda i=i: c_recv.at[i], {"dp": t * PLANE + q},
        ))

    own_feat.wait()
    for i, p in enumerate(plane_from):
        theirs = at(p, rows)
        landed(gath.at[theirs, :], p_recv.at[0, i])
        landed(rg_all.at[theirs, :], p_recv.at[3, i])

    count = len(chunks)

    def has(c, owner):
        return owner == PLANE - 1 if chunks[c][0] >= per else None

    def only(cond, body):
        if cond is None:
            body()
        else:
            pl.when(cond)(body)

    def exchange(cond, src, dst, sends, recvs, dev, *spot):
        send(cond, remote(
            lambda: src(), lambda: dst(), lambda: sends.at[spot], lambda: recvs.at[spot], dev,
        ))

    def pair(c, p, which):
        return slabs[c].at[p, pl.ds(which * 2, 2), :, :]

    def multiply(c, part):
        def body():
            product = lax.dot_general(
                gath[:, part], rg_all[...], (((0,), (0,)), ((), ())), preferred_element_type=jnp.float32
            )
            for j in range(nz):
                f[j, part, :] = product[:, j * LANES:(j + 1) * LANES]
            for i in range(2):
                send1[i, part, :] = f[(1 - side) * 2 + i, part, :].astype(ROUNDED)

        only(has(c, q), body)
        exchange(
            has(c, q), lambda: send1.at[:, part, :], lambda: recv1.at[:, part, :], z_send, z_recv, near, 0, c
        )

    def sum_near(c, part):
        def body():
            landed(recv1.at[:, part, :], z_recv.at[0, c])
            send2[part, :] = (
                f[side * 2 + 1 - half, part, :] + recv1[1 - half, part, :].astype(jnp.float32)
            ).astype(ROUNDED)

        only(has(c, q), body)
        exchange(has(c, q), lambda: send2.at[part, :], lambda: recv2.at[part, :], z_send, z_recv, far, 1, c)

    def sum_far(c, part):
        def body():
            landed(recv2.at[part, :], z_recv.at[1, c])
            slabs[c][q, owned, :, :] = (
                f[owned, part, :]
                + recv1[half, part, :].astype(jnp.float32)
                + recv2[part, :].astype(jnp.float32)
            ).astype(ROUNDED)

        only(has(c, q), body)
        block = lambda: slabs[c].at[q, owned, :, :]
        exchange(has(c, q), block, block, z_send, z_recv, far, 2, c)

    def gather_far(c, part):
        only(has(c, q), lambda: landed(slabs[c].at[q, side * 2 + 1 - half, :, :], z_recv.at[2, c]))
        block = lambda: pair(c, q, side)
        exchange(has(c, q), block, block, z_send, z_recv, near, 3, c)
        exchange(has(c, q), block, block, y_send, y_recv, y_dev, side, c)
        exchange(has(c, q), block, block, n_send, n_recv, c_dev, side, c)

    def gather_near(c, part):
        block = lambda: pair(c, q, 1 - side)
        only(has(c, q), lambda: landed(block(), z_recv.at[3, c]))
        exchange(has(c, q), block, block, y_send, y_recv, y_dev, 1 - side, c)
        exchange(has(c, q), block, block, n_send, n_recv, c_dev, 1 - side, c)

    def gather_across(c, part):
        for which in (side, 1 - side):
            block = lambda which=which: pair(c, q_y, which)
            only(has(c, q_y), lambda: landed(block(), y_recv.at[which, c]))
            exchange(has(c, q_y), block, block, n_send, n_recv, c_dev, 2 + which, c)

    def gather_core(c, part):
        for which in range(2):
            only(has(c, q_c), lambda: landed(pair(c, q_c, which), n_recv.at[which, c]))
            only(has(c, q_d), lambda: landed(pair(c, q_d, which), n_recv.at[2 + which, c]))

    def class_rows():
        for i, t in enumerate(line_from):
            landed(cslots.at[t], c_recv.at[i])
        here = pl.ds(pl.multiple_of(q * cq + z * cz, cz), cz)
        sums = cpart[at(z, cz), :]
        for i, t in enumerate(line_from):
            sums = sums + cslots[t]
        mine_f = cw_ref[here, :].astype(jnp.float32)
        mine_norm = jnp.sqrt(jnp.sum(mine_f * mine_f, axis=1, keepdims=True) + EPSILON)
        mine_unit = mine_f / mine_norm
        along = jnp.sum(mine_unit * sums, axis=1, keepdims=True)
        cout[here, :] = ((sums - mine_unit * along) / mine_norm).astype(ROUNDED)
        for i, t in enumerate(line):
            send(None, remote(
                lambda: cout.at[here, :], lambda: cout.at[here, :],
                lambda i=i: ca_send.at[i], lambda i=i: ca_recv.at[i], {"dp": t * PLANE + q},
            ))

    def class_plane():
        for i, t in enumerate(line_from):
            there = pl.ds(pl.multiple_of(q * cq + t * cz, cz), cz)
            landed(cout.at[there, :], ca_recv.at[i])
        block = lambda: cout.at[at(q, cq), :]
        send(None, remote(block, block, lambda: cp_send.at[0], lambda: cp_recv.at[0], y_dev))
        send(None, remote(block, block, lambda: cp_send.at[1], lambda: cp_recv.at[1], c_dev))

    def class_across():
        landed(cout.at[at(q_y, cq), :], cp_recv.at[0])
        block = lambda: cout.at[at(q_y, cq), :]
        send(None, remote(block, block, lambda: cp_send.at[2], lambda: cp_recv.at[2], c_dev))

    stages = (
        (0, multiply), (1, sum_near), (2, sum_far), (3, gather_far), (4, gather_near),
        (6, gather_across), (8, gather_core),
    )
    for tick in range(count + stages[-1][0]):
        for late, run in stages:
            c = tick - late
            if 0 <= c < count:
                run(c, pl.ds(*chunks[c]))
        if tick == 1:
            class_rows()
        if tick == 2:
            class_plane()
        if tick == 3:
            class_across()

    landed(cout.at[at(q_c, cq), :], cp_recv.at[1])
    landed(cout.at[at(q_d, cq), :], cp_recv.at[2])
    for cond, make in pending:
        only(cond, lambda: make().wait_send())


def place(chunks, per, *refs):
    count = len(chunks)
    slabs, cout = refs[:count], refs[count]
    fc_out, class_out, rows_of, sems = refs[count + 1:]
    copies = [pltpu.make_async_copy(cout, class_out, sems.at[0])]
    copies[0].start()
    for p in range(PLANE):
        for c, (first, size) in enumerate(chunks):
            if p == PLANE - 1 or first < per:
                start = p * per + first
                for j in range(slabs[c].shape[1]):
                    rows_of[pl.ds(start, size), pl.ds(j * LANES, LANES)] = slabs[c][p, j, pl.ds(0, size), :]
                copies.append(pltpu.make_async_copy(
                    rows_of.at[pl.ds(start, size), :], fc_out.at[pl.ds(start, size), :], sems.at[len(copies)],
                ))
                copies[-1].start()
    for copy in copies:
        copy.wait()


def fused(n_dp, features, fc_weight, class_weight, labels):
    rows, fin = features.shape
    classes, dim = class_weight.shape
    nz = n_dp // PLANE
    blocks = fin // LANES
    wide = (blocks - (PLANE - 1) * (blocks // PLANE)) * LANES
    per = blocks // PLANE
    chunks = split_rows(per)
    if wide // LANES > per:
        chunks.append((per * LANES, wide - per * LANES))
    count = len(chunks)
    steps = max(d for d in range(1, 9) if blocks % d == 0)
    bf, f32, dma = jnp.bfloat16, jnp.float32, pltpu.SemaphoreType.DMA
    vmem, whole = pltpu.VMEM, pl.BlockSpec(memory_space=pltpu.VMEM)
    anywhere = pl.BlockSpec(memory_space=pl.ANY)
    results = pl.pallas_call(
        functools.partial(kernel, nz, chunks, rows * n_dp),
        out_shape=(
            *[jax.ShapeDtypeStruct((PLANE, nz, size, LANES), bf) for _, size in chunks],
            jax.ShapeDtypeStruct((classes, dim), bf),
        ),
        in_specs=[anywhere] * 4,
        out_specs=(whole,) * (count + 1),
        scratch_shapes=[
            vmem((rows, fin), bf), vmem((fin, dim), bf), vmem((classes, dim), bf),
            vmem((1, rows), jnp.int32), vmem((PLANE * rows, wide), bf),
            vmem((rows, dim), bf), vmem((rows, dim), bf), vmem((PLANE * rows, dim), bf),
            vmem((classes, dim), bf), vmem((8, rows), f32), vmem((8, rows), f32),
            vmem((rows, classes), bf), vmem((PLANE * rows, classes // PLANE), bf),
            vmem((rows, dim), bf), vmem((rows, dim), bf), vmem((PLANE * rows, dim), bf),
            vmem((classes // PLANE, dim), f32), vmem((nz, classes // PLANE // nz, dim), f32),
            vmem((nz, wide, LANES), f32), vmem((2, wide, LANES), bf), vmem((2, wide, LANES), bf),
            vmem((wide, LANES), bf), vmem((wide, LANES), bf),
            dma((steps,)), dma((3,)), dma((3,)), dma((4, PLANE - 1)), dma((4, PLANE - 1)),
            dma((4,)), dma((nz - 1,)), dma((nz - 1,)), dma((nz - 1,)), dma((nz - 1,)),
            dma((3,)), dma((3,)), dma((4, count)), dma((4, count)),
            dma((2, count)), dma((2, count)), dma((4, count)), dma((4, count)),
        ],
        compiler_params=pltpu.CompilerParams(
            collective_id=0, has_side_effects=True, vmem_limit_bytes=46 * 2**20
        ),
    )(features, fc_weight, class_weight, labels.reshape(1, rows))
    return pl.pallas_call(
        functools.partial(place, chunks, blocks // PLANE * LANES),
        out_shape=(
            jax.ShapeDtypeStruct((fin, dim), bf),
            jax.ShapeDtypeStruct((classes, dim), bf),
        ),
        in_specs=[whole] * (count + 1),
        out_specs=(anywhere, anywhere),
        scratch_shapes=[vmem((fin, dim), bf), dma((PLANE * count + 1,))],
        compiler_params=pltpu.CompilerParams(vmem_limit_bytes=16 * 2**20),
    )(*results)


def choose(n_dp, n_cls, features, fc_weight, class_weight, labels):
    rows, fin = features.shape
    classes, dim = class_weight.shape
    nz = n_dp // PLANE
    fits = (
        n_cls == 2
        and n_dp % PLANE == 0
        and nz == 4
        and dim == nz * LANES
        and fin % LANES == 0
        and fin // LANES >= PLANE
        and rows == LANES
        and classes % (PLANE * LANES) == 0
        and classes // PLANE % (16 * nz) == 0
        and classes <= 512
        and fin <= 6272
    )
    if fits:
        return fused(n_dp, features, fc_weight, class_weight, labels)
    return shards(features, fc_weight, class_weight, labels)


def solution(mesh):
    placed = (P("dp", "cls"), P("cls", None), P("cls", None), P("dp"))
    return jax.shard_map(
        functools.partial(choose, mesh.shape["dp"], mesh.shape["cls"]),
        mesh=mesh,
        in_specs=placed,
        out_specs=(P("cls", None), P("cls", None)),
        check_vma=False,
    )
```

```python
import functools
import math

import jax
import jax.numpy as jnp
from jax import lax
from jax.experimental import pallas as pl
from jax.experimental.pallas import tpu as pltpu
from jax.sharding import PartitionSpec as P

SCALE = 64.0
MARGIN = 0.5
SOFTEN = 0.01
EPSILON = 1e-06


def margin_terms(cosine, is_target):
    sine = jnp.sqrt(1.0 + SOFTEN - cosine * cosine)
    shifted = cosine * math.cos(MARGIN) - sine * math.sin(MARGIN)
    powers = jnp.exp(SCALE * jnp.where(is_target, shifted, cosine))
    slopes = SCALE * jnp.where(is_target, math.cos(MARGIN) + math.sin(MARGIN) * cosine / sine, 1.0)
    return (powers, slopes)


def softmax_grad(powers, totals, slopes, is_target, loss_weight):
    onehot = is_target.astype(jnp.float32)
    return ((powers / totals[:, None] - onehot) * loss_weight * slopes).astype(jnp.bfloat16)


def shards(features, fc_weight, class_weight, labels):
    rows_group = features.shape[0]
    class_count = class_weight.shape[0]
    loss_weight = 1.0 / math.sqrt(rows_group * lax.axis_size("dp"))
    position = lax.axis_index("cls")
    rows_block = features
    raw_embed = lax.psum_scatter(
        jnp.dot(rows_block, fc_weight, preferred_element_type=jnp.float32).astype(jnp.bfloat16),
        "cls",
        scatter_dimension=0,
        tiled=True,
    ).astype(jnp.float32)
    embed_norm = jnp.sqrt(jnp.sum(raw_embed * raw_embed, axis=1, keepdims=True) + EPSILON)
    unit_f = raw_embed / embed_norm
    unit_embed = unit_f.astype(jnp.bfloat16)
    class_f = class_weight.astype(jnp.float32)
    class_norm = jnp.sqrt(jnp.sum(class_f * class_f, axis=1, keepdims=True) + EPSILON)
    class_unit_f = class_f / class_norm
    class_unit = class_unit_f.astype(jnp.bfloat16)
    faces_all = lax.all_gather(unit_embed, "cls", axis=0, tiled=True)
    cosine = lax.dot_general(
        faces_all, class_unit, (((1,), (1,)), ((), ())), preferred_element_type=jnp.float32
    )
    columns = position * class_count + lax.broadcasted_iota(jnp.int32, cosine.shape, 1)
    is_target = columns == labels[:, None]
    powers, slopes = margin_terms(cosine, is_target)
    totals = lax.psum(jnp.sum(powers, axis=1), "cls")
    cos_grad = softmax_grad(powers, totals, slopes, is_target, loss_weight)
    rows_block = cos_grad
    unit_grad = lax.psum_scatter(
        jnp.dot(rows_block, class_unit, preferred_element_type=jnp.float32).astype(jnp.bfloat16),
        "cls",
        scatter_dimension=0,
        tiled=True,
    ).astype(jnp.float32)
    class_part = lax.dot_general(
        cos_grad, faces_all, (((0,), (0,)), ((), ())), preferred_element_type=jnp.float32
    )
    raw_grad = (
        (unit_grad - unit_f * jnp.sum(unit_f * unit_grad, axis=1, keepdims=True)) / embed_norm
    ).astype(jnp.bfloat16)
    rows_block = features
    fc_part = lax.dot_general(
        rows_block,
        lax.all_gather(raw_grad, "cls", axis=0, tiled=True),
        (((0,), (0,)), ((), ())),
        preferred_element_type=jnp.float32,
    )
    fc_total, class_total = lax.psum((fc_part, class_part), "dp")
    fc_out = fc_total.astype(jnp.bfloat16)
    class_grad = (
        class_total - class_unit_f * jnp.sum(class_unit_f * class_total, axis=1, keepdims=True)
    ) / class_norm
    return (fc_out, class_grad.astype(jnp.bfloat16))


MESH = pl.DeviceIdType.MESH
LANES = 128
PLANE = 4
ROUNDED = jnp.bfloat16


def split_rows(blocks):
    sizes = [1] + [2] * ((blocks - 1) // 2)
    sizes += [1] * (blocks - sum(sizes))
    return [(sum(sizes[:i]) * LANES, size * LANES) for i, size in enumerate(sizes)]


def kernel(
    nz, chunks, faces_total,
    feat_hbm, w_hbm, cw_hbm, lab_hbm,
    *refs,
):
    count = len(chunks)
    slabs, refs = refs[:count], refs[count:]
    kernel_body(nz, chunks, faces_total, feat_hbm, w_hbm, cw_hbm, lab_hbm, slabs, *refs)


def kernel_body(
    nz, chunks, faces_total,
    feat_hbm, w_hbm, cw_hbm, lab_hbm,
    slabs, cout,
    feat, w, cw_ref, lab_ref, gath, praw, rraw, unit_all, cu, tot_s, tot_r, cosg, cg_all, pgrad, rgrad,
    rg_all, cpart, cslots, f, send1, recv1, send2, recv2,
    load_sem, x_send, x_recv, p_send, p_recv, own_sem, c_send, c_recv,
    ca_send, ca_recv, cp_send, cp_recv, z_send, z_recv, y_send, y_recv, n_send, n_recv,
):
    rows, fin = feat.shape
    classes, dim = cw_ref.shape
    wide = gath.shape[1]
    per = (fin // LANES // PLANE) * LANES
    cq = classes // PLANE
    cz = cq // nz
    dp = lax.axis_index("dp")
    x = lax.axis_index("cls")
    z, q = dp // PLANE, dp % PLANE
    y, core = q // 2, q % 2
    q_y = (1 - y) * 2 + core
    q_c = y * 2 + 1 - core
    q_d = (1 - y) * 2 + 1 - core
    x_dev = {"cls": 1 - x}
    y_dev = {"dp": z * PLANE + q_y}
    c_dev = {"dp": z * PLANE + q_c}
    half, side = z // 2, z % 2
    near = {"dp": (half * 2 + 1 - side) * PLANE + q}
    far = {"dp": ((1 - half) * 2 + side) * PLANE + q}
    owned = side * 2 + half
    beside = side * 2 + 1 - half
    plane = [(q + d) % PLANE for d in range(1, PLANE)]
    plane_from = [(q + PLANE - d) % PLANE for d in range(1, PLANE)]
    line = [(z + d) % nz for d in range(1, nz)]
    line_from = [(z + nz - d) % nz for d in range(1, nz)]
    pending = []

    def send(cond, make):
        if cond is None:
            make().start()
        else:
            @pl.when(cond)
            def _():
                make().start()
        pending.append((cond, make))

    def remote(src, dst, s, r, dev):
        return lambda: pltpu.make_async_remote_copy(
            src_ref=src(), dst_ref=dst(), send_sem=s(), recv_sem=r(),
            device_id=dev, device_id_type=MESH,
        )

    def landed(dst, r):
        pltpu.make_async_remote_copy(
            src_ref=dst, dst_ref=dst, send_sem=r, recv_sem=r,
            device_id=x_dev, device_id_type=MESH,
        ).wait_recv()

    def at(i, n):
        return pl.ds(pl.multiple_of(i * n, n), n)

    small = [
        pltpu.make_async_copy(cw_hbm, cw_ref, own_sem.at[1]),
        pltpu.make_async_copy(lab_hbm, lab_ref, own_sem.at[2]),
    ]
    for copy in small:
        copy.start()
    steps = load_sem.shape[0]
    kk = fin // steps
    feat_load = pltpu.make_async_copy(feat_hbm, feat, own_sem.at[3])
    feat_load.start()
    loads = []
    for k in range(steps):
        part = pl.ds(k * kk, kk)
        copy = pltpu.make_async_copy(w_hbm.at[part, :], w.at[part, :], load_sem.at[k])
        copy.start()
        loads.append(copy)

    barrier = pltpu.get_barrier_semaphore()
    peers = [x_dev] + [{"dp": z * PLANE + p} for p in plane] + [{"dp": t * PLANE + q} for t in line]
    for dev in peers:
        pl.semaphore_signal(barrier, inc=1, device_id=dev, device_id_type=MESH)
    pl.semaphore_wait(barrier, len(peers))

    mine = at(q, rows)
    own_feat = pltpu.make_async_copy(
        feat_hbm.at[:, pl.ds(pl.multiple_of(q * per, LANES), wide)], gath.at[mine, :], own_sem.at[0]
    )
    own_feat.start()
    feat_load.wait()
    for i, p in enumerate(plane):
        cols = pl.ds(pl.multiple_of(p * per, LANES), wide)
        send(None, remote(
            lambda cols=cols: feat.at[:, cols], lambda: gath.at[mine, :],
            lambda i=i: p_send.at[0, i], lambda i=i: p_recv.at[0, i], {"dp": z * PLANE + p},
        ))

    for h in range(2):
        columns = pl.ds(h * (dim // 2), dim // 2)
        total = jnp.zeros((rows, dim // 2), jnp.float32)
        for k in range(steps):
            if h == 0:
                loads[k].wait()
            part = pl.ds(k * kk, kk)
            total = total + jnp.dot(
                feat[:, part], w[part, columns], preferred_element_type=jnp.float32
            )
        praw[:, columns] = total.astype(ROUNDED)
        send(None, remote(
            lambda columns=columns: praw.at[:, columns], lambda columns=columns: rraw.at[:, columns],
            lambda h=h: x_send.at[3 * h], lambda h=h: x_recv.at[3 * h], x_dev,
        ))

    for copy in small:
        copy.wait()
    class_f = cw_ref[...].astype(jnp.float32)
    class_norm = jnp.sqrt(jnp.sum(class_f * class_f, axis=1, keepdims=True) + EPSILON)
    cu[...] = (class_f / class_norm).astype(ROUNDED)

    landed(rraw.at[:, pl.ds(0, dim // 2)], x_recv.at[0])
    landed(rraw.at[:, pl.ds(dim // 2, dim // 2)], x_recv.at[3])
    raw = praw[...].astype(jnp.float32) + rraw[...].astype(jnp.float32)
    norm = jnp.sqrt(jnp.sum(raw * raw, axis=1, keepdims=True) + EPSILON)
    unit_f = raw / norm
    unit = unit_f.astype(ROUNDED)
    unit_all[mine, :] = unit
    for i, dev in enumerate((y_dev, c_dev)):
        send(None, remote(
            lambda: unit_all.at[mine, :], lambda: unit_all.at[mine, :],
            lambda i=i: p_send.at[1, i], lambda i=i: p_recv.at[1, i], dev,
        ))
    cosine = lax.dot_general(
        unit, cu[...], (((1,), (1,)), ((), ())), preferred_element_type=jnp.float32
    )
    columns = x * classes + lax.broadcasted_iota(jnp.int32, cosine.shape, 1)
    label = jnp.broadcast_to(lab_ref[...], (LANES, rows)).T[:, 0:1]
    is_target = columns == label
    powers, slopes = margin_terms(cosine, is_target)
    partial = jnp.sum(powers, axis=1, keepdims=True)
    tot_s[...] = jnp.broadcast_to(partial, (rows, LANES)).T[0:8, :]
    send(None, remote(lambda: tot_s, lambda: tot_r, lambda: x_send.at[1], lambda: x_recv.at[1], x_dev))
    landed(tot_r, x_recv.at[1])
    totals = partial + jnp.broadcast_to(tot_r[0:1, :], (LANES, rows)).T[:, 0:1]
    weight = 1.0 / math.sqrt(faces_total)
    grad = ((powers / totals - is_target.astype(jnp.float32)) * weight * slopes).astype(ROUNDED)
    cosg[...] = grad
    pgrad[...] = jnp.dot(grad, cu[...], preferred_element_type=jnp.float32).astype(ROUNDED)
    send(None, remote(lambda: pgrad, lambda: rgrad, lambda: x_send.at[2], lambda: x_recv.at[2], x_dev))
    for i, p in enumerate(plane):
        cols = at(p, cq)
        send(None, remote(
            lambda cols=cols: cosg.at[:, cols], lambda: cg_all.at[mine, :],
            lambda i=i: p_send.at[2, i], lambda i=i: p_recv.at[2, i], {"dp": z * PLANE + p},
        ))
    cg_all[mine, :] = cosg[:, at(q, cq)]

    landed(rgrad, x_recv.at[2])
    unit_grad = pgrad[...].astype(jnp.float32) + rgrad[...].astype(jnp.float32)
    along = jnp.sum(unit_f * unit_grad, axis=1, keepdims=True)
    rg_all[mine, :] = ((unit_grad - unit_f * along) / norm).astype(ROUNDED)
    for i, p in enumerate(plane):
        send(None, remote(
            lambda: rg_all.at[mine, :], lambda: rg_all.at[mine, :],
            lambda i=i: p_send.at[3, i], lambda i=i: p_recv.at[3, i], {"dp": z * PLANE + p},
        ))

    across = at(q_y, rows)
    landed(unit_all.at[across, :], p_recv.at[1, 0])
    send(None, remote(
        lambda: unit_all.at[across, :], lambda: unit_all.at[across, :],
        lambda: p_send.at[1, 2], lambda: p_recv.at[1, 2], c_dev,
    ))
    for i, p in enumerate(plane_from):
        landed(cg_all.at[at(p, rows), :], p_recv.at[2, i])
    landed(unit_all.at[at(q_c, rows), :], p_recv.at[1, 1])
    landed(unit_all.at[at(q_d, rows), :], p_recv.at[1, 2])
    cpart[...] = lax.dot_general(
        cg_all[...], unit_all[...], (((0,), (0,)), ((), ())), preferred_element_type=jnp.float32
    )
    for i, t in enumerate(line):
        send(None, remote(
            lambda t=t: cpart.at[at(t, cz), :], lambda: cslots.at[z],
            lambda i=i: c_send.at[i], lambda i=i: c_recv.at[i], {"dp": t * PLANE + q},
        ))

    own_feat.wait()
    for i, p in enumerate(plane_from):
        theirs = at(p, rows)
        landed(gath.at[theirs, :], p_recv.at[0, i])
        landed(rg_all.at[theirs, :], p_recv.at[3, i])

    count = len(chunks)

    def has(c, owner):
        return owner == PLANE - 1 if chunks[c][0] >= per else None

    def only(cond, body):
        if cond is None:
            body()
        else:
            pl.when(cond)(body)

    def exchange(cond, src, dst, sends, recvs, dev, *spot):
        send(cond, remote(
            lambda: src(), lambda: dst(), lambda: sends.at[spot], lambda: recvs.at[spot], dev,
        ))

    def pair(c, p, which):
        return slabs[c].at[p, pl.ds(which * 2, 2), :, :]

    def multiply(c, part):
        def body():
            product = lax.dot_general(
                gath[:, part], rg_all[...], (((0,), (0,)), ((), ())), preferred_element_type=jnp.float32
            )
            for j in range(nz):
                f[j, part, :] = product[:, j * LANES:(j + 1) * LANES]
            for i in range(2):
                send1[i, part, :] = f[(1 - side) * 2 + i, part, :].astype(ROUNDED)

        only(has(c, q), body)
        exchange(
            has(c, q), lambda: send1.at[:, part, :], lambda: recv1.at[:, part, :], z_send, z_recv, near, 0, c
        )

    def sum_near(c, part):
        def body():
            landed(recv1.at[:, part, :], z_recv.at[0, c])
            send2[part, :] = (
                f[side * 2 + 1 - half, part, :] + recv1[1 - half, part, :].astype(jnp.float32)
            ).astype(ROUNDED)

        only(has(c, q), body)
        exchange(has(c, q), lambda: send2.at[part, :], lambda: recv2.at[part, :], z_send, z_recv, far, 1, c)

    def sum_far(c, part):
        def body():
            landed(recv2.at[part, :], z_recv.at[1, c])
            slabs[c][q, owned, :, :] = (
                f[owned, part, :]
                + recv1[half, part, :].astype(jnp.float32)
                + recv2[part, :].astype(jnp.float32)
            ).astype(ROUNDED)

        only(has(c, q), body)
        block = lambda: slabs[c].at[q, owned, :, :]
        exchange(has(c, q), block, block, z_send, z_recv, far, 2, c)
        exchange(has(c, q), block, block, y_send, y_recv, y_dev, 0, c)
        exchange(has(c, q), block, block, n_send, n_recv, c_dev, 0, c)

    def gather_far(c, part):
        other = lambda: slabs[c].at[q, beside, :, :]
        only(has(c, q), lambda: landed(other(), z_recv.at[2, c]))
        block = lambda: pair(c, q, side)
        exchange(has(c, q), block, block, z_send, z_recv, near, 3, c)
        exchange(has(c, q), other, other, y_send, y_recv, y_dev, 1, c)
        exchange(has(c, q), other, other, n_send, n_recv, c_dev, 1, c)

    def gather_near(c, part):
        block = lambda: pair(c, q, 1 - side)
        only(has(c, q), lambda: landed(block(), z_recv.at[3, c]))
        exchange(has(c, q), block, block, y_send, y_recv, y_dev, 2, c)
        exchange(has(c, q), block, block, n_send, n_recv, c_dev, 2, c)

    def arrived(c, p, recvs, first):
        landed(slabs[c].at[p, owned, :, :], recvs.at[first, c])
        landed(slabs[c].at[p, beside, :, :], recvs.at[first + 1, c])

    def gather_across(c, part):
        for i, which in enumerate((side, 1 - side)):
            block = lambda which=which: pair(c, q_y, which)
            if i == 0:
                only(has(c, q_y), lambda: arrived(c, q_y, y_recv, 0))
            else:
                only(has(c, q_y), lambda: landed(block(), y_recv.at[2, c]))
            exchange(has(c, q_y), block, block, n_send, n_recv, c_dev, 3 + i, c)

    def gather_core(c, part):
        def own():
            arrived(c, q_c, n_recv, 0)
            landed(pair(c, q_c, 1 - side), n_recv.at[2, c])

        def crossed():
            landed(pair(c, q_d, side), n_recv.at[3, c])
            landed(pair(c, q_d, 1 - side), n_recv.at[4, c])

        only(has(c, q_c), own)
        only(has(c, q_d), crossed)

    def class_rows():
        for i, t in enumerate(line_from):
            landed(cslots.at[t], c_recv.at[i])
        here = pl.ds(pl.multiple_of(q * cq + z * cz, cz), cz)
        sums = cpart[at(z, cz), :]
        for i, t in enumerate(line_from):
            sums = sums + cslots[t]
        mine_f = cw_ref[here, :].astype(jnp.float32)
        mine_norm = jnp.sqrt(jnp.sum(mine_f * mine_f, axis=1, keepdims=True) + EPSILON)
        mine_unit = mine_f / mine_norm
        along = jnp.sum(mine_unit * sums, axis=1, keepdims=True)
        cout[here, :] = ((sums - mine_unit * along) / mine_norm).astype(ROUNDED)
        for i, t in enumerate(line):
            send(None, remote(
                lambda: cout.at[here, :], lambda: cout.at[here, :],
                lambda i=i: ca_send.at[i], lambda i=i: ca_recv.at[i], {"dp": t * PLANE + q},
            ))

    def class_plane():
        for i, t in enumerate(line_from):
            there = pl.ds(pl.multiple_of(q * cq + t * cz, cz), cz)
            landed(cout.at[there, :], ca_recv.at[i])
        block = lambda: cout.at[at(q, cq), :]
        send(None, remote(block, block, lambda: cp_send.at[0], lambda: cp_recv.at[0], y_dev))
        send(None, remote(block, block, lambda: cp_send.at[1], lambda: cp_recv.at[1], c_dev))

    def class_across():
        landed(cout.at[at(q_y, cq), :], cp_recv.at[0])
        block = lambda: cout.at[at(q_y, cq), :]
        send(None, remote(block, block, lambda: cp_send.at[2], lambda: cp_recv.at[2], c_dev))

    stages = (
        (0, multiply), (1, sum_near), (2, sum_far), (3, gather_far), (4, gather_near),
        (7, gather_across), (9, gather_core),
    )
    for tick in range(count + stages[-1][0]):
        for late, run in stages:
            c = tick - late
            if 0 <= c < count:
                run(c, pl.ds(*chunks[c]))
        if tick == 3:
            class_rows()
        if tick == 6:
            class_plane()
        if tick == 9:
            class_across()

    landed(cout.at[at(q_c, cq), :], cp_recv.at[1])
    landed(cout.at[at(q_d, cq), :], cp_recv.at[2])
    for cond, make in pending:
        only(cond, lambda: make().wait_send())


def place(chunks, per, *refs):
    count = len(chunks)
    slabs, cout = refs[:count], refs[count]
    fc_out, class_out, rows_of, sems = refs[count + 1:]
    copies = [pltpu.make_async_copy(cout, class_out, sems.at[0])]
    copies[0].start()
    for p in range(PLANE):
        for c, (first, size) in enumerate(chunks):
            if p == PLANE - 1 or first < per:
                start = p * per + first
                for j in range(slabs[c].shape[1]):
                    rows_of[pl.ds(start, size), pl.ds(j * LANES, LANES)] = slabs[c][p, j, pl.ds(0, size), :]
                copies.append(pltpu.make_async_copy(
                    rows_of.at[pl.ds(start, size), :], fc_out.at[pl.ds(start, size), :], sems.at[len(copies)],
                ))
                copies[-1].start()
    for copy in copies:
        copy.wait()


def fused(n_dp, features, fc_weight, class_weight, labels):
    rows, fin = features.shape
    classes, dim = class_weight.shape
    nz = n_dp // PLANE
    blocks = fin // LANES
    wide = (blocks - (PLANE - 1) * (blocks // PLANE)) * LANES
    per = blocks // PLANE
    chunks = split_rows(per)
    if wide // LANES > per:
        chunks.append((per * LANES, wide - per * LANES))
    count = len(chunks)
    steps = max(d for d in range(1, 9) if blocks % d == 0)
    bf, f32, dma = jnp.bfloat16, jnp.float32, pltpu.SemaphoreType.DMA
    vmem, whole = pltpu.VMEM, pl.BlockSpec(memory_space=pltpu.VMEM)
    anywhere = pl.BlockSpec(memory_space=pl.ANY)
    results = pl.pallas_call(
        functools.partial(kernel, nz, chunks, rows * n_dp),
        out_shape=(
            *[jax.ShapeDtypeStruct((PLANE, nz, size, LANES), bf) for _, size in chunks],
            jax.ShapeDtypeStruct((classes, dim), bf),
        ),
        in_specs=[anywhere] * 4,
        out_specs=(whole,) * (count + 1),
        scratch_shapes=[
            vmem((rows, fin), bf), vmem((fin, dim), bf), vmem((classes, dim), bf),
            vmem((1, rows), jnp.int32), vmem((PLANE * rows, wide), bf),
            vmem((rows, dim), bf), vmem((rows, dim), bf), vmem((PLANE * rows, dim), bf),
            vmem((classes, dim), bf), vmem((8, rows), f32), vmem((8, rows), f32),
            vmem((rows, classes), bf), vmem((PLANE * rows, classes // PLANE), bf),
            vmem((rows, dim), bf), vmem((rows, dim), bf), vmem((PLANE * rows, dim), bf),
            vmem((classes // PLANE, dim), f32), vmem((nz, classes // PLANE // nz, dim), f32),
            vmem((nz, wide, LANES), f32), vmem((2, wide, LANES), bf), vmem((2, wide, LANES), bf),
            vmem((wide, LANES), bf), vmem((wide, LANES), bf),
            dma((steps,)), dma((4,)), dma((4,)), dma((4, PLANE - 1)), dma((4, PLANE - 1)),
            dma((4,)), dma((nz - 1,)), dma((nz - 1,)), dma((nz - 1,)), dma((nz - 1,)),
            dma((3,)), dma((3,)), dma((4, count)), dma((4, count)),
            dma((3, count)), dma((3, count)), dma((5, count)), dma((5, count)),
        ],
        compiler_params=pltpu.CompilerParams(
            collective_id=0, has_side_effects=True, vmem_limit_bytes=46 * 2**20
        ),
    )(features, fc_weight, class_weight, labels.reshape(1, rows))
    return pl.pallas_call(
        functools.partial(place, chunks, blocks // PLANE * LANES),
        out_shape=(
            jax.ShapeDtypeStruct((fin, dim), bf),
            jax.ShapeDtypeStruct((classes, dim), bf),
        ),
        in_specs=[whole] * (count + 1),
        out_specs=(anywhere, anywhere),
        scratch_shapes=[vmem((fin, dim), bf), dma((PLANE * count + 1,))],
        compiler_params=pltpu.CompilerParams(vmem_limit_bytes=16 * 2**20),
    )(*results)


def choose(n_dp, n_cls, features, fc_weight, class_weight, labels):
    rows, fin = features.shape
    classes, dim = class_weight.shape
    nz = n_dp // PLANE
    fits = (
        n_cls == 2
        and n_dp % PLANE == 0
        and nz == 4
        and dim == nz * LANES
        and fin % LANES == 0
        and fin // LANES >= PLANE
        and rows == LANES
        and classes % (PLANE * LANES) == 0
        and classes // PLANE % (16 * nz) == 0
        and classes <= 512
        and fin <= 6272
    )
    if fits:
        return fused(n_dp, features, fc_weight, class_weight, labels)
    return shards(features, fc_weight, class_weight, labels)


def solution(mesh):
    placed = (P("dp", "cls"), P("cls", None), P("cls", None), P("dp"))
    return jax.shard_map(
        functools.partial(choose, mesh.shape["dp"], mesh.shape["cls"]),
        mesh=mesh,
        in_specs=placed,
        out_specs=(P("cls", None), P("cls", None)),
        check_vma=False,
    )
```

```python
import functools
import math

import jax
import jax.numpy as jnp
from jax import lax
from jax.experimental import pallas as pl
from jax.experimental.pallas import tpu as pltpu
from jax.sharding import PartitionSpec as P

SCALE = 64.0
MARGIN = 0.5
SOFTEN = 0.01
EPSILON = 1e-06


def margin_terms(cosine, is_target):
    sine = jnp.sqrt(1.0 + SOFTEN - cosine * cosine)
    shifted = cosine * math.cos(MARGIN) - sine * math.sin(MARGIN)
    powers = jnp.exp(SCALE * jnp.where(is_target, shifted, cosine))
    slopes = SCALE * jnp.where(is_target, math.cos(MARGIN) + math.sin(MARGIN) * cosine / sine, 1.0)
    return (powers, slopes)


def softmax_grad(powers, totals, slopes, is_target, loss_weight):
    onehot = is_target.astype(jnp.float32)
    return ((powers / totals[:, None] - onehot) * loss_weight * slopes).astype(jnp.bfloat16)


def shards(features, fc_weight, class_weight, labels):
    rows_group = features.shape[0]
    class_count = class_weight.shape[0]
    loss_weight = 1.0 / math.sqrt(rows_group * lax.axis_size("dp"))
    position = lax.axis_index("cls")
    rows_block = features
    raw_embed = lax.psum_scatter(
        jnp.dot(rows_block, fc_weight, preferred_element_type=jnp.float32).astype(jnp.bfloat16),
        "cls",
        scatter_dimension=0,
        tiled=True,
    ).astype(jnp.float32)
    embed_norm = jnp.sqrt(jnp.sum(raw_embed * raw_embed, axis=1, keepdims=True) + EPSILON)
    unit_f = raw_embed / embed_norm
    unit_embed = unit_f.astype(jnp.bfloat16)
    class_f = class_weight.astype(jnp.float32)
    class_norm = jnp.sqrt(jnp.sum(class_f * class_f, axis=1, keepdims=True) + EPSILON)
    class_unit_f = class_f / class_norm
    class_unit = class_unit_f.astype(jnp.bfloat16)
    faces_all = lax.all_gather(unit_embed, "cls", axis=0, tiled=True)
    cosine = lax.dot_general(
        faces_all, class_unit, (((1,), (1,)), ((), ())), preferred_element_type=jnp.float32
    )
    columns = position * class_count + lax.broadcasted_iota(jnp.int32, cosine.shape, 1)
    is_target = columns == labels[:, None]
    powers, slopes = margin_terms(cosine, is_target)
    totals = lax.psum(jnp.sum(powers, axis=1), "cls")
    cos_grad = softmax_grad(powers, totals, slopes, is_target, loss_weight)
    rows_block = cos_grad
    unit_grad = lax.psum_scatter(
        jnp.dot(rows_block, class_unit, preferred_element_type=jnp.float32).astype(jnp.bfloat16),
        "cls",
        scatter_dimension=0,
        tiled=True,
    ).astype(jnp.float32)
    class_part = lax.dot_general(
        cos_grad, faces_all, (((0,), (0,)), ((), ())), preferred_element_type=jnp.float32
    )
    raw_grad = (
        (unit_grad - unit_f * jnp.sum(unit_f * unit_grad, axis=1, keepdims=True)) / embed_norm
    ).astype(jnp.bfloat16)
    rows_block = features
    fc_part = lax.dot_general(
        rows_block,
        lax.all_gather(raw_grad, "cls", axis=0, tiled=True),
        (((0,), (0,)), ((), ())),
        preferred_element_type=jnp.float32,
    )
    fc_total, class_total = lax.psum((fc_part, class_part), "dp")
    fc_out = fc_total.astype(jnp.bfloat16)
    class_grad = (
        class_total - class_unit_f * jnp.sum(class_unit_f * class_total, axis=1, keepdims=True)
    ) / class_norm
    return (fc_out, class_grad.astype(jnp.bfloat16))


MESH = pl.DeviceIdType.MESH
LANES = 128
PLANE = 4
ROUNDED = jnp.bfloat16


def split_rows(blocks):
    sizes = [1] + [2] * ((blocks - 1) // 2)
    sizes += [1] * (blocks - sum(sizes))
    return [(sum(sizes[:i]) * LANES, size * LANES) for i, size in enumerate(sizes)]


def kernel(
    nz, chunks, faces_total,
    feat_hbm, w_hbm, cw_hbm, lab_hbm,
    *refs,
):
    count = len(chunks)
    slabs, refs = refs[:count], refs[count:]
    kernel_body(nz, chunks, faces_total, feat_hbm, w_hbm, cw_hbm, lab_hbm, slabs, *refs)


def kernel_body(
    nz, chunks, faces_total,
    feat_hbm, w_hbm, cw_hbm, lab_hbm,
    slabs, cout,
    feat, w, cw_ref, lab_ref, gath, praw, rraw, unit_all, cu, tot_s, tot_r, cosg, cg_all, pgrad, rgrad,
    rg_all, cpart, cslots, f, send1, recv1, send2, recv2,
    load_sem, x_send, x_recv, p_send, p_recv, own_sem, c_send, c_recv,
    ca_send, ca_recv, cp_send, cp_recv, z_send, z_recv, y_send, y_recv, n_send, n_recv,
):
    rows, fin = feat.shape
    classes, dim = cw_ref.shape
    wide = gath.shape[1]
    per = (fin // LANES // PLANE) * LANES
    cq = classes // PLANE
    cz = cq // nz
    dp = lax.axis_index("dp")
    x = lax.axis_index("cls")
    z, q = dp // PLANE, dp % PLANE
    y, core = q // 2, q % 2
    q_y = (1 - y) * 2 + core
    q_c = y * 2 + 1 - core
    q_d = (1 - y) * 2 + 1 - core
    x_dev = {"cls": 1 - x}
    y_dev = {"dp": z * PLANE + q_y}
    c_dev = {"dp": z * PLANE + q_c}
    half, side = z // 2, z % 2
    near = {"dp": (half * 2 + 1 - side) * PLANE + q}
    far = {"dp": ((1 - half) * 2 + side) * PLANE + q}
    owned = side * 2 + half
    beside = side * 2 + 1 - half
    plane = [(q + d) % PLANE for d in range(1, PLANE)]
    plane_from = [(q + PLANE - d) % PLANE for d in range(1, PLANE)]
    line = [(z + d) % nz for d in range(1, nz)]
    line_from = [(z + nz - d) % nz for d in range(1, nz)]
    pending = []

    def send(cond, make):
        if cond is None:
            make().start()
        else:
            @pl.when(cond)
            def _():
                make().start()
        pending.append((cond, make))

    def remote(src, dst, s, r, dev):
        return lambda: pltpu.make_async_remote_copy(
            src_ref=src(), dst_ref=dst(), send_sem=s(), recv_sem=r(),
            device_id=dev, device_id_type=MESH,
        )

    def landed(dst, r):
        pltpu.make_async_remote_copy(
            src_ref=dst, dst_ref=dst, send_sem=r, recv_sem=r,
            device_id=x_dev, device_id_type=MESH,
        ).wait_recv()

    def at(i, n):
        return pl.ds(pl.multiple_of(i * n, n), n)

    small = [
        pltpu.make_async_copy(cw_hbm, cw_ref, own_sem.at[1]),
        pltpu.make_async_copy(lab_hbm, lab_ref, own_sem.at[2]),
    ]
    for copy in small:
        copy.start()
    steps = load_sem.shape[0]
    kk = fin // steps
    feat_load = pltpu.make_async_copy(feat_hbm, feat, own_sem.at[3])
    feat_load.start()
    loads = []
    for k in range(steps):
        part = pl.ds(k * kk, kk)
        copy = pltpu.make_async_copy(w_hbm.at[part, :], w.at[part, :], load_sem.at[k])
        copy.start()
        loads.append(copy)

    barrier = pltpu.get_barrier_semaphore()
    peers = [x_dev] + [{"dp": z * PLANE + p} for p in plane] + [{"dp": t * PLANE + q} for t in line]
    for dev in peers:
        pl.semaphore_signal(barrier, inc=1, device_id=dev, device_id_type=MESH)
    pl.semaphore_wait(barrier, len(peers))

    mine = at(q, rows)
    own_feat = pltpu.make_async_copy(
        feat_hbm.at[:, pl.ds(pl.multiple_of(q * per, LANES), wide)], gath.at[mine, :], own_sem.at[0]
    )
    own_feat.start()
    feat_load.wait()
    for i, p in enumerate(plane):
        cols = pl.ds(pl.multiple_of(p * per, LANES), wide)
        send(None, remote(
            lambda cols=cols: feat.at[:, cols], lambda: gath.at[mine, :],
            lambda i=i: p_send.at[0, i], lambda i=i: p_recv.at[0, i], {"dp": z * PLANE + p},
        ))

    for h in range(2):
        columns = pl.ds(h * (dim // 2), dim // 2)
        total = jnp.zeros((rows, dim // 2), jnp.float32)
        for k in range(steps):
            if h == 0:
                loads[k].wait()
            part = pl.ds(k * kk, kk)
            total = total + jnp.dot(
                feat[:, part], w[part, columns], preferred_element_type=jnp.float32
            )
        praw[:, columns] = total.astype(ROUNDED)
        send(None, remote(
            lambda columns=columns: praw.at[:, columns], lambda columns=columns: rraw.at[:, columns],
            lambda h=h: x_send.at[3 * h], lambda h=h: x_recv.at[3 * h], x_dev,
        ))

    for copy in small:
        copy.wait()
    class_f = cw_ref[...].astype(jnp.float32)
    class_norm = jnp.sqrt(jnp.sum(class_f * class_f, axis=1, keepdims=True) + EPSILON)
    cu[...] = (class_f / class_norm).astype(ROUNDED)

    landed(rraw.at[:, pl.ds(0, dim // 2)], x_recv.at[0])
    landed(rraw.at[:, pl.ds(dim // 2, dim // 2)], x_recv.at[3])
    raw = praw[...].astype(jnp.float32) + rraw[...].astype(jnp.float32)
    norm = jnp.sqrt(jnp.sum(raw * raw, axis=1, keepdims=True) + EPSILON)
    unit_f = raw / norm
    unit = unit_f.astype(ROUNDED)
    unit_all[mine, :] = unit
    for i, dev in enumerate((y_dev, c_dev)):
        send(None, remote(
            lambda: unit_all.at[mine, :], lambda: unit_all.at[mine, :],
            lambda i=i: p_send.at[1, i], lambda i=i: p_recv.at[1, i], dev,
        ))
    cosine = lax.dot_general(
        unit, cu[...], (((1,), (1,)), ((), ())), preferred_element_type=jnp.float32
    )
    columns = x * classes + lax.broadcasted_iota(jnp.int32, cosine.shape, 1)
    label = jnp.broadcast_to(lab_ref[...], (LANES, rows)).T[:, 0:1]
    is_target = columns == label
    powers, slopes = margin_terms(cosine, is_target)
    partial = jnp.sum(powers, axis=1, keepdims=True)
    tot_s[...] = jnp.broadcast_to(partial, (rows, LANES)).T[0:8, :]
    send(None, remote(lambda: tot_s, lambda: tot_r, lambda: x_send.at[1], lambda: x_recv.at[1], x_dev))
    landed(tot_r, x_recv.at[1])
    totals = partial + jnp.broadcast_to(tot_r[0:1, :], (LANES, rows)).T[:, 0:1]
    weight = 1.0 / math.sqrt(faces_total)
    grad = ((powers / totals - is_target.astype(jnp.float32)) * weight * slopes).astype(ROUNDED)
    cosg[...] = grad
    pgrad[...] = jnp.dot(grad, cu[...], preferred_element_type=jnp.float32).astype(ROUNDED)
    send(None, remote(lambda: pgrad, lambda: rgrad, lambda: x_send.at[2], lambda: x_recv.at[2], x_dev))
    for i, p in enumerate(plane):
        cols = at(p, cq)
        send(None, remote(
            lambda cols=cols: cosg.at[:, cols], lambda: cg_all.at[mine, :],
            lambda i=i: p_send.at[2, i], lambda i=i: p_recv.at[2, i], {"dp": z * PLANE + p},
        ))
    cg_all[mine, :] = cosg[:, at(q, cq)]

    landed(rgrad, x_recv.at[2])
    unit_grad = pgrad[...].astype(jnp.float32) + rgrad[...].astype(jnp.float32)
    along = jnp.sum(unit_f * unit_grad, axis=1, keepdims=True)
    rg_all[mine, :] = ((unit_grad - unit_f * along) / norm).astype(ROUNDED)
    for i, p in enumerate(plane):
        send(None, remote(
            lambda: rg_all.at[mine, :], lambda: rg_all.at[mine, :],
            lambda i=i: p_send.at[3, i], lambda i=i: p_recv.at[3, i], {"dp": z * PLANE + p},
        ))

    across = at(q_y, rows)
    landed(unit_all.at[across, :], p_recv.at[1, 0])
    send(None, remote(
        lambda: unit_all.at[across, :], lambda: unit_all.at[across, :],
        lambda: p_send.at[1, 2], lambda: p_recv.at[1, 2], c_dev,
    ))
    own_feat.wait()
    for i, p in enumerate(plane_from):
        theirs = at(p, rows)
        landed(gath.at[theirs, :], p_recv.at[0, i])
        landed(rg_all.at[theirs, :], p_recv.at[3, i])

    count = len(chunks)

    def has(c, owner):
        return owner == PLANE - 1 if chunks[c][0] >= per else None

    def only(cond, body):
        if cond is None:
            body()
        else:
            pl.when(cond)(body)

    def exchange(cond, src, dst, sends, recvs, dev, *spot):
        send(cond, remote(
            lambda: src(), lambda: dst(), lambda: sends.at[spot], lambda: recvs.at[spot], dev,
        ))

    def pair(c, p, which):
        return slabs[c].at[p, pl.ds(which * 2, 2), :, :]

    def multiply(c, part):
        def body():
            product = lax.dot_general(
                gath[:, part], rg_all[...], (((0,), (0,)), ((), ())), preferred_element_type=jnp.float32
            )
            for j in range(nz):
                f[j, part, :] = product[:, j * LANES:(j + 1) * LANES]
            for i in range(2):
                send1[i, part, :] = f[(1 - side) * 2 + i, part, :].astype(ROUNDED)

        only(has(c, q), body)
        exchange(
            has(c, q), lambda: send1.at[:, part, :], lambda: recv1.at[:, part, :], z_send, z_recv, near, 0, c
        )

    def sum_near(c, part):
        def body():
            landed(recv1.at[:, part, :], z_recv.at[0, c])
            send2[part, :] = (
                f[side * 2 + 1 - half, part, :] + recv1[1 - half, part, :].astype(jnp.float32)
            ).astype(ROUNDED)

        only(has(c, q), body)
        exchange(has(c, q), lambda: send2.at[part, :], lambda: recv2.at[part, :], z_send, z_recv, far, 1, c)

    def sum_far(c, part):
        def body():
            landed(recv2.at[part, :], z_recv.at[1, c])
            slabs[c][q, owned, :, :] = (
                f[owned, part, :]
                + recv1[half, part, :].astype(jnp.float32)
                + recv2[part, :].astype(jnp.float32)
            ).astype(ROUNDED)

        only(has(c, q), body)
        block = lambda: slabs[c].at[q, owned, :, :]
        exchange(has(c, q), block, block, z_send, z_recv, far, 2, c)
        exchange(has(c, q), block, block, y_send, y_recv, y_dev, 0, c)
        exchange(has(c, q), block, block, n_send, n_recv, c_dev, 0, c)

    def gather_far(c, part):
        other = lambda: slabs[c].at[q, beside, :, :]
        only(has(c, q), lambda: landed(other(), z_recv.at[2, c]))
        block = lambda: pair(c, q, side)
        exchange(has(c, q), block, block, z_send, z_recv, near, 3, c)
        exchange(has(c, q), other, other, y_send, y_recv, y_dev, 1, c)
        exchange(has(c, q), other, other, n_send, n_recv, c_dev, 1, c)

    def gather_near(c, part):
        block = lambda: pair(c, q, 1 - side)
        only(has(c, q), lambda: landed(block(), z_recv.at[3, c]))
        exchange(has(c, q), block, block, y_send, y_recv, y_dev, 2, c)
        exchange(has(c, q), block, block, n_send, n_recv, c_dev, 2, c)

    def arrived(c, p, recvs, first):
        landed(slabs[c].at[p, owned, :, :], recvs.at[first, c])
        landed(slabs[c].at[p, beside, :, :], recvs.at[first + 1, c])

    def gather_across(c, part):
        for i, which in enumerate((side, 1 - side)):
            block = lambda which=which: pair(c, q_y, which)
            if i == 0:
                only(has(c, q_y), lambda: arrived(c, q_y, y_recv, 0))
            else:
                only(has(c, q_y), lambda: landed(block(), y_recv.at[2, c]))
            exchange(has(c, q_y), block, block, n_send, n_recv, c_dev, 3 + i, c)

    def gather_core(c, part):
        def own():
            arrived(c, q_c, n_recv, 0)
            landed(pair(c, q_c, 1 - side), n_recv.at[2, c])

        def crossed():
            landed(pair(c, q_d, side), n_recv.at[3, c])
            landed(pair(c, q_d, 1 - side), n_recv.at[4, c])

        only(has(c, q_c), own)
        only(has(c, q_d), crossed)

    def class_sums():
        for i, p in enumerate(plane_from):
            landed(cg_all.at[at(p, rows), :], p_recv.at[2, i])
        landed(unit_all.at[at(q_c, rows), :], p_recv.at[1, 1])
        landed(unit_all.at[at(q_d, rows), :], p_recv.at[1, 2])
        cpart[...] = lax.dot_general(
            cg_all[...], unit_all[...], (((0,), (0,)), ((), ())), preferred_element_type=jnp.float32
        )
        for i, t in enumerate(line):
            send(None, remote(
                lambda t=t: cpart.at[at(t, cz), :], lambda: cslots.at[z],
                lambda i=i: c_send.at[i], lambda i=i: c_recv.at[i], {"dp": t * PLANE + q},
            ))

    def class_rows():
        for i, t in enumerate(line_from):
            landed(cslots.at[t], c_recv.at[i])
        here = pl.ds(pl.multiple_of(q * cq + z * cz, cz), cz)
        sums = cpart[at(z, cz), :]
        for i, t in enumerate(line_from):
            sums = sums + cslots[t]
        mine_f = cw_ref[here, :].astype(jnp.float32)
        mine_norm = jnp.sqrt(jnp.sum(mine_f * mine_f, axis=1, keepdims=True) + EPSILON)
        mine_unit = mine_f / mine_norm
        along = jnp.sum(mine_unit * sums, axis=1, keepdims=True)
        cout[here, :] = ((sums - mine_unit * along) / mine_norm).astype(ROUNDED)
        for i, t in enumerate(line):
            send(None, remote(
                lambda: cout.at[here, :], lambda: cout.at[here, :],
                lambda i=i: ca_send.at[i], lambda i=i: ca_recv.at[i], {"dp": t * PLANE + q},
            ))

    def class_plane():
        for i, t in enumerate(line_from):
            there = pl.ds(pl.multiple_of(q * cq + t * cz, cz), cz)
            landed(cout.at[there, :], ca_recv.at[i])
        block = lambda: cout.at[at(q, cq), :]
        send(None, remote(block, block, lambda: cp_send.at[0], lambda: cp_recv.at[0], y_dev))
        send(None, remote(block, block, lambda: cp_send.at[1], lambda: cp_recv.at[1], c_dev))

    def class_across():
        landed(cout.at[at(q_y, cq), :], cp_recv.at[0])
        block = lambda: cout.at[at(q_y, cq), :]
        send(None, remote(block, block, lambda: cp_send.at[2], lambda: cp_recv.at[2], c_dev))

    stages = (
        (0, multiply), (1, sum_near), (2, sum_far), (3, gather_far), (4, gather_near),
        (7, gather_across), (9, gather_core),
    )
    starts, settled = [], [0]

    def settle(end):
        for cond, make in pending[settled[0]:end]:
            only(cond, lambda: make().wait_send())
        settled[0] = max(settled[0], end)

    for tick in range(count + stages[-1][0]):
        for late, run in stages:
            c = tick - late
            if 0 <= c < count:
                run(c, pl.ds(*chunks[c]))
        if tick == 2:
            class_sums()
        if tick == 5:
            class_rows()
        if tick == 8:
            class_plane()
        if tick == 11:
            class_across()
        starts.append(len(pending))
        if tick >= 5:
            settle(starts[tick - 5])

    landed(cout.at[at(q_c, cq), :], cp_recv.at[1])
    landed(cout.at[at(q_d, cq), :], cp_recv.at[2])
    settle(len(pending))


def place(chunks, per, *refs):
    count = len(chunks)
    slabs, cout = refs[:count], refs[count]
    fc_out, class_out, rows_of, sems = refs[count + 1:]
    copies = [pltpu.make_async_copy(cout, class_out, sems.at[0])]
    copies[0].start()
    for p in range(PLANE):
        for c, (first, size) in enumerate(chunks):
            if p == PLANE - 1 or first < per:
                start = p * per + first
                for j in range(slabs[c].shape[1]):
                    rows_of[pl.ds(start, size), pl.ds(j * LANES, LANES)] = slabs[c][p, j, pl.ds(0, size), :]
                copies.append(pltpu.make_async_copy(
                    rows_of.at[pl.ds(start, size), :], fc_out.at[pl.ds(start, size), :], sems.at[len(copies)],
                ))
                copies[-1].start()
    for copy in copies:
        copy.wait()


def fused(n_dp, features, fc_weight, class_weight, labels):
    rows, fin = features.shape
    classes, dim = class_weight.shape
    nz = n_dp // PLANE
    blocks = fin // LANES
    wide = (blocks - (PLANE - 1) * (blocks // PLANE)) * LANES
    per = blocks // PLANE
    chunks = split_rows(per)
    if wide // LANES > per:
        chunks.append((per * LANES, wide - per * LANES))
    count = len(chunks)
    steps = max(d for d in range(1, 9) if blocks % d == 0)
    bf, f32, dma = jnp.bfloat16, jnp.float32, pltpu.SemaphoreType.DMA
    vmem, whole = pltpu.VMEM, pl.BlockSpec(memory_space=pltpu.VMEM)
    anywhere = pl.BlockSpec(memory_space=pl.ANY)
    results = pl.pallas_call(
        functools.partial(kernel, nz, chunks, rows * n_dp),
        out_shape=(
            *[jax.ShapeDtypeStruct((PLANE, nz, size, LANES), bf) for _, size in chunks],
            jax.ShapeDtypeStruct((classes, dim), bf),
        ),
        in_specs=[anywhere] * 4,
        out_specs=(whole,) * (count + 1),
        scratch_shapes=[
            vmem((rows, fin), bf), vmem((fin, dim), bf), vmem((classes, dim), bf),
            vmem((1, rows), jnp.int32), vmem((PLANE * rows, wide), bf),
            vmem((rows, dim), bf), vmem((rows, dim), bf), vmem((PLANE * rows, dim), bf),
            vmem((classes, dim), bf), vmem((8, rows), f32), vmem((8, rows), f32),
            vmem((rows, classes), bf), vmem((PLANE * rows, classes // PLANE), bf),
            vmem((rows, dim), bf), vmem((rows, dim), bf), vmem((PLANE * rows, dim), bf),
            vmem((classes // PLANE, dim), f32), vmem((nz, classes // PLANE // nz, dim), f32),
            vmem((nz, wide, LANES), f32), vmem((2, wide, LANES), bf), vmem((2, wide, LANES), bf),
            vmem((wide, LANES), bf), vmem((wide, LANES), bf),
            dma((steps,)), dma((4,)), dma((4,)), dma((4, PLANE - 1)), dma((4, PLANE - 1)),
            dma((4,)), dma((nz - 1,)), dma((nz - 1,)), dma((nz - 1,)), dma((nz - 1,)),
            dma((3,)), dma((3,)), dma((4, count)), dma((4, count)),
            dma((3, count)), dma((3, count)), dma((5, count)), dma((5, count)),
        ],
        compiler_params=pltpu.CompilerParams(
            collective_id=0, has_side_effects=True, vmem_limit_bytes=46 * 2**20
        ),
    )(features, fc_weight, class_weight, labels.reshape(1, rows))
    return pl.pallas_call(
        functools.partial(place, chunks, blocks // PLANE * LANES),
        out_shape=(
            jax.ShapeDtypeStruct((fin, dim), bf),
            jax.ShapeDtypeStruct((classes, dim), bf),
        ),
        in_specs=[whole] * (count + 1),
        out_specs=(anywhere, anywhere),
        scratch_shapes=[vmem((fin, dim), bf), dma((PLANE * count + 1,))],
        compiler_params=pltpu.CompilerParams(vmem_limit_bytes=16 * 2**20),
    )(*results)


def choose(n_dp, n_cls, features, fc_weight, class_weight, labels):
    rows, fin = features.shape
    classes, dim = class_weight.shape
    nz = n_dp // PLANE
    fits = (
        n_cls == 2
        and n_dp % PLANE == 0
        and nz == 4
        and dim == nz * LANES
        and fin % LANES == 0
        and fin // LANES >= PLANE
        and rows == LANES
        and classes % (PLANE * LANES) == 0
        and classes // PLANE % (16 * nz) == 0
        and classes <= 512
        and fin <= 6272
    )
    if fits:
        return fused(n_dp, features, fc_weight, class_weight, labels)
    return shards(features, fc_weight, class_weight, labels)


def solution(mesh):
    placed = (P("dp", "cls"), P("cls", None), P("cls", None), P("dp"))
    return jax.shard_map(
        functools.partial(choose, mesh.shape["dp"], mesh.shape["cls"]),
        mesh=mesh,
        in_specs=placed,
        out_specs=(P("cls", None), P("cls", None)),
        check_vma=False,
    )
```

```python
import functools
import math

import jax
import jax.numpy as jnp
from jax import lax
from jax.experimental import pallas as pl
from jax.experimental.pallas import tpu as pltpu
from jax.sharding import PartitionSpec as P

SCALE = 64.0
MARGIN = 0.5
SOFTEN = 0.01
EPSILON = 1e-06


def margin_terms(cosine, is_target):
    sine = jnp.sqrt(1.0 + SOFTEN - cosine * cosine)
    shifted = cosine * math.cos(MARGIN) - sine * math.sin(MARGIN)
    powers = jnp.exp(SCALE * jnp.where(is_target, shifted, cosine))
    slopes = SCALE * jnp.where(is_target, math.cos(MARGIN) + math.sin(MARGIN) * cosine / sine, 1.0)
    return (powers, slopes)


def softmax_grad(powers, totals, slopes, is_target, loss_weight):
    onehot = is_target.astype(jnp.float32)
    return ((powers / totals[:, None] - onehot) * loss_weight * slopes).astype(jnp.bfloat16)


def shards(features, fc_weight, class_weight, labels):
    rows_group = features.shape[0]
    class_count = class_weight.shape[0]
    loss_weight = 1.0 / math.sqrt(rows_group * lax.axis_size("dp"))
    position = lax.axis_index("cls")
    rows_block = features
    raw_embed = lax.psum_scatter(
        jnp.dot(rows_block, fc_weight, preferred_element_type=jnp.float32).astype(jnp.bfloat16),
        "cls",
        scatter_dimension=0,
        tiled=True,
    ).astype(jnp.float32)
    embed_norm = jnp.sqrt(jnp.sum(raw_embed * raw_embed, axis=1, keepdims=True) + EPSILON)
    unit_f = raw_embed / embed_norm
    unit_embed = unit_f.astype(jnp.bfloat16)
    class_f = class_weight.astype(jnp.float32)
    class_norm = jnp.sqrt(jnp.sum(class_f * class_f, axis=1, keepdims=True) + EPSILON)
    class_unit_f = class_f / class_norm
    class_unit = class_unit_f.astype(jnp.bfloat16)
    faces_all = lax.all_gather(unit_embed, "cls", axis=0, tiled=True)
    cosine = lax.dot_general(
        faces_all, class_unit, (((1,), (1,)), ((), ())), preferred_element_type=jnp.float32
    )
    columns = position * class_count + lax.broadcasted_iota(jnp.int32, cosine.shape, 1)
    is_target = columns == labels[:, None]
    powers, slopes = margin_terms(cosine, is_target)
    totals = lax.psum(jnp.sum(powers, axis=1), "cls")
    cos_grad = softmax_grad(powers, totals, slopes, is_target, loss_weight)
    rows_block = cos_grad
    unit_grad = lax.psum_scatter(
        jnp.dot(rows_block, class_unit, preferred_element_type=jnp.float32).astype(jnp.bfloat16),
        "cls",
        scatter_dimension=0,
        tiled=True,
    ).astype(jnp.float32)
    class_part = lax.dot_general(
        cos_grad, faces_all, (((0,), (0,)), ((), ())), preferred_element_type=jnp.float32
    )
    raw_grad = (
        (unit_grad - unit_f * jnp.sum(unit_f * unit_grad, axis=1, keepdims=True)) / embed_norm
    ).astype(jnp.bfloat16)
    rows_block = features
    fc_part = lax.dot_general(
        rows_block,
        lax.all_gather(raw_grad, "cls", axis=0, tiled=True),
        (((0,), (0,)), ((), ())),
        preferred_element_type=jnp.float32,
    )
    fc_total, class_total = lax.psum((fc_part, class_part), "dp")
    fc_out = fc_total.astype(jnp.bfloat16)
    class_grad = (
        class_total - class_unit_f * jnp.sum(class_unit_f * class_total, axis=1, keepdims=True)
    ) / class_norm
    return (fc_out, class_grad.astype(jnp.bfloat16))


MESH = pl.DeviceIdType.MESH
LANES = 128
PLANE = 4
ROUNDED = jnp.bfloat16


def split_rows(blocks):
    sizes = [1] + [2] * ((blocks - 1) // 2)
    sizes += [1] * (blocks - sum(sizes))
    return [(sum(sizes[:i]) * LANES, size * LANES) for i, size in enumerate(sizes)]


def kernel(
    nz, chunks, faces_total,
    feat_hbm, w_hbm, cw_hbm, lab_hbm,
    *refs,
):
    count = len(chunks)
    slabs, refs = refs[:count], refs[count:]
    kernel_body(nz, chunks, faces_total, feat_hbm, w_hbm, cw_hbm, lab_hbm, slabs, *refs)


def kernel_body(
    nz, chunks, faces_total,
    feat_hbm, w_hbm, cw_hbm, lab_hbm,
    slabs, cout,
    feat, w, cw_ref, lab_ref, gath, praw, rraw, unit_all, cu, tot_s, tot_r, cosg, cg_all, pgrad, rgrad,
    rg_all, cpart, cslots, f, send1, recv1, send2, recv2,
    load_sem, x_send, x_recv, p_send, p_recv, own_sem, c_send, c_recv,
    ca_send, ca_recv, cp_send, cp_recv, z_send, z_recv, y_send, y_recv, n_send, n_recv,
):
    rows, fin = feat.shape
    classes, dim = cw_ref.shape
    wide = gath.shape[1]
    per = (fin // LANES // PLANE) * LANES
    cq = classes // PLANE
    cz = cq // nz
    dp = lax.axis_index("dp")
    x = lax.axis_index("cls")
    z, q = dp // PLANE, dp % PLANE
    y, core = q // 2, q % 2
    q_y = (1 - y) * 2 + core
    q_c = y * 2 + 1 - core
    q_d = (1 - y) * 2 + 1 - core
    x_dev = {"cls": 1 - x}
    y_dev = {"dp": z * PLANE + q_y}
    c_dev = {"dp": z * PLANE + q_c}
    half, side = z // 2, z % 2
    near = {"dp": (half * 2 + 1 - side) * PLANE + q}
    far = {"dp": ((1 - half) * 2 + side) * PLANE + q}
    owned = side * 2 + half
    beside = side * 2 + 1 - half
    plane = [(q + d) % PLANE for d in range(1, PLANE)]
    plane_from = [(q + PLANE - d) % PLANE for d in range(1, PLANE)]
    line = [(z + d) % nz for d in range(1, nz)]
    line_from = [(z + nz - d) % nz for d in range(1, nz)]
    pending = []

    def send(cond, make):
        if cond is None:
            make().start()
        else:
            @pl.when(cond)
            def _():
                make().start()
        pending.append((cond, make))

    def remote(src, dst, s, r, dev):
        return lambda: pltpu.make_async_remote_copy(
            src_ref=src(), dst_ref=dst(), send_sem=s(), recv_sem=r(),
            device_id=dev, device_id_type=MESH,
        )

    def landed(dst, r):
        pltpu.make_async_remote_copy(
            src_ref=dst, dst_ref=dst, send_sem=r, recv_sem=r,
            device_id=x_dev, device_id_type=MESH,
        ).wait_recv()

    def at(i, n):
        return pl.ds(pl.multiple_of(i * n, n), n)

    small = [
        pltpu.make_async_copy(cw_hbm, cw_ref, own_sem.at[1]),
        pltpu.make_async_copy(lab_hbm, lab_ref, own_sem.at[2]),
    ]
    for copy in small:
        copy.start()
    steps = load_sem.shape[0]
    kk = fin // steps
    feat_load = pltpu.make_async_copy(feat_hbm, feat, own_sem.at[3])
    feat_load.start()
    loads = []
    for k in range(steps):
        part = pl.ds(k * kk, kk)
        copy = pltpu.make_async_copy(w_hbm.at[part, :], w.at[part, :], load_sem.at[k])
        copy.start()
        loads.append(copy)

    barrier = pltpu.get_barrier_semaphore()
    peers = [x_dev] + [{"dp": z * PLANE + p} for p in plane] + [{"dp": t * PLANE + q} for t in line]
    for dev in peers:
        pl.semaphore_signal(barrier, inc=1, device_id=dev, device_id_type=MESH)
    pl.semaphore_wait(barrier, len(peers))

    mine = at(q, rows)
    own_feat = pltpu.make_async_copy(
        feat_hbm.at[:, pl.ds(pl.multiple_of(q * per, LANES), wide)], gath.at[mine, :], own_sem.at[0]
    )
    own_feat.start()
    feat_load.wait()
    for i, p in enumerate(plane):
        cols = pl.ds(pl.multiple_of(p * per, LANES), wide)
        send(None, remote(
            lambda cols=cols: feat.at[:, cols], lambda: gath.at[mine, :],
            lambda i=i: p_send.at[0, i], lambda i=i: p_recv.at[0, i], {"dp": z * PLANE + p},
        ))

    for h in range(2):
        columns = pl.ds(h * (dim // 2), dim // 2)
        total = jnp.zeros((rows, dim // 2), jnp.float32)
        for k in range(steps):
            if h == 0:
                loads[k].wait()
            part = pl.ds(k * kk, kk)
            total = total + jnp.dot(
                feat[:, part], w[part, columns], preferred_element_type=jnp.float32
            )
        praw[:, columns] = total.astype(ROUNDED)
        send(None, remote(
            lambda columns=columns: praw.at[:, columns], lambda columns=columns: rraw.at[:, columns],
            lambda h=h: x_send.at[3 * h], lambda h=h: x_recv.at[3 * h], x_dev,
        ))

    for copy in small:
        copy.wait()
    class_f = cw_ref[...].astype(jnp.float32)
    class_norm = jnp.sqrt(jnp.sum(class_f * class_f, axis=1, keepdims=True) + EPSILON)
    cu[...] = (class_f / class_norm).astype(ROUNDED)

    landed(rraw.at[:, pl.ds(0, dim // 2)], x_recv.at[0])
    landed(rraw.at[:, pl.ds(dim // 2, dim // 2)], x_recv.at[3])
    raw = praw[...].astype(jnp.float32) + rraw[...].astype(jnp.float32)
    norm = jnp.sqrt(jnp.sum(raw * raw, axis=1, keepdims=True) + EPSILON)
    unit_f = raw / norm
    unit = unit_f.astype(ROUNDED)
    unit_all[mine, :] = unit
    for i, dev in enumerate((y_dev, c_dev)):
        send(None, remote(
            lambda: unit_all.at[mine, :], lambda: unit_all.at[mine, :],
            lambda i=i: p_send.at[1, i], lambda i=i: p_recv.at[1, i], dev,
        ))
    cosine = lax.dot_general(
        unit, cu[...], (((1,), (1,)), ((), ())), preferred_element_type=jnp.float32
    )
    columns = x * classes + lax.broadcasted_iota(jnp.int32, cosine.shape, 1)
    label = jnp.broadcast_to(lab_ref[...], (LANES, rows)).T[:, 0:1]
    is_target = columns == label
    powers, slopes = margin_terms(cosine, is_target)
    partial = jnp.sum(powers, axis=1, keepdims=True)
    tot_s[...] = jnp.broadcast_to(partial, (rows, LANES)).T[0:8, :]
    send(None, remote(lambda: tot_s, lambda: tot_r, lambda: x_send.at[1], lambda: x_recv.at[1], x_dev))
    landed(tot_r, x_recv.at[1])
    totals = partial + jnp.broadcast_to(tot_r[0:1, :], (LANES, rows)).T[:, 0:1]
    weight = 1.0 / math.sqrt(faces_total)
    grad = ((powers / totals - is_target.astype(jnp.float32)) * weight * slopes).astype(ROUNDED)
    cosg[...] = grad
    pgrad[...] = jnp.dot(grad, cu[...], preferred_element_type=jnp.float32).astype(ROUNDED)
    send(None, remote(lambda: pgrad, lambda: rgrad, lambda: x_send.at[2], lambda: x_recv.at[2], x_dev))
    for i, p in enumerate(plane):
        cols = at(p, cq)
        send(None, remote(
            lambda cols=cols: cosg.at[:, cols], lambda: cg_all.at[mine, :],
            lambda i=i: p_send.at[2, i], lambda i=i: p_recv.at[2, i], {"dp": z * PLANE + p},
        ))
    cg_all[mine, :] = cosg[:, at(q, cq)]

    landed(rgrad, x_recv.at[2])
    unit_grad = pgrad[...].astype(jnp.float32) + rgrad[...].astype(jnp.float32)
    along = jnp.sum(unit_f * unit_grad, axis=1, keepdims=True)
    rg_all[mine, :] = ((unit_grad - unit_f * along) / norm).astype(ROUNDED)
    for i, dev in enumerate((y_dev, c_dev)):
        send(None, remote(
            lambda: rg_all.at[mine, :], lambda: rg_all.at[mine, :],
            lambda i=i: p_send.at[3, i], lambda i=i: p_recv.at[3, i], dev,
        ))

    across = at(q_y, rows)
    landed(unit_all.at[across, :], p_recv.at[1, 0])
    send(None, remote(
        lambda: unit_all.at[across, :], lambda: unit_all.at[across, :],
        lambda: p_send.at[1, 2], lambda: p_recv.at[1, 2], c_dev,
    ))
    for i, p in enumerate(plane_from):
        landed(cg_all.at[at(p, rows), :], p_recv.at[2, i])
    landed(unit_all.at[at(q_c, rows), :], p_recv.at[1, 1])
    landed(unit_all.at[at(q_d, rows), :], p_recv.at[1, 2])
    cpart[...] = lax.dot_general(
        cg_all[...], unit_all[...], (((0,), (0,)), ((), ())), preferred_element_type=jnp.float32
    )
    for i, t in enumerate(line):
        send(None, remote(
            lambda t=t: cpart.at[at(t, cz), :], lambda: cslots.at[z],
            lambda i=i: c_send.at[i], lambda i=i: c_recv.at[i], {"dp": t * PLANE + q},
        ))

    landed(rg_all.at[across, :], p_recv.at[3, 0])
    send(None, remote(
        lambda: rg_all.at[across, :], lambda: rg_all.at[across, :],
        lambda: p_send.at[3, 2], lambda: p_recv.at[3, 2], c_dev,
    ))
    own_feat.wait()
    for i, p in enumerate(plane_from):
        landed(gath.at[at(p, rows), :], p_recv.at[0, i])
    landed(rg_all.at[at(q_c, rows), :], p_recv.at[3, 1])
    landed(rg_all.at[at(q_d, rows), :], p_recv.at[3, 2])

    count = len(chunks)

    def has(c, owner):
        return owner == PLANE - 1 if chunks[c][0] >= per else None

    def only(cond, body):
        if cond is None:
            body()
        else:
            pl.when(cond)(body)

    def exchange(cond, src, dst, sends, recvs, dev, *spot):
        send(cond, remote(
            lambda: src(), lambda: dst(), lambda: sends.at[spot], lambda: recvs.at[spot], dev,
        ))

    def pair(c, p, which):
        return slabs[c].at[p, pl.ds(which * 2, 2), :, :]

    def multiply(c, part):
        def body():
            product = lax.dot_general(
                gath[:, part], rg_all[...], (((0,), (0,)), ((), ())), preferred_element_type=jnp.float32
            )
            for j in range(nz):
                f[j, part, :] = product[:, j * LANES:(j + 1) * LANES]
            for i in range(2):
                send1[i, part, :] = f[(1 - side) * 2 + i, part, :].astype(ROUNDED)

        only(has(c, q), body)
        exchange(
            has(c, q), lambda: send1.at[:, part, :], lambda: recv1.at[:, part, :], z_send, z_recv, near, 0, c
        )

    def sum_near(c, part):
        def body():
            landed(recv1.at[:, part, :], z_recv.at[0, c])
            send2[part, :] = (
                f[side * 2 + 1 - half, part, :] + recv1[1 - half, part, :].astype(jnp.float32)
            ).astype(ROUNDED)

        only(has(c, q), body)
        exchange(has(c, q), lambda: send2.at[part, :], lambda: recv2.at[part, :], z_send, z_recv, far, 1, c)

    def sum_far(c, part):
        def body():
            landed(recv2.at[part, :], z_recv.at[1, c])
            slabs[c][q, owned, :, :] = (
                f[owned, part, :]
                + recv1[half, part, :].astype(jnp.float32)
                + recv2[part, :].astype(jnp.float32)
            ).astype(ROUNDED)

        only(has(c, q), body)
        block = lambda: slabs[c].at[q, owned, :, :]
        exchange(has(c, q), block, block, z_send, z_recv, far, 2, c)
        exchange(has(c, q), block, block, y_send, y_recv, y_dev, 0, c)
        exchange(has(c, q), block, block, n_send, n_recv, c_dev, 0, c)

    def gather_far(c, part):
        other = lambda: slabs[c].at[q, beside, :, :]
        only(has(c, q), lambda: landed(other(), z_recv.at[2, c]))
        block = lambda: pair(c, q, side)
        exchange(has(c, q), block, block, z_send, z_recv, near, 3, c)
        exchange(has(c, q), other, other, y_send, y_recv, y_dev, 1, c)
        exchange(has(c, q), other, other, n_send, n_recv, c_dev, 1, c)

    def gather_near(c, part):
        block = lambda: pair(c, q, 1 - side)
        only(has(c, q), lambda: landed(block(), z_recv.at[3, c]))
        exchange(has(c, q), block, block, y_send, y_recv, y_dev, 2, c)
        exchange(has(c, q), block, block, n_send, n_recv, c_dev, 2, c)

    def arrived(c, p, recvs, first):
        landed(slabs[c].at[p, owned, :, :], recvs.at[first, c])
        landed(slabs[c].at[p, beside, :, :], recvs.at[first + 1, c])

    def gather_across(c, part):
        for i, which in enumerate((side, 1 - side)):
            block = lambda which=which: pair(c, q_y, which)
            if i == 0:
                only(has(c, q_y), lambda: arrived(c, q_y, y_recv, 0))
            else:
                only(has(c, q_y), lambda: landed(block(), y_recv.at[2, c]))
            exchange(has(c, q_y), block, block, n_send, n_recv, c_dev, 3 + i, c)

    def gather_core(c, part):
        def own():
            arrived(c, q_c, n_recv, 0)
            landed(pair(c, q_c, 1 - side), n_recv.at[2, c])

        def crossed():
            landed(pair(c, q_d, side), n_recv.at[3, c])
            landed(pair(c, q_d, 1 - side), n_recv.at[4, c])

        only(has(c, q_c), own)
        only(has(c, q_d), crossed)

    def class_rows():
        for i, t in enumerate(line_from):
            landed(cslots.at[t], c_recv.at[i])
        here = pl.ds(pl.multiple_of(q * cq + z * cz, cz), cz)
        sums = cpart[at(z, cz), :]
        for i, t in enumerate(line_from):
            sums = sums + cslots[t]
        mine_f = cw_ref[here, :].astype(jnp.float32)
        mine_norm = jnp.sqrt(jnp.sum(mine_f * mine_f, axis=1, keepdims=True) + EPSILON)
        mine_unit = mine_f / mine_norm
        along = jnp.sum(mine_unit * sums, axis=1, keepdims=True)
        cout[here, :] = ((sums - mine_unit * along) / mine_norm).astype(ROUNDED)
        for i, t in enumerate(line):
            send(None, remote(
                lambda: cout.at[here, :], lambda: cout.at[here, :],
                lambda i=i: ca_send.at[i], lambda i=i: ca_recv.at[i], {"dp": t * PLANE + q},
            ))

    def class_plane():
        for i, t in enumerate(line_from):
            there = pl.ds(pl.multiple_of(q * cq + t * cz, cz), cz)
            landed(cout.at[there, :], ca_recv.at[i])
        block = lambda: cout.at[at(q, cq), :]
        send(None, remote(block, block, lambda: cp_send.at[0], lambda: cp_recv.at[0], y_dev))
        send(None, remote(block, block, lambda: cp_send.at[1], lambda: cp_recv.at[1], c_dev))

    def class_across():
        landed(cout.at[at(q_y, cq), :], cp_recv.at[0])
        block = lambda: cout.at[at(q_y, cq), :]
        send(None, remote(block, block, lambda: cp_send.at[2], lambda: cp_recv.at[2], c_dev))

    stages = (
        (0, multiply), (1, sum_near), (2, sum_far), (3, gather_far), (4, gather_near),
        (7, gather_across), (9, gather_core),
    )
    for tick in range(count + stages[-1][0]):
        for late, run in stages:
            c = tick - late
            if 0 <= c < count:
                run(c, pl.ds(*chunks[c]))
        if tick == 3:
            class_rows()
        if tick == 6:
            class_plane()
        if tick == 9:
            class_across()

    landed(cout.at[at(q_c, cq), :], cp_recv.at[1])
    landed(cout.at[at(q_d, cq), :], cp_recv.at[2])
    for cond, make in pending:
        only(cond, lambda: make().wait_send())


def place(chunks, per, *refs):
    count = len(chunks)
    slabs, cout = refs[:count], refs[count]
    fc_out, class_out, rows_of, sems = refs[count + 1:]
    copies = [pltpu.make_async_copy(cout, class_out, sems.at[0])]
    copies[0].start()
    for p in range(PLANE):
        for c, (first, size) in enumerate(chunks):
            if p == PLANE - 1 or first < per:
                start = p * per + first
                for j in range(slabs[c].shape[1]):
                    rows_of[pl.ds(start, size), pl.ds(j * LANES, LANES)] = slabs[c][p, j, pl.ds(0, size), :]
                copies.append(pltpu.make_async_copy(
                    rows_of.at[pl.ds(start, size), :], fc_out.at[pl.ds(start, size), :], sems.at[len(copies)],
                ))
                copies[-1].start()
    for copy in copies:
        copy.wait()


def fused(n_dp, features, fc_weight, class_weight, labels):
    rows, fin = features.shape
    classes, dim = class_weight.shape
    nz = n_dp // PLANE
    blocks = fin // LANES
    wide = (blocks - (PLANE - 1) * (blocks // PLANE)) * LANES
    per = blocks // PLANE
    chunks = split_rows(per)
    if wide // LANES > per:
        chunks.append((per * LANES, wide - per * LANES))
    count = len(chunks)
    steps = max(d for d in range(1, 9) if blocks % d == 0)
    bf, f32, dma = jnp.bfloat16, jnp.float32, pltpu.SemaphoreType.DMA
    vmem, whole = pltpu.VMEM, pl.BlockSpec(memory_space=pltpu.VMEM)
    anywhere = pl.BlockSpec(memory_space=pl.ANY)
    results = pl.pallas_call(
        functools.partial(kernel, nz, chunks, rows * n_dp),
        out_shape=(
            *[jax.ShapeDtypeStruct((PLANE, nz, size, LANES), bf) for _, size in chunks],
            jax.ShapeDtypeStruct((classes, dim), bf),
        ),
        in_specs=[anywhere] * 4,
        out_specs=(whole,) * (count + 1),
        scratch_shapes=[
            vmem((rows, fin), bf), vmem((fin, dim), bf), vmem((classes, dim), bf),
            vmem((1, rows), jnp.int32), vmem((PLANE * rows, wide), bf),
            vmem((rows, dim), bf), vmem((rows, dim), bf), vmem((PLANE * rows, dim), bf),
            vmem((classes, dim), bf), vmem((8, rows), f32), vmem((8, rows), f32),
            vmem((rows, classes), bf), vmem((PLANE * rows, classes // PLANE), bf),
            vmem((rows, dim), bf), vmem((rows, dim), bf), vmem((PLANE * rows, dim), bf),
            vmem((classes // PLANE, dim), f32), vmem((nz, classes // PLANE // nz, dim), f32),
            vmem((nz, wide, LANES), f32), vmem((2, wide, LANES), bf), vmem((2, wide, LANES), bf),
            vmem((wide, LANES), bf), vmem((wide, LANES), bf),
            dma((steps,)), dma((4,)), dma((4,)), dma((4, PLANE - 1)), dma((4, PLANE - 1)),
            dma((4,)), dma((nz - 1,)), dma((nz - 1,)), dma((nz - 1,)), dma((nz - 1,)),
            dma((3,)), dma((3,)), dma((4, count)), dma((4, count)),
            dma((3, count)), dma((3, count)), dma((5, count)), dma((5, count)),
        ],
        compiler_params=pltpu.CompilerParams(
            collective_id=0, has_side_effects=True, vmem_limit_bytes=46 * 2**20
        ),
    )(features, fc_weight, class_weight, labels.reshape(1, rows))
    return pl.pallas_call(
        functools.partial(place, chunks, blocks // PLANE * LANES),
        out_shape=(
            jax.ShapeDtypeStruct((fin, dim), bf),
            jax.ShapeDtypeStruct((classes, dim), bf),
        ),
        in_specs=[whole] * (count + 1),
        out_specs=(anywhere, anywhere),
        scratch_shapes=[vmem((fin, dim), bf), dma((PLANE * count + 1,))],
        compiler_params=pltpu.CompilerParams(vmem_limit_bytes=16 * 2**20),
    )(*results)


def choose(n_dp, n_cls, features, fc_weight, class_weight, labels):
    rows, fin = features.shape
    classes, dim = class_weight.shape
    nz = n_dp // PLANE
    fits = (
        n_cls == 2
        and n_dp % PLANE == 0
        and nz == 4
        and dim == nz * LANES
        and fin % LANES == 0
        and fin // LANES >= PLANE
        and rows == LANES
        and classes % (PLANE * LANES) == 0
        and classes // PLANE % (16 * nz) == 0
        and classes <= 512
        and fin <= 6272
    )
    if fits:
        return fused(n_dp, features, fc_weight, class_weight, labels)
    return shards(features, fc_weight, class_weight, labels)


def solution(mesh):
    placed = (P("dp", "cls"), P("cls", None), P("cls", None), P("dp"))
    return jax.shard_map(
        functools.partial(choose, mesh.shape["dp"], mesh.shape["cls"]),
        mesh=mesh,
        in_specs=placed,
        out_specs=(P("cls", None), P("cls", None)),
        check_vma=False,
    )
```

```python
import functools
import math

import jax
import jax.numpy as jnp
from jax import lax
from jax.experimental import pallas as pl
from jax.experimental.pallas import tpu as pltpu
from jax.sharding import PartitionSpec as P

SCALE = 64.0
MARGIN = 0.5
SOFTEN = 0.01
EPSILON = 1e-06


def margin_terms(cosine, is_target):
    sine = jnp.sqrt(1.0 + SOFTEN - cosine * cosine)
    shifted = cosine * math.cos(MARGIN) - sine * math.sin(MARGIN)
    powers = jnp.exp(SCALE * jnp.where(is_target, shifted, cosine))
    slopes = SCALE * jnp.where(is_target, math.cos(MARGIN) + math.sin(MARGIN) * cosine / sine, 1.0)
    return (powers, slopes)


def softmax_grad(powers, totals, slopes, is_target, loss_weight):
    onehot = is_target.astype(jnp.float32)
    return ((powers / totals[:, None] - onehot) * loss_weight * slopes).astype(jnp.bfloat16)


def shards(features, fc_weight, class_weight, labels):
    rows_group = features.shape[0]
    class_count = class_weight.shape[0]
    loss_weight = 1.0 / math.sqrt(rows_group * lax.axis_size("dp"))
    position = lax.axis_index("cls")
    rows_block = features
    raw_embed = lax.psum_scatter(
        jnp.dot(rows_block, fc_weight, preferred_element_type=jnp.float32).astype(jnp.bfloat16),
        "cls",
        scatter_dimension=0,
        tiled=True,
    ).astype(jnp.float32)
    embed_norm = jnp.sqrt(jnp.sum(raw_embed * raw_embed, axis=1, keepdims=True) + EPSILON)
    unit_f = raw_embed / embed_norm
    unit_embed = unit_f.astype(jnp.bfloat16)
    class_f = class_weight.astype(jnp.float32)
    class_norm = jnp.sqrt(jnp.sum(class_f * class_f, axis=1, keepdims=True) + EPSILON)
    class_unit_f = class_f / class_norm
    class_unit = class_unit_f.astype(jnp.bfloat16)
    faces_all = lax.all_gather(unit_embed, "cls", axis=0, tiled=True)
    cosine = lax.dot_general(
        faces_all, class_unit, (((1,), (1,)), ((), ())), preferred_element_type=jnp.float32
    )
    columns = position * class_count + lax.broadcasted_iota(jnp.int32, cosine.shape, 1)
    is_target = columns == labels[:, None]
    powers, slopes = margin_terms(cosine, is_target)
    totals = lax.psum(jnp.sum(powers, axis=1), "cls")
    cos_grad = softmax_grad(powers, totals, slopes, is_target, loss_weight)
    rows_block = cos_grad
    unit_grad = lax.psum_scatter(
        jnp.dot(rows_block, class_unit, preferred_element_type=jnp.float32).astype(jnp.bfloat16),
        "cls",
        scatter_dimension=0,
        tiled=True,
    ).astype(jnp.float32)
    class_part = lax.dot_general(
        cos_grad, faces_all, (((0,), (0,)), ((), ())), preferred_element_type=jnp.float32
    )
    raw_grad = (
        (unit_grad - unit_f * jnp.sum(unit_f * unit_grad, axis=1, keepdims=True)) / embed_norm
    ).astype(jnp.bfloat16)
    rows_block = features
    fc_part = lax.dot_general(
        rows_block,
        lax.all_gather(raw_grad, "cls", axis=0, tiled=True),
        (((0,), (0,)), ((), ())),
        preferred_element_type=jnp.float32,
    )
    fc_total, class_total = lax.psum((fc_part, class_part), "dp")
    fc_out = fc_total.astype(jnp.bfloat16)
    class_grad = (
        class_total - class_unit_f * jnp.sum(class_unit_f * class_total, axis=1, keepdims=True)
    ) / class_norm
    return (fc_out, class_grad.astype(jnp.bfloat16))


MESH = pl.DeviceIdType.MESH
LANES = 128
PLANE = 4
ROUNDED = jnp.bfloat16


def split_rows(blocks):
    sizes = [1] + [3] * ((blocks - 2) // 3)
    sizes += [1] * (blocks - sum(sizes))
    return [(sum(sizes[:i]) * LANES, size * LANES) for i, size in enumerate(sizes)]


def kernel(
    nz, chunks, faces_total,
    feat_hbm, w_hbm, cw_hbm, lab_hbm,
    *refs,
):
    count = len(chunks)
    slabs, refs = refs[:count], refs[count:]
    kernel_body(nz, chunks, faces_total, feat_hbm, w_hbm, cw_hbm, lab_hbm, slabs, *refs)


def kernel_body(
    nz, chunks, faces_total,
    feat_hbm, w_hbm, cw_hbm, lab_hbm,
    slabs, cout,
    feat, w, cw_ref, lab_ref, gath, praw, rraw, unit_all, cu, tot_s, tot_r, cosg, cg_all, pgrad, rgrad,
    rg_all, cpart, cslots, f, send1, recv1, send2, recv2,
    load_sem, x_send, x_recv, p_send, p_recv, own_sem, c_send, c_recv,
    ca_send, ca_recv, cp_send, cp_recv, z_send, z_recv, y_send, y_recv, n_send, n_recv,
):
    rows, fin = feat.shape
    classes, dim = cw_ref.shape
    wide = gath.shape[1]
    per = (fin // LANES // PLANE) * LANES
    cq = classes // PLANE
    cz = cq // nz
    dp = lax.axis_index("dp")
    x = lax.axis_index("cls")
    z, q = dp // PLANE, dp % PLANE
    y, core = q // 2, q % 2
    q_y = (1 - y) * 2 + core
    q_c = y * 2 + 1 - core
    q_d = (1 - y) * 2 + 1 - core
    x_dev = {"cls": 1 - x}
    y_dev = {"dp": z * PLANE + q_y}
    c_dev = {"dp": z * PLANE + q_c}
    half, side = z // 2, z % 2
    near = {"dp": (half * 2 + 1 - side) * PLANE + q}
    far = {"dp": ((1 - half) * 2 + side) * PLANE + q}
    owned = side * 2 + half
    beside = side * 2 + 1 - half
    plane = [(q + d) % PLANE for d in range(1, PLANE)]
    plane_from = [(q + PLANE - d) % PLANE for d in range(1, PLANE)]
    line = [(z + d) % nz for d in range(1, nz)]
    line_from = [(z + nz - d) % nz for d in range(1, nz)]
    pending = []

    def send(cond, make):
        if cond is None:
            make().start()
        else:
            @pl.when(cond)
            def _():
                make().start()
        pending.append((cond, make))

    def remote(src, dst, s, r, dev):
        return lambda: pltpu.make_async_remote_copy(
            src_ref=src(), dst_ref=dst(), send_sem=s(), recv_sem=r(),
            device_id=dev, device_id_type=MESH,
        )

    def landed(dst, r):
        pltpu.make_async_remote_copy(
            src_ref=dst, dst_ref=dst, send_sem=r, recv_sem=r,
            device_id=x_dev, device_id_type=MESH,
        ).wait_recv()

    def at(i, n):
        return pl.ds(pl.multiple_of(i * n, n), n)

    small = [
        pltpu.make_async_copy(cw_hbm, cw_ref, own_sem.at[1]),
        pltpu.make_async_copy(lab_hbm, lab_ref, own_sem.at[2]),
    ]
    for copy in small:
        copy.start()
    steps = load_sem.shape[0]
    kk = fin // steps
    feat_load = pltpu.make_async_copy(feat_hbm, feat, own_sem.at[3])
    feat_load.start()
    loads = []
    for k in range(steps):
        part = pl.ds(k * kk, kk)
        copy = pltpu.make_async_copy(w_hbm.at[part, :], w.at[part, :], load_sem.at[k])
        copy.start()
        loads.append(copy)

    barrier = pltpu.get_barrier_semaphore()
    peers = [x_dev] + [{"dp": z * PLANE + p} for p in plane] + [{"dp": t * PLANE + q} for t in line]
    for dev in peers:
        pl.semaphore_signal(barrier, inc=1, device_id=dev, device_id_type=MESH)
    pl.semaphore_wait(barrier, len(peers))

    mine = at(q, rows)
    own_feat = pltpu.make_async_copy(
        feat_hbm.at[:, pl.ds(pl.multiple_of(q * per, LANES), wide)], gath.at[mine, :], own_sem.at[0]
    )
    own_feat.start()
    feat_load.wait()
    for i, p in enumerate(plane):
        cols = pl.ds(pl.multiple_of(p * per, LANES), wide)
        send(None, remote(
            lambda cols=cols: feat.at[:, cols], lambda: gath.at[mine, :],
            lambda i=i: p_send.at[0, i], lambda i=i: p_recv.at[0, i], {"dp": z * PLANE + p},
        ))

    for h in range(2):
        columns = pl.ds(h * (dim // 2), dim // 2)
        total = jnp.zeros((rows, dim // 2), jnp.float32)
        for k in range(steps):
            if h == 0:
                loads[k].wait()
            part = pl.ds(k * kk, kk)
            total = total + jnp.dot(
                feat[:, part], w[part, columns], preferred_element_type=jnp.float32
            )
        praw[:, columns] = total.astype(ROUNDED)
        send(None, remote(
            lambda columns=columns: praw.at[:, columns], lambda columns=columns: rraw.at[:, columns],
            lambda h=h: x_send.at[3 * h], lambda h=h: x_recv.at[3 * h], x_dev,
        ))

    for copy in small:
        copy.wait()
    class_f = cw_ref[...].astype(jnp.float32)
    class_norm = jnp.sqrt(jnp.sum(class_f * class_f, axis=1, keepdims=True) + EPSILON)
    cu[...] = (class_f / class_norm).astype(ROUNDED)

    landed(rraw.at[:, pl.ds(0, dim // 2)], x_recv.at[0])
    landed(rraw.at[:, pl.ds(dim // 2, dim // 2)], x_recv.at[3])
    raw = praw[...].astype(jnp.float32) + rraw[...].astype(jnp.float32)
    norm = jnp.sqrt(jnp.sum(raw * raw, axis=1, keepdims=True) + EPSILON)
    unit_f = raw / norm
    unit = unit_f.astype(ROUNDED)
    unit_all[mine, :] = unit
    for i, dev in enumerate((y_dev, c_dev)):
        send(None, remote(
            lambda: unit_all.at[mine, :], lambda: unit_all.at[mine, :],
            lambda i=i: p_send.at[1, i], lambda i=i: p_recv.at[1, i], dev,
        ))
    cosine = lax.dot_general(
        unit, cu[...], (((1,), (1,)), ((), ())), preferred_element_type=jnp.float32
    )
    columns = x * classes + lax.broadcasted_iota(jnp.int32, cosine.shape, 1)
    label = jnp.broadcast_to(lab_ref[...], (LANES, rows)).T[:, 0:1]
    is_target = columns == label
    powers, slopes = margin_terms(cosine, is_target)
    partial = jnp.sum(powers, axis=1, keepdims=True)
    tot_s[...] = jnp.broadcast_to(partial, (rows, LANES)).T[0:8, :]
    send(None, remote(lambda: tot_s, lambda: tot_r, lambda: x_send.at[1], lambda: x_recv.at[1], x_dev))
    landed(tot_r, x_recv.at[1])
    totals = partial + jnp.broadcast_to(tot_r[0:1, :], (LANES, rows)).T[:, 0:1]
    weight = 1.0 / math.sqrt(faces_total)
    grad = ((powers / totals - is_target.astype(jnp.float32)) * weight * slopes).astype(ROUNDED)
    cosg[...] = grad
    pgrad[...] = jnp.dot(grad, cu[...], preferred_element_type=jnp.float32).astype(ROUNDED)
    send(None, remote(lambda: pgrad, lambda: rgrad, lambda: x_send.at[2], lambda: x_recv.at[2], x_dev))
    for i, p in enumerate(plane):
        cols = at(p, cq)
        send(None, remote(
            lambda cols=cols: cosg.at[:, cols], lambda: cg_all.at[mine, :],
            lambda i=i: p_send.at[2, i], lambda i=i: p_recv.at[2, i], {"dp": z * PLANE + p},
        ))
    cg_all[mine, :] = cosg[:, at(q, cq)]

    landed(rgrad, x_recv.at[2])
    unit_grad = pgrad[...].astype(jnp.float32) + rgrad[...].astype(jnp.float32)
    along = jnp.sum(unit_f * unit_grad, axis=1, keepdims=True)
    rg_all[mine, :] = ((unit_grad - unit_f * along) / norm).astype(ROUNDED)
    for i, p in enumerate(plane):
        send(None, remote(
            lambda: rg_all.at[mine, :], lambda: rg_all.at[mine, :],
            lambda i=i: p_send.at[3, i], lambda i=i: p_recv.at[3, i], {"dp": z * PLANE + p},
        ))

    across = at(q_y, rows)
    landed(unit_all.at[across, :], p_recv.at[1, 0])
    send(None, remote(
        lambda: unit_all.at[across, :], lambda: unit_all.at[across, :],
        lambda: p_send.at[1, 2], lambda: p_recv.at[1, 2], c_dev,
    ))
    for i, p in enumerate(plane_from):
        landed(cg_all.at[at(p, rows), :], p_recv.at[2, i])
    landed(unit_all.at[at(q_c, rows), :], p_recv.at[1, 1])
    landed(unit_all.at[at(q_d, rows), :], p_recv.at[1, 2])
    cpart[...] = lax.dot_general(
        cg_all[...], unit_all[...], (((0,), (0,)), ((), ())), preferred_element_type=jnp.float32
    )
    for i, t in enumerate(line):
        send(None, remote(
            lambda t=t: cpart.at[at(t, cz), :], lambda: cslots.at[z],
            lambda i=i: c_send.at[i], lambda i=i: c_recv.at[i], {"dp": t * PLANE + q},
        ))

    own_feat.wait()
    for i, p in enumerate(plane_from):
        theirs = at(p, rows)
        landed(gath.at[theirs, :], p_recv.at[0, i])
        landed(rg_all.at[theirs, :], p_recv.at[3, i])

    count = len(chunks)

    def has(c, owner):
        return owner == PLANE - 1 if chunks[c][0] >= per else None

    def only(cond, body):
        if cond is None:
            body()
        else:
            pl.when(cond)(body)

    def exchange(cond, src, dst, sends, recvs, dev, *spot):
        send(cond, remote(
            lambda: src(), lambda: dst(), lambda: sends.at[spot], lambda: recvs.at[spot], dev,
        ))

    def pair(c, p, which):
        return slabs[c].at[p, pl.ds(which * 2, 2), :, :]

    def multiply(c, part):
        def body():
            product = lax.dot_general(
                gath[:, part], rg_all[...], (((0,), (0,)), ((), ())), preferred_element_type=jnp.float32
            )
            for j in range(nz):
                f[j, part, :] = product[:, j * LANES:(j + 1) * LANES]
            for i in range(2):
                send1[i, part, :] = f[(1 - side) * 2 + i, part, :].astype(ROUNDED)

        only(has(c, q), body)
        exchange(
            has(c, q), lambda: send1.at[:, part, :], lambda: recv1.at[:, part, :], z_send, z_recv, near, 0, c
        )

    def sum_near(c, part):
        def body():
            landed(recv1.at[:, part, :], z_recv.at[0, c])
            send2[part, :] = (
                f[side * 2 + 1 - half, part, :] + recv1[1 - half, part, :].astype(jnp.float32)
            ).astype(ROUNDED)

        only(has(c, q), body)
        exchange(has(c, q), lambda: send2.at[part, :], lambda: recv2.at[part, :], z_send, z_recv, far, 1, c)

    def sum_far(c, part):
        def body():
            landed(recv2.at[part, :], z_recv.at[1, c])
            slabs[c][q, owned, :, :] = (
                f[owned, part, :]
                + recv1[half, part, :].astype(jnp.float32)
                + recv2[part, :].astype(jnp.float32)
            ).astype(ROUNDED)

        only(has(c, q), body)
        block = lambda: slabs[c].at[q, owned, :, :]
        exchange(has(c, q), block, block, z_send, z_recv, far, 2, c)
        exchange(has(c, q), block, block, y_send, y_recv, y_dev, 0, c)
        exchange(has(c, q), block, block, n_send, n_recv, c_dev, 0, c)

    def gather_far(c, part):
        other = lambda: slabs[c].at[q, beside, :, :]
        only(has(c, q), lambda: landed(other(), z_recv.at[2, c]))
        block = lambda: pair(c, q, side)
        exchange(has(c, q), block, block, z_send, z_recv, near, 3, c)
        exchange(has(c, q), other, other, y_send, y_recv, y_dev, 1, c)
        exchange(has(c, q), other, other, n_send, n_recv, c_dev, 1, c)

    def gather_near(c, part):
        block = lambda: pair(c, q, 1 - side)
        only(has(c, q), lambda: landed(block(), z_recv.at[3, c]))
        exchange(has(c, q), block, block, y_send, y_recv, y_dev, 2, c)
        exchange(has(c, q), block, block, n_send, n_recv, c_dev, 2, c)

    def arrived(c, p, recvs, first):
        landed(slabs[c].at[p, owned, :, :], recvs.at[first, c])
        landed(slabs[c].at[p, beside, :, :], recvs.at[first + 1, c])

    def gather_across(c, part):
        for i, which in enumerate((side, 1 - side)):
            block = lambda which=which: pair(c, q_y, which)
            if i == 0:
                only(has(c, q_y), lambda: arrived(c, q_y, y_recv, 0))
            else:
                only(has(c, q_y), lambda: landed(block(), y_recv.at[2, c]))
            exchange(has(c, q_y), block, block, n_send, n_recv, c_dev, 3 + i, c)

    def gather_core(c, part):
        def own():
            arrived(c, q_c, n_recv, 0)
            landed(pair(c, q_c, 1 - side), n_recv.at[2, c])

        def crossed():
            landed(pair(c, q_d, side), n_recv.at[3, c])
            landed(pair(c, q_d, 1 - side), n_recv.at[4, c])

        only(has(c, q_c), own)
        only(has(c, q_d), crossed)

    def class_rows():
        for i, t in enumerate(line_from):
            landed(cslots.at[t], c_recv.at[i])
        here = pl.ds(pl.multiple_of(q * cq + z * cz, cz), cz)
        sums = cpart[at(z, cz), :]
        for i, t in enumerate(line_from):
            sums = sums + cslots[t]
        mine_f = cw_ref[here, :].astype(jnp.float32)
        mine_norm = jnp.sqrt(jnp.sum(mine_f * mine_f, axis=1, keepdims=True) + EPSILON)
        mine_unit = mine_f / mine_norm
        along = jnp.sum(mine_unit * sums, axis=1, keepdims=True)
        cout[here, :] = ((sums - mine_unit * along) / mine_norm).astype(ROUNDED)
        for i, t in enumerate(line):
            send(None, remote(
                lambda: cout.at[here, :], lambda: cout.at[here, :],
                lambda i=i: ca_send.at[i], lambda i=i: ca_recv.at[i], {"dp": t * PLANE + q},
            ))

    def class_plane():
        for i, t in enumerate(line_from):
            there = pl.ds(pl.multiple_of(q * cq + t * cz, cz), cz)
            landed(cout.at[there, :], ca_recv.at[i])
        block = lambda: cout.at[at(q, cq), :]
        send(None, remote(block, block, lambda: cp_send.at[0], lambda: cp_recv.at[0], y_dev))
        send(None, remote(block, block, lambda: cp_send.at[1], lambda: cp_recv.at[1], c_dev))

    def class_across():
        landed(cout.at[at(q_y, cq), :], cp_recv.at[0])
        block = lambda: cout.at[at(q_y, cq), :]
        send(None, remote(block, block, lambda: cp_send.at[2], lambda: cp_recv.at[2], c_dev))

    stages = (
        (0, multiply), (1, sum_near), (2, sum_far), (3, gather_far), (4, gather_near),
        (7, gather_across), (9, gather_core),
    )
    for tick in range(count + stages[-1][0]):
        for late, run in stages:
            c = tick - late
            if 0 <= c < count:
                run(c, pl.ds(*chunks[c]))
        if tick == 3:
            class_rows()
        if tick == 6:
            class_plane()
        if tick == 9:
            class_across()

    landed(cout.at[at(q_c, cq), :], cp_recv.at[1])
    landed(cout.at[at(q_d, cq), :], cp_recv.at[2])
    for cond, make in pending:
        only(cond, lambda: make().wait_send())


def place(chunks, per, *refs):
    count = len(chunks)
    slabs, cout = refs[:count], refs[count]
    fc_out, class_out, rows_of, sems = refs[count + 1:]
    copies = [pltpu.make_async_copy(cout, class_out, sems.at[0])]
    copies[0].start()
    for p in range(PLANE):
        for c, (first, size) in enumerate(chunks):
            if p == PLANE - 1 or first < per:
                start = p * per + first
                for j in range(slabs[c].shape[1]):
                    rows_of[pl.ds(start, size), pl.ds(j * LANES, LANES)] = slabs[c][p, j, pl.ds(0, size), :]
                copies.append(pltpu.make_async_copy(
                    rows_of.at[pl.ds(start, size), :], fc_out.at[pl.ds(start, size), :], sems.at[len(copies)],
                ))
                copies[-1].start()
    for copy in copies:
        copy.wait()


def fused(n_dp, features, fc_weight, class_weight, labels):
    rows, fin = features.shape
    classes, dim = class_weight.shape
    nz = n_dp // PLANE
    blocks = fin // LANES
    wide = (blocks - (PLANE - 1) * (blocks // PLANE)) * LANES
    per = blocks // PLANE
    chunks = split_rows(per)
    if wide // LANES > per:
        chunks.append((per * LANES, wide - per * LANES))
    count = len(chunks)
    steps = max(d for d in range(1, 9) if blocks % d == 0)
    bf, f32, dma = jnp.bfloat16, jnp.float32, pltpu.SemaphoreType.DMA
    vmem, whole = pltpu.VMEM, pl.BlockSpec(memory_space=pltpu.VMEM)
    anywhere = pl.BlockSpec(memory_space=pl.ANY)
    results = pl.pallas_call(
        functools.partial(kernel, nz, chunks, rows * n_dp),
        out_shape=(
            *[jax.ShapeDtypeStruct((PLANE, nz, size, LANES), bf) for _, size in chunks],
            jax.ShapeDtypeStruct((classes, dim), bf),
        ),
        in_specs=[anywhere] * 4,
        out_specs=(whole,) * (count + 1),
        scratch_shapes=[
            vmem((rows, fin), bf), vmem((fin, dim), bf), vmem((classes, dim), bf),
            vmem((1, rows), jnp.int32), vmem((PLANE * rows, wide), bf),
            vmem((rows, dim), bf), vmem((rows, dim), bf), vmem((PLANE * rows, dim), bf),
            vmem((classes, dim), bf), vmem((8, rows), f32), vmem((8, rows), f32),
            vmem((rows, classes), bf), vmem((PLANE * rows, classes // PLANE), bf),
            vmem((rows, dim), bf), vmem((rows, dim), bf), vmem((PLANE * rows, dim), bf),
            vmem((classes // PLANE, dim), f32), vmem((nz, classes // PLANE // nz, dim), f32),
            vmem((nz, wide, LANES), f32), vmem((2, wide, LANES), bf), vmem((2, wide, LANES), bf),
            vmem((wide, LANES), bf), vmem((wide, LANES), bf),
            dma((steps,)), dma((4,)), dma((4,)), dma((4, PLANE - 1)), dma((4, PLANE - 1)),
            dma((4,)), dma((nz - 1,)), dma((nz - 1,)), dma((nz - 1,)), dma((nz - 1,)),
            dma((3,)), dma((3,)), dma((4, count)), dma((4, count)),
            dma((3, count)), dma((3, count)), dma((5, count)), dma((5, count)),
        ],
        compiler_params=pltpu.CompilerParams(
            collective_id=0, has_side_effects=True, vmem_limit_bytes=46 * 2**20
        ),
    )(features, fc_weight, class_weight, labels.reshape(1, rows))
    return pl.pallas_call(
        functools.partial(place, chunks, blocks // PLANE * LANES),
        out_shape=(
            jax.ShapeDtypeStruct((fin, dim), bf),
            jax.ShapeDtypeStruct((classes, dim), bf),
        ),
        in_specs=[whole] * (count + 1),
        out_specs=(anywhere, anywhere),
        scratch_shapes=[vmem((fin, dim), bf), dma((PLANE * count + 1,))],
        compiler_params=pltpu.CompilerParams(vmem_limit_bytes=16 * 2**20),
    )(*results)


def choose(n_dp, n_cls, features, fc_weight, class_weight, labels):
    rows, fin = features.shape
    classes, dim = class_weight.shape
    nz = n_dp // PLANE
    fits = (
        n_cls == 2
        and n_dp % PLANE == 0
        and nz == 4
        and dim == nz * LANES
        and fin % LANES == 0
        and fin // LANES >= PLANE
        and rows == LANES
        and classes % (PLANE * LANES) == 0
        and classes // PLANE % (16 * nz) == 0
        and classes <= 512
        and fin <= 6272
    )
    if fits:
        return fused(n_dp, features, fc_weight, class_weight, labels)
    return shards(features, fc_weight, class_weight, labels)


def solution(mesh):
    placed = (P("dp", "cls"), P("cls", None), P("cls", None), P("dp"))
    return jax.shard_map(
        functools.partial(choose, mesh.shape["dp"], mesh.shape["cls"]),
        mesh=mesh,
        in_specs=placed,
        out_specs=(P("cls", None), P("cls", None)),
        check_vma=False,
    )
```
